512 devices in a mesh: tm: 16 (over y, core), space: 32 (over x, z).
Axes of the slice: x: 4, y: 8, z: 8, core: 2. Of those that a mesh axis runs over, the one named last changes fastest.
Arguments:
- latent: bfloat16 [16, 2048, 2560], P('tm', 'space'), may hold values from -44 to 44
- past_cache: bfloat16 [2, 256, 81920], P(None, 'tm', 'space'), may hold values from -5 to 5
- neighbour_mask: int32 [16, 32, 4], P('tm', 'space'), may hold values 0 or 1
- gains: float32 [2, 2560], replicated, may hold values from 0.45 to 1.25
- step_sizes: float32 [2], replicated, may hold values from 0.3 to 0.8
Outputs:
- denoised: bfloat16 [16, 2048, 2560], P('tm', 'space')
- velocity: bfloat16 [16, 2048, 2560], P('tm', 'space')
The draws below stay inside these ranges and needn't reach their ends.
All inputs are finite; a program needn't handle non-finite values. No bound on the sum of `neighbour_mask` on one device may be relied on, other than what follows from the above.
Results may differ from the reference program's by a relative error of at most 0.0069.
The reference program's roundings to bfloat16 on the way (of `current`) count: a program that leaves them out, or rounds other values in their place, can miss the bound.
Values may be sent and summed in bfloat16 or wider, within the bound.
A program may use at most 64 MiB of HBM per device.

```python
import math
import jax
import jax.numpy as jnp
from jax import lax

HD = 128
HEADS = 20
HW = 2560
TOK_DEV = 64
STEPS = 2
OFFSETS = 4
ROWS = 2048
PAST = 256
N_TM = 16
N_SPACE = 32


def sharp_heads(key):
    ranking = jax.random.permutation(jax.random.fold_in(key, 101), HEADS)
    return ranking[:max(1, HEADS // 4)]


def draw_gains(key, part):
    chosen = sharp_heads(key)
    key = jax.random.fold_in(key, 7)
    first_key, second_key = jax.random.split(key)
    head_of = jnp.arange(HW, dtype=jnp.int32) // HD
    in_sharp = jnp.any(head_of[:, None] == chosen[None, :], axis=1)
    drawn = jnp.exp(jax.random.uniform(first_key, (2, HW), jnp.float32, jnp.log(0.45), jnp.log(0.9)))
    strong = jnp.exp(jax.random.uniform(second_key, (2, HW), jnp.float32, jnp.log(0.95), jnp.log(1.25)))
    return jnp.where(in_sharp[None, :], strong, drawn).astype(jnp.float32)


def draw_latent(key, part):
    chosen = sharp_heads(key)
    key = jax.random.fold_in(key, 11)
    subkeys = jax.random.split(key, 9)
    tiles = N_TM * N_SPACE
    half = HD // 2
    first_pos = jax.random.randint(subkeys[3], (tiles,), 0, TOK_DEV // 2)
    second_pos = first_pos + 1 + jax.random.randint(subkeys[4], (tiles,), 0, TOK_DEV // 2)
    picked = jax.random.randint(subkeys[5], (tiles,), 0, chosen.shape[0])
    head_pick = chosen[picked]
    row_ids = jnp.arange(TOK_DEV, dtype=jnp.int32)
    is_first = row_ids[None, :] == first_pos[:, None]
    is_second = row_ids[None, :] == second_pos[:, None]
    background = jnp.clip(jax.random.normal(subkeys[0], (tiles, TOK_DEV, HW), jnp.float32), -6.0, 6.0)
    power = jax.random.uniform(subkeys[6], (tiles,), jnp.float32)
    power = power.at[0].set(1.0)
    strength = 8.0 * jnp.power(4.0, power)
    magnitude = jax.random.uniform(subkeys[7], (2, tiles, half), jnp.float32, 0.8, 1.2)
    signs = jnp.where(jax.random.bernoulli(subkeys[8], 0.5, (2, tiles, half)), 1.0, -1.0)
    pattern = magnitude * signs
    base_full = jnp.repeat(pattern[0], 2, axis=1)
    tilt_full = (pattern[1][:, :, None] * jnp.array([1.0, -1.0], jnp.float32)).reshape(tiles, HD)
    first_vec = strength[:, None] * base_full
    second_vec = strength[:, None] * (base_full + 0.14 * tilt_full)
    first_spread = jnp.tile(first_vec, (1, HEADS))
    second_spread = jnp.tile(second_vec, (1, HEADS))
    in_head = (jnp.arange(HW, dtype=jnp.int32) // HD)[None, :] == head_pick[:, None]
    result = jnp.where(is_first[:, :, None] & in_head[:, None, :], first_spread[:, None, :], background)
    result = jnp.where(is_second[:, :, None] & in_head[:, None, :], second_spread[:, None, :], result)
    result = result.reshape(N_TM, N_SPACE * TOK_DEV, HW)
    return result.astype(jnp.bfloat16)


def set_ends(values, key, least, top_value):
    longest = values.shape.index(max(values.shape))
    spots = []
    for shift in (0, 1):
        where = [jax.random.randint(jax.random.fold_in(key, axis), (), 0, length) for axis, length in enumerate(values.shape)]
        where[longest] = (where[longest] + shift) % values.shape[longest]
        spots.append(tuple(where))
    return values.at[spots[0]].set(least).at[spots[1]].set(top_value)


def level_of(own_key, dims, pieces, least, largest):
    def one(axis_at, parts):
        steps = jax.random.uniform(jax.random.fold_in(jax.random.fold_in(own_key, 6), axis_at), (parts,), jnp.float32, least / len(pieces), largest / len(pieces))
        return jnp.repeat(jnp.exp(steps), dims[axis_at] // parts).reshape((-1,) + (1,) * (len(dims) - axis_at - 1))

    level = one(*pieces[0])
    for cut in pieces[1:]:
        level = level * one(*cut)
    return level


def noise(rng, dims, scale, limit, shards=(), held_as=jnp.bfloat16):
    loudness = level_of(rng, dims, shards, -0.22, 0.18) if shards else 1.0
    values = jax.random.normal(rng, dims, jnp.float32) * scale * loudness
    return jnp.minimum(jnp.maximum(values, -limit), limit).astype(held_as)


def setup_inputs(seed: int = 0) -> dict:
    key_of = jax.random.split(jax.random.key(seed), 6)
    latent = draw_latent(jax.random.fold_in(key_of[5], 71), 0)
    past_cache = noise(key_of[1], (2, PAST, N_SPACE * HW), 0.7, 5.0, ((1, 16), (2, 32)))
    neighbour_mask = set_ends((jax.random.randint(key_of[2], (N_TM, N_SPACE, OFFSETS), 0, 2) < 1).astype(jnp.int32), jax.random.fold_in(key_of[2], 1), 0, 1)
    gains = draw_gains(jax.random.fold_in(key_of[5], 71), 0)
    step_sizes = jnp.clip(jnp.exp(jax.random.uniform(key_of[4], (STEPS,), jnp.float32, math.log(0.3), math.log(0.8))), 0.3, 0.8)
    return {"latent": latent, "past_cache": past_cache, "neighbour_mask": neighbour_mask, "gains": gains, "step_sizes": step_sizes}


epsilon = 1e-06

def normed(values):
    values = values.astype(jnp.float32)
    return values * lax.rsqrt(lax.optimization_barrier(jnp.mean(values * values, axis=-1, keepdims=True)) + epsilon)

def reference(latent, past_cache, neighbour_mask, gains, step_sizes):
    offsets = (-2, -1, 1, 2)
    cache_keys = past_cache[0].reshape(PAST, N_SPACE, HW).transpose(1, 0, 2)
    cache_values = past_cache[1].reshape(PAST, N_SPACE, HW).transpose(1, 0, 2)
    columns = jnp.arange(N_SPACE, dtype=jnp.int32)
    current = latent
    velocity_last = jnp.zeros(latent.shape, jnp.float32)
    for section in range(STEPS):
        normal = normed(current)
        query = (normal * gains[0]).astype(jnp.bfloat16)
        key = (normal * gains[1]).astype(jnp.bfloat16)
        query_tiles = query.reshape(N_TM, N_SPACE, TOK_DEV, HW)
        key_tiles = key.reshape(N_TM, N_SPACE, TOK_DEV, HW)
        value_tiles = current.reshape(N_TM, N_SPACE, TOK_DEV, HW)

        def band(inputs):
            query_band, key_band, value_band, mask_band = inputs
            padded_keys = jnp.pad(key_band, ((2, 2), (0, 0), (0, 0)))
            padded_values = jnp.pad(value_band, ((2, 2), (0, 0), (0, 0)))
            key_parts = [key_band, cache_keys]
            value_parts = [value_band, cache_values]
            valid_parts = [jnp.ones((N_SPACE, TOK_DEV + PAST), bool)]
            for slot in range(OFFSETS):
                offset = offsets[slot]
                key_parts.append(padded_keys[2 + offset:2 + offset + N_SPACE])
                value_parts.append(padded_values[2 + offset:2 + offset + N_SPACE])
                inside = (columns + offset >= 0) & (columns + offset < N_SPACE)
                usable = (mask_band[:, slot] > 0) & inside
                valid_parts.append(jnp.broadcast_to(usable[:, None], (N_SPACE, TOK_DEV)))
            all_keys = jnp.concatenate(key_parts, axis=1).astype(jnp.float32)
            all_values = jnp.concatenate(value_parts, axis=1).astype(jnp.float32)
            valid = jnp.concatenate(valid_parts, axis=1)
            q_heads = query_band.astype(jnp.float32).reshape(N_SPACE, TOK_DEV, HEADS, HD)
            k_heads = all_keys.reshape(N_SPACE, -1, HEADS, HD)
            v_heads = all_values.reshape(N_SPACE, -1, HEADS, HD)
            scores = jnp.einsum('sthd,snhd->shtn', q_heads, k_heads) / jnp.sqrt(jnp.float32(HD))
            scores = jnp.where(valid[:, None, None, :], scores, jnp.float32(-1e+30))
            top = lax.optimization_barrier(jnp.max(scores, axis=-1, keepdims=True))
            expo = jnp.exp(scores - top)
            total = lax.optimization_barrier(jnp.sum(expo, axis=-1))
            weights = expo.astype(jnp.bfloat16).astype(jnp.float32)
            mixed = jnp.einsum('shtn,snhd->shtd', weights, v_heads) / total[..., None]
            return mixed.transpose(0, 2, 1, 3).reshape(N_SPACE, TOK_DEV, HW)
        attended = lax.map(band, (query_tiles, key_tiles, value_tiles, neighbour_mask))
        attended = attended.reshape(N_TM, ROWS, HW)
        velocity_last = normed(attended)
        current = (current.astype(jnp.float32) + step_sizes[section] * velocity_last).astype(jnp.bfloat16)
    return (current, velocity_last.astype(jnp.bfloat16))
```

```python
import math

import jax
import jax.numpy as jnp
from jax import lax
from jax.experimental import pallas as pl
from jax.experimental.pallas import tpu as pltpu
from jax.sharding import PartitionSpec as P

HD = 128
HEADS = 20
HW = HD * HEADS
TOK = 64
STEPS = 2
SHARD = 16
GROUPS = 4
PER = HEADS // GROUPS
GW = PER * HD
BATCH = 20
EPS = 1e-6
SCORE_SCALE = math.log2(math.e) / math.sqrt(HD)
MASKED = -1e30
MESH = pl.DeviceIdType.MESH
F32 = jnp.float32
BF16 = jnp.bfloat16

STAGE = 128
NEAR, FAR = 3, 4
TILES = 3 * STAGE
ROWS = TILES + STEPS * 2 * STAGE
CHIP = TOK
RING = 14


def kernel(
    latent_hbm, cache_hbm, mask_hbm, gains_hbm, steps_hbm,
    denoised_ref, velocity_ref,
    mask_ref, gains_ref, steps_ref, buf, query, accum, peak, total, scale_own, scale_in, scale_col, bias, square,
    local_sem, ysend, ssend, yrecv, zsend, zrecv, rsend, rrecv,
):
    tm, space = lax.axis_index("tm"), lax.axis_index("space")
    n_tm, n_space = lax.axis_size("tm"), lax.axis_size("space")
    along_y = ((lax.rem(tm + 2, n_tm), space), (lax.rem(tm + n_tm - 2, n_tm), space))
    sibling = (tm + 1 - 2 * lax.rem(tm, 2), space)
    along_z = ((tm, lax.rem(space + 1, n_space)), (tm, lax.rem(space + n_space - 1, n_space)))
    has_low, has_high = space > 0, space < n_space - 1
    sends = ((has_high, has_low & has_high), (has_low, has_low & has_high))
    receives = ((has_low, space > 1), (has_high, space < n_space - 2))

    def remote(src, dst, send, recv, device):
        return pltpu.make_async_remote_copy(
            src_ref=src, dst_ref=dst, send_sem=send, recv_sem=recv, device_id=device, device_id_type=MESH
        )

    def half_cols(half):
        return pl.ds(pl.multiple_of(half * (HW // 2), HW // 2), HW // 2)

    def shard(which, index, half):
        rows = CHIP + SHARD * index + jnp.where(index >= 2, 2 * SHARD, 0)
        return buf.at[which, pl.ds(pl.multiple_of(rows, SHARD), SHARD), half_cols(half)]

    def slot(distance, direction):
        return 4 * distance - 2 + jnp.where(distance == 4, 0, 2 * direction)

    def ring_place(direction, number):
        which = lax.rem(number // 2 + direction, 2)
        return which, lax.rem(number, 2), number // 4 + 1

    def ring_copy(direction, number, own):
        which, half, distance = ring_place(direction, number)
        target = slot(distance, direction)
        if own:
            src = cache_hbm.at[which, :, half_cols(half)]
        else:
            src = shard(which, slot(distance - 1, direction), half)
        return remote(
            src, shard(which, target, half), ysend.at[direction, number], yrecv.at[which, target, half],
            along_y[direction],
        )

    def sib_copy(which, half, target, own=False):
        src = cache_hbm.at[which, :, half_cols(half)] if own else shard(which, target - 1, half)
        return remote(
            src, shard(which, target, half), ssend.at[which, target, half], yrecv.at[which, target, half], sibling
        )

    def ring_round(number):
        for direction in range(2):
            which, half, distance = ring_place(direction, number)
            ring_copy(direction, number, False).wait_recv()

            @pl.when(number + 4 < RING)
            def _():
                ring_copy(direction, number + 4, False).start()

            sib_copy(which, half, slot(distance, direction) + 1).start()

    def each_sibling(first, count, act):
        def body(i, _):
            act(sib_copy(lax.rem(i, 2), lax.rem(i // 2, 2), first + 2 * (i // 4)))
            return 0

        lax.fori_loop(0, 4 * count, body, 0)

    def columns(group):
        return pl.ds(pl.multiple_of(group * GW, GW), GW)

    def head_cols(head):
        return pl.ds(pl.multiple_of(head * HD, HD), HD)

    def tile_rows(phase, number):
        return pl.ds(pl.multiple_of(TILES + phase * 2 * STAGE + number * TOK, TOK), TOK)

    def tile_part(phase, number, cols):
        return buf.at[1, tile_rows(phase, number), cols]

    def tile_copy(phase, direction, hop, group):
        cols = columns(group)
        if hop == 1:
            src = tile_part(phase, direction, cols)
        elif isinstance(phase, int) and phase == 0:
            src = latent_hbm.at[0, :, cols]
        else:
            src = buf.at[1, pl.ds(0, TOK), cols]
        target = 2 * hop + direction
        return remote(
            src, tile_part(phase, target, cols), zsend.at[phase, direction, hop, group],
            zrecv.at[phase, target, group], along_z[direction],
        )

    def scale_copy(phase, direction, hop):
        src = scale_own.at[phase] if hop == 0 else scale_in.at[phase, direction]
        target = 2 * hop + direction
        return remote(
            src, scale_in.at[phase, target], rsend.at[phase, direction, hop], rrecv.at[phase, target], along_z[direction]
        )

    def start_tile(phase, hop, group):
        for direction in range(2):
            @pl.when(sends[direction][hop])
            def _():
                tile_copy(phase, direction, hop, group).start()

    def wait_tile(phase, hop, group):
        for direction in range(2):
            @pl.when(receives[direction][hop])
            def _():
                tile_copy(phase, direction, hop, group).wait_recv()

        if hop == 0:
            start_tile(phase, 1, group)

    diagonal = lax.broadcasted_iota(jnp.int32, (TOK, HD), 0) == lax.broadcasted_iota(jnp.int32, (TOK, HD), 1)

    def take_scales(phase, hop):
        for direction in range(2):
            target = 2 * hop + direction

            @pl.when(receives[direction][hop])
            def _():
                scale_copy(phase, direction, hop).wait_recv()

            if hop == 0:
                @pl.when(sends[direction][1])
                def _():
                    scale_copy(phase, direction, 1).start()

            row = jnp.broadcast_to(scale_in[phase, target, 0:1, :], (TOK, HD))
            col = jnp.sum(jnp.where(diagonal, row, 0.0), axis=1, keepdims=True)
            scale_col[pl.ds(target * TOK, TOK), :] = jnp.broadcast_to(col, (TOK, HD))

    def root_scale():
        mean = jnp.sum(square[...], axis=1, keepdims=True) * (1.0 / HW)
        return jnp.broadcast_to(lax.rsqrt(mean + EPS), (TOK, HD))

    def send_scale(phase, col):
        row = jnp.sum(jnp.where(diagonal, col, 0.0), axis=0, keepdims=True)
        scale_own[phase] = jnp.broadcast_to(row, (8, HD))
        for direction in range(2):
            @pl.when(sends[direction][0])
            def _():
                scale_copy(phase, direction, 0).start()

    def begin_heads(col):
        def body(group, _):
            heads = [group * PER + i for i in range(PER)]
            normals = [buf[1, pl.ds(0, TOK), head_cols(head)].astype(F32) * col for head in heads]
            for head, normal in zip(heads, normals):
                cols = head_cols(head)
                query[:, cols] = (normal * gains_ref[0:1, cols]).astype(BF16)
                buf[0, pl.ds(0, TOK), cols] = (normal * gains_ref[1:2, cols]).astype(BF16)
                peak[head] = jnp.full((TOK, HD), MASKED, F32)
                total[head] = jnp.zeros((TOK, HD), F32)
                accum[:, cols] = jnp.zeros((TOK, HD), F32)
            return 0

        lax.fori_loop(0, GROUPS, body, 0)

    def tile_keys(stage, phase, heads):
        scales = scale_col[pl.ds(pl.multiple_of((stage - NEAR) * STAGE, STAGE), STAGE), :]
        source = pl.ds(pl.multiple_of((stage + phase * 2) * STAGE, STAGE), STAGE)
        return [
            (buf[1, source, head_cols(head)].astype(F32) * scales * gains_ref[1:2, head_cols(head)]).astype(BF16)
            for head in heads
        ]

    def update(stage, phase, heads):
        cols = [head_cols(head) for head in heads]
        value_stage = stage + phase * 2 if stage >= NEAR else stage
        value_rows = pl.ds(pl.multiple_of(value_stage * STAGE, STAGE), STAGE)
        allowed = bias[stage, 0:1, :]
        if stage >= NEAR:
            keys = tile_keys(stage, phase, heads)
        else:
            keys = [buf[0, value_rows, c] for c in cols]
        queries = [query[:, c] for c in cols]
        old_peaks = [peak[head] for head in heads]
        scores = [
            lax.dot_general(q, k, (((1,), (1,)), ((), ())), preferred_element_type=F32) * SCORE_SCALE + allowed
            for q, k in zip(queries, keys)
        ]
        peaks = [
            jnp.maximum(old, jnp.broadcast_to(jnp.max(s, axis=1, keepdims=True), (TOK, HD)))
            for old, s in zip(old_peaks, scores)
        ]
        expos = [jnp.exp2(s - p) for s, p in zip(scores, peaks)]
        values = [buf[1, value_rows, c] for c in cols]
        mixed = [jnp.dot(e.astype(BF16), v, preferred_element_type=F32) for e, v in zip(expos, values)]
        factors = [jnp.exp2(old - new) for old, new in zip(old_peaks, peaks)]
        totals = [total[head] * f + e for head, f, e in zip(heads, factors, expos)]
        sums = [accum[:, c] * f + m for c, f, m in zip(cols, factors, mixed)]
        for i, head in enumerate(heads):
            peak[head] = peaks[i]
            total[head] = totals[i]
            accum[:, cols[i]] = sums[i]

    def finish(group, _):
        heads = [group * PER + i for i in range(PER)]
        squares = square[...]
        attended = [accum[:, head_cols(head)] / jnp.sum(total[head], axis=1, keepdims=True) for head in heads]
        for head, values in zip(heads, attended):
            accum[:, head_cols(head)] = values
            squares = squares + values * values
        square[...] = squares
        return 0

    loads = [
        pltpu.make_async_copy(latent_hbm.at[0], buf.at[1, pl.ds(0, TOK)], local_sem.at[0]),
        pltpu.make_async_copy(cache_hbm.at[0], buf.at[0, pl.ds(CHIP, SHARD)], local_sem.at[1]),
        pltpu.make_async_copy(cache_hbm.at[1], buf.at[1, pl.ds(CHIP, SHARD)], local_sem.at[2]),
        pltpu.make_async_copy(mask_hbm, mask_ref, local_sem.at[3]),
        pltpu.make_async_copy(gains_hbm, gains_ref, local_sem.at[4]),
        pltpu.make_async_copy(steps_hbm, steps_ref, local_sem.at[5]),
    ]
    for load in loads:
        load.start()
    barrier = pltpu.get_barrier_semaphore()
    for device in (*along_y, sibling):
        pl.semaphore_signal(barrier, inc=1, device_id=device, device_id_type=MESH)
    for direction in range(2):
        @pl.when(sends[direction][0])
        def _():
            pl.semaphore_signal(barrier, inc=1, device_id=along_z[direction], device_id_type=MESH)

    pl.semaphore_wait(barrier, 3 + lax.min(space, 1) + lax.min(n_space - 1 - space, 1))

    for number in range(2):
        for direction in range(2):
            ring_copy(direction, number, True).start()
    start_tile(0, 0, 0)
    for number in range(2, 4):
        for direction in range(2):
            ring_copy(direction, number, True).start()
    for which in range(2):
        for half in range(2):
            sib_copy(which, half, 1, True).start()

    for hop in range(2):
        for direction in range(2):
            @pl.when(jnp.logical_not(receives[direction][hop]))
            def _():
                for phase in range(STEPS):
                    buf[1, tile_rows(phase, 2 * hop + direction), :] = jnp.zeros((TOK, HW), BF16)
                    scale_in[phase, 2 * hop + direction] = jnp.zeros((8, HD), F32)

    for which in range(2):
        for stage in (0, 2):
            buf[which, pl.ds(stage * STAGE + 3 * STAGE // 4, STAGE // 4), :] = jnp.zeros((STAGE // 4, HW), BF16)

    for load in loads[3:]:
        load.wait()
    lane = lax.broadcasted_iota(jnp.int32, (8, HD), 1)
    for stage in (0, 2):
        bias[stage] = jnp.where(lane < 3 * STAGE // 4, 0.0, MASKED).astype(F32)
    bias[1] = jnp.zeros((8, HD), F32)
    for hop in range(2):
        low, high = (1, 2) if hop == 0 else (0, 3)
        low_ok = (mask_ref[0, 0, low] > 0) & (space - hop > 0)
        high_ok = (mask_ref[0, 0, high] > 0) & (space + hop + 1 < n_space)
        low_bias = jnp.where(low_ok, 0.0, MASKED).astype(F32)
        high_bias = jnp.where(high_ok, 0.0, MASKED).astype(F32)
        bias[NEAR + hop] = jnp.where(lane < TOK, low_bias, high_bias)

    loads[0].wait()
    square[...] = jnp.zeros((TOK, HD), F32)

    def add_squares(group, _):
        squares = square[...]
        for i in range(PER):
            values = buf[1, pl.ds(0, TOK), head_cols(group * PER + i)].astype(F32)
            squares = squares + values * values
        square[...] = squares
        return 0

    lax.fori_loop(0, GROUPS, add_squares, 0)
    col = root_scale()
    send_scale(0, col)
    for group in range(1, GROUPS):
        start_tile(0, 0, group)
    begin_heads(col)
    for load in loads[1:3]:
        load.wait()

    def phase_body(phase, _):
        first = phase == 0
        square[...] = jnp.zeros((TOK, HD), F32)

        def heads_of(part, count):
            return [part * count + i for i in range(count)]

        def arrive(hop, group, rounds=True):
            if rounds:
                @pl.when(first)
                def _():
                    ring_round(8 * hop + 2 * group)
                    ring_round(8 * hop + 2 * group + 1)

            wait_tile(phase, hop, group)

        @pl.when(first)
        def _():
            each_sibling(1, 1, lambda copy: copy.wait_recv())

        def stored(stage):
            def body(part, _):
                update(stage, phase, heads_of(part, BATCH))
                return 0

            lax.fori_loop(0, HEADS // BATCH, body, 0)

        stored(0)

        def near(part, _):
            arrive(0, 2 * part)

            @pl.when(part == 0)
            def _():
                take_scales(phase, 0)

            arrive(0, 2 * part + 1)
            update(NEAR, phase, heads_of(part, 2 * PER))
            return 0

        lax.fori_loop(0, GROUPS // 2, near, 0)

        @pl.when(first)
        def _():
            each_sibling(3, 4, lambda copy: copy.wait_recv())

        stored(1)
        arrive(1, 0)
        take_scales(phase, 1)
        arrive(1, 1)
        update(FAR, phase, heads_of(0, 2 * PER))
        arrive(1, 2)
        update(FAR, phase, heads_of(2, PER))

        @pl.when(first)
        def _():
            each_sibling(11, 3, lambda copy: copy.wait_recv())

        stored(2)
        lax.fori_loop(0, 3, finish, 0)
        arrive(1, 3, rounds=False)
        update(FAR, phase, heads_of(3, PER))
        finish(3, 0)

        @pl.when(first)
        def _():
            col = root_scale()
            step_size = steps_ref[0]
            square[...] = jnp.zeros((TOK, HD), F32)

            def move(group, _):
                squares = square[...]
                cols = [head_cols(group * PER + i) for i in range(PER)]
                moved = [
                    (buf[1, pl.ds(0, TOK), c].astype(F32) + step_size * (accum[:, c] * col)).astype(BF16)
                    for c in cols
                ]
                for c, values in zip(cols, moved):
                    buf[1, pl.ds(0, TOK), c] = values
                    wide = values.astype(F32)
                    squares = squares + wide * wide
                square[...] = squares
                start_tile(1, 0, group)
                return 0

            lax.fori_loop(0, GROUPS, move, 0)
            col = root_scale()
            send_scale(1, col)
            begin_heads(col)

        return 0

    lax.fori_loop(0, STEPS, phase_body, 0)

    col = root_scale()
    last_size = steps_ref[STEPS - 1]

    def put(group, _):
        cols = [head_cols(group * PER + i) for i in range(PER)]
        velocities = [accum[:, c] * col for c in cols]
        moved = [buf[1, pl.ds(0, TOK), c].astype(F32) + last_size * v for c, v in zip(cols, velocities)]
        for c, velocity, denoised in zip(cols, velocities, moved):
            denoised_ref[0, :, c] = denoised.astype(BF16)
            velocity_ref[0, :, c] = velocity.astype(BF16)
        return 0

    lax.fori_loop(0, GROUPS, put, 0)

    def ring_left(number, _):
        for direction in range(2):
            ring_copy(direction, number, False).wait_send()
        return 0

    for number in range(4):
        for direction in range(2):
            ring_copy(direction, number, True).wait_send()
    lax.fori_loop(4, RING, ring_left, 0)
    for which in range(2):
        for half in range(2):
            sib_copy(which, half, 1, True).wait_send()
    each_sibling(3, 7, lambda copy: copy.wait_send())
    for direction in range(2):
        for hop in range(2):
            @pl.when(sends[direction][hop])
            def _():
                for phase in range(STEPS):
                    scale_copy(phase, direction, hop).wait_send()
                    for group in range(GROUPS):
                        tile_copy(phase, direction, hop, group).wait_send()


PIECE = 16
PIECES = TOK // PIECE


def hand_over(denoised_in, velocity_in, denoised_out, velocity_out, sems):
    copies = [
        pltpu.make_async_copy(source.at[0, pl.ds(PIECE * i, PIECE)], target.at[0, pl.ds(PIECE * i, PIECE)], sems.at[which, i])
        for i in range(PIECES)
        for which, (source, target) in enumerate(((denoised_in, denoised_out), (velocity_in, velocity_out)))
    ]
    for copy in copies:
        copy.start()
    for copy in copies:
        copy.wait()


def per_device(latent, past_cache, neighbour_mask, gains, step_sizes):
    dma = pltpu.SemaphoreType.DMA
    hbm = pl.BlockSpec(memory_space=pltpu.HBM)
    vmem = pl.BlockSpec(memory_space=pltpu.VMEM)
    operands = [
        pltpu.with_memory_space_constraint(x, pltpu.HBM)
        for x in (latent, past_cache, neighbour_mask, gains, step_sizes)
    ]
    results = pl.pallas_call(
        kernel,
        out_shape=(pltpu.VMEM((1, TOK, HW), BF16),) * 2,
        in_specs=[hbm] * 5,
        out_specs=(vmem,) * 2,
        scratch_shapes=[
            pltpu.SMEM((1, 1, 4), jnp.int32),
            pltpu.VMEM((2, HW), F32),
            pltpu.SMEM((STEPS,), F32),
            pltpu.VMEM((2, ROWS, HW), BF16),
            pltpu.VMEM((TOK, HW), BF16),
            pltpu.VMEM((TOK, HW), F32),
            pltpu.VMEM((HEADS, TOK, HD), F32),
            pltpu.VMEM((HEADS, TOK, HD), F32),
            pltpu.VMEM((STEPS, 8, HD), F32),
            pltpu.VMEM((STEPS, 4, 8, HD), F32),
            pltpu.VMEM((4 * TOK, HD), F32),
            pltpu.VMEM((5, 8, HD), F32),
            pltpu.VMEM((TOK, HD), F32),
            dma((6,)),
            dma((2, RING)),
            dma((2, 16, 2)),
            dma((2, 16, 2)),
            dma((STEPS, 2, 2, GROUPS)),
            dma((STEPS, 4, GROUPS)),
            dma((STEPS, 2, 2)),
            dma((STEPS, 4)),
        ],
        compiler_params=pltpu.CompilerParams(
            collective_id=0, has_side_effects=True, vmem_limit_bytes=32 * 1024 * 1024
        ),
        cost_estimate=pl.CostEstimate(flops=760_000_000, bytes_accessed=1_200_000, transcendentals=1_600_000),
    )(*operands)
    return pl.pallas_call(
        hand_over,
        out_shape=(jax.ShapeDtypeStruct((1, TOK, HW), BF16),) * 2,
        in_specs=[vmem] * 2,
        out_specs=(hbm,) * 2,
        scratch_shapes=[dma((2, PIECES))],
    )(*(pltpu.with_memory_space_constraint(x, pltpu.VMEM) for x in results))


def solution(mesh):
    in_specs = (P("tm", "space", None), P(None, "tm", "space"), P("tm", "space", None), P(), P())
    out_specs = (P("tm", "space", None), P("tm", "space", None))
    return jax.shard_map(
        per_device, mesh=mesh, in_specs=in_specs, out_specs=out_specs, check_vma=False
    )
```

```python
import math

import jax
import jax.numpy as jnp
from jax import lax
from jax.experimental import pallas as pl
from jax.experimental.pallas import tpu as pltpu
from jax.sharding import PartitionSpec as P

HD = 128
HEADS = 20
HW = HD * HEADS
TOK = 64
STEPS = 2
SHARD = 16
GROUPS = 4
PER = HEADS // GROUPS
GW = PER * HD
BATCH = 20
EPS = 1e-6
SCORE_SCALE = math.log2(math.e) / math.sqrt(HD)
MASKED = -1e30
MESH = pl.DeviceIdType.MESH
F32 = jnp.float32
BF16 = jnp.bfloat16

STAGE = 128
NEAR, FAR = 3, 4
TILES = 3 * STAGE
ROWS = TILES + STEPS * 2 * STAGE
CHIP = TOK
RING = 14


def kernel(
    latent_hbm, cache_hbm, mask_hbm, gains_hbm, steps_hbm,
    denoised_ref, velocity_ref,
    mask_ref, gains_ref, steps_ref, buf, query, accum, peak, total, scale_own, scale_in, scale_col, bias, square,
    local_sem, ysend, ssend, yrecv, zsend, zrecv, rsend, rrecv,
):
    tm, space = lax.axis_index("tm"), lax.axis_index("space")
    n_tm, n_space = lax.axis_size("tm"), lax.axis_size("space")
    along_y = ((lax.rem(tm + 2, n_tm), space), (lax.rem(tm + n_tm - 2, n_tm), space))
    sibling = (tm + 1 - 2 * lax.rem(tm, 2), space)
    along_z = ((tm, lax.rem(space + 1, n_space)), (tm, lax.rem(space + n_space - 1, n_space)))
    has_low, has_high = space > 0, space < n_space - 1
    sends = ((has_high, has_low & has_high), (has_low, has_low & has_high))
    receives = ((has_low, space > 1), (has_high, space < n_space - 2))

    def remote(src, dst, send, recv, device):
        return pltpu.make_async_remote_copy(
            src_ref=src, dst_ref=dst, send_sem=send, recv_sem=recv, device_id=device, device_id_type=MESH
        )

    def half_cols(half):
        return pl.ds(pl.multiple_of(half * (HW // 2), HW // 2), HW // 2)

    def shard(which, index, half):
        rows = CHIP + SHARD * index + jnp.where(index >= 2, 2 * SHARD, 0)
        return buf.at[which, pl.ds(pl.multiple_of(rows, SHARD), SHARD), half_cols(half)]

    def slot(distance, direction):
        return 4 * distance - 2 + jnp.where(distance == 4, 0, 2 * direction)

    def ring_place(direction, number):
        which = lax.rem(number // 2 + direction, 2)
        return which, lax.rem(number, 2), number // 4 + 1

    def ring_copy(direction, number, own):
        which, half, distance = ring_place(direction, number)
        target = slot(distance, direction)
        if own:
            src = cache_hbm.at[which, :, half_cols(half)]
        else:
            src = shard(which, jnp.where(distance == 1, 0, slot(distance - 1, direction)), half)
        return remote(
            src, shard(which, target, half), ysend.at[direction, number], yrecv.at[which, target, half],
            along_y[direction],
        )

    def sib_copy(which, half, target, own=False):
        src = cache_hbm.at[which, :, half_cols(half)] if own else shard(which, target - 1, half)
        return remote(
            src, shard(which, target, half), ssend.at[which, target, half], yrecv.at[which, target, half], sibling
        )

    def ring_round(number):
        for direction in range(2):
            which, half, distance = ring_place(direction, number)
            ring_copy(direction, number, False).wait_recv()

            @pl.when(number + 1 < RING)
            def _():
                ring_copy(direction, number + 1, False).wait_send()

            @pl.when(number + 3 < RING)
            def _():
                ring_copy(direction, number + 3, False).start()

            sib_copy(which, half, slot(distance, direction) + 1).start()

    def each_sibling(first, count, act):
        def body(i, _):
            act(sib_copy(lax.rem(i, 2), lax.rem(i // 2, 2), first + 2 * (i // 4)))
            return 0

        lax.fori_loop(0, 4 * count, body, 0)

    def columns(group):
        return pl.ds(pl.multiple_of(group * GW, GW), GW)

    def head_cols(head):
        return pl.ds(pl.multiple_of(head * HD, HD), HD)

    def tile_rows(phase, number):
        return pl.ds(pl.multiple_of(TILES + phase * 2 * STAGE + number * TOK, TOK), TOK)

    def tile_part(phase, number, cols):
        return buf.at[1, tile_rows(phase, number), cols]

    def tile_copy(phase, direction, hop, group, from_hbm=False):
        cols = columns(group)
        if hop == 1:
            src = tile_part(phase, direction, cols)
        elif from_hbm:
            src = latent_hbm.at[0, :, cols]
        else:
            src = buf.at[1, pl.ds(0, TOK), cols]
        target = 2 * hop + direction
        return remote(
            src, tile_part(phase, target, cols), zsend.at[phase, direction, hop, group],
            zrecv.at[phase, target, group], along_z[direction],
        )

    def scale_copy(phase, direction, hop):
        src = scale_own.at[phase] if hop == 0 else scale_in.at[phase, direction]
        target = 2 * hop + direction
        return remote(
            src, scale_in.at[phase, target], rsend.at[phase, direction, hop], rrecv.at[phase, target], along_z[direction]
        )

    def start_tile(phase, hop, group, from_hbm=False):
        for direction in range(2):
            @pl.when(sends[direction][hop])
            def _():
                tile_copy(phase, direction, hop, group, from_hbm).start()

    def tile_left(phase, hop, group):
        for direction in range(2):
            @pl.when(sends[direction][hop])
            def _():
                tile_copy(phase, direction, hop, group).wait_send()

    def wait_tile(phase, hop, group):
        for direction in range(2):
            @pl.when(receives[direction][hop])
            def _():
                tile_copy(phase, direction, hop, group).wait_recv()

        if hop == 0:
            @pl.when(group < GROUPS - 1)
            def _():
                tile_left(phase, 0, group + 1)

            @pl.when(group == GROUPS - 1)
            def _():
                tile_left(phase, 1, 0)

            @pl.when(group == 0)
            def _():
                start_tile(phase, 0, GROUPS - 1)

            @pl.when(group > 0)
            def _():
                start_tile(phase, 1, group - 1)
        elif group == 0:
            tile_left(phase, 1, 1)
            start_tile(phase, 1, GROUPS - 1)

    diagonal = lax.broadcasted_iota(jnp.int32, (TOK, HD), 0) == lax.broadcasted_iota(jnp.int32, (TOK, HD), 1)

    def take_scales(phase, hop):
        for direction in range(2):
            target = 2 * hop + direction

            @pl.when(receives[direction][hop])
            def _():
                scale_copy(phase, direction, hop).wait_recv()

            if hop == 0:
                @pl.when(sends[direction][1])
                def _():
                    scale_copy(phase, direction, 1).start()

            row = jnp.broadcast_to(scale_in[phase, target, 0:1, :], (TOK, HD))
            col = jnp.sum(jnp.where(diagonal, row, 0.0), axis=1, keepdims=True)
            scale_col[pl.ds(target * TOK, TOK), :] = jnp.broadcast_to(col, (TOK, HD))

    def root_scale():
        mean = jnp.sum(square[...], axis=1, keepdims=True) * (1.0 / HW)
        return jnp.broadcast_to(lax.rsqrt(mean + EPS), (TOK, HD))

    def send_scale(phase, col):
        row = jnp.sum(jnp.where(diagonal, col, 0.0), axis=0, keepdims=True)
        scale_own[phase] = jnp.broadcast_to(row, (8, HD))
        for direction in range(2):
            @pl.when(sends[direction][0])
            def _():
                scale_copy(phase, direction, 0).start()

    def begin_heads(col):
        def body(group, _):
            heads = [group * PER + i for i in range(PER)]
            normals = [buf[1, pl.ds(0, TOK), head_cols(head)].astype(F32) * col for head in heads]
            for head, normal in zip(heads, normals):
                cols = head_cols(head)
                query[:, cols] = (normal * gains_ref[0:1, cols]).astype(BF16)
                buf[0, pl.ds(0, TOK), cols] = (normal * gains_ref[1:2, cols]).astype(BF16)
                peak[head] = jnp.full((TOK, HD), MASKED, F32)
                total[head] = jnp.zeros((TOK, HD), F32)
                accum[:, cols] = jnp.zeros((TOK, HD), F32)
            return 0

        lax.fori_loop(0, GROUPS, body, 0)

    def tile_keys(stage, phase, heads):
        scales = scale_col[pl.ds(pl.multiple_of((stage - NEAR) * STAGE, STAGE), STAGE), :]
        source = pl.ds(pl.multiple_of((stage + phase * 2) * STAGE, STAGE), STAGE)
        return [
            (buf[1, source, head_cols(head)].astype(F32) * scales * gains_ref[1:2, head_cols(head)]).astype(BF16)
            for head in heads
        ]

    def update(stage, phase, heads):
        cols = [head_cols(head) for head in heads]
        value_stage = stage + phase * 2 if stage >= NEAR else stage
        value_rows = pl.ds(pl.multiple_of(value_stage * STAGE, STAGE), STAGE)
        allowed = bias[stage, 0:1, :]
        if stage >= NEAR:
            keys = tile_keys(stage, phase, heads)
        else:
            keys = [buf[0, value_rows, c] for c in cols]
        queries = [query[:, c] for c in cols]
        old_peaks = [peak[head] for head in heads]
        scores = [
            lax.dot_general(q, k, (((1,), (1,)), ((), ())), preferred_element_type=F32) * SCORE_SCALE + allowed
            for q, k in zip(queries, keys)
        ]
        peaks = [
            jnp.maximum(old, jnp.broadcast_to(jnp.max(s, axis=1, keepdims=True), (TOK, HD)))
            for old, s in zip(old_peaks, scores)
        ]
        expos = [jnp.exp2(s - p) for s, p in zip(scores, peaks)]
        values = [buf[1, value_rows, c] for c in cols]
        mixed = [jnp.dot(e.astype(BF16), v, preferred_element_type=F32) for e, v in zip(expos, values)]
        factors = [jnp.exp2(old - new) for old, new in zip(old_peaks, peaks)]
        totals = [total[head] * f + e for head, f, e in zip(heads, factors, expos)]
        sums = [accum[:, c] * f + m for c, f, m in zip(cols, factors, mixed)]
        for i, head in enumerate(heads):
            peak[head] = peaks[i]
            total[head] = totals[i]
            accum[:, cols[i]] = sums[i]

    def finish(group, _):
        heads = [group * PER + i for i in range(PER)]
        squares = square[...]
        attended = [accum[:, head_cols(head)] / jnp.sum(total[head], axis=1, keepdims=True) for head in heads]
        for head, values in zip(heads, attended):
            accum[:, head_cols(head)] = values
            squares = squares + values * values
        square[...] = squares
        return 0

    loads = [
        pltpu.make_async_copy(latent_hbm.at[0], buf.at[1, pl.ds(0, TOK)], local_sem.at[0]),
        pltpu.make_async_copy(cache_hbm.at[0], buf.at[0, pl.ds(CHIP, SHARD)], local_sem.at[1]),
        pltpu.make_async_copy(cache_hbm.at[1], buf.at[1, pl.ds(CHIP, SHARD)], local_sem.at[2]),
        pltpu.make_async_copy(mask_hbm, mask_ref, local_sem.at[3]),
        pltpu.make_async_copy(gains_hbm, gains_ref, local_sem.at[4]),
        pltpu.make_async_copy(steps_hbm, steps_ref, local_sem.at[5]),
    ]
    for load in loads:
        load.start()
    barrier = pltpu.get_barrier_semaphore()
    for device in (*along_y, sibling):
        pl.semaphore_signal(barrier, inc=1, device_id=device, device_id_type=MESH)
    for direction in range(2):
        @pl.when(sends[direction][0])
        def _():
            pl.semaphore_signal(barrier, inc=1, device_id=along_z[direction], device_id_type=MESH)

    pl.semaphore_wait(barrier, 3 + lax.min(space, 1) + lax.min(n_space - 1 - space, 1))

    for number in range(2):
        for direction in range(2):
            ring_copy(direction, number, True).start()
    for group in range(2):
        start_tile(0, 0, group, True)
    for which in range(2):
        for half in range(2):
            sib_copy(which, half, 1, True).start()

    for hop in range(2):
        for direction in range(2):
            @pl.when(jnp.logical_not(receives[direction][hop]))
            def _():
                for phase in range(STEPS):
                    buf[1, tile_rows(phase, 2 * hop + direction), :] = jnp.zeros((TOK, HW), BF16)
                    scale_in[phase, 2 * hop + direction] = jnp.zeros((8, HD), F32)

    for which in range(2):
        for stage in (0, 2):
            buf[which, pl.ds(stage * STAGE + 3 * STAGE // 4, STAGE // 4), :] = jnp.zeros((STAGE // 4, HW), BF16)

    for load in loads[3:]:
        load.wait()
    lane = lax.broadcasted_iota(jnp.int32, (8, HD), 1)
    for stage in (0, 2):
        bias[stage] = jnp.where(lane < 3 * STAGE // 4, 0.0, MASKED).astype(F32)
    bias[1] = jnp.zeros((8, HD), F32)
    for hop in range(2):
        low, high = (1, 2) if hop == 0 else (0, 3)
        low_ok = (mask_ref[0, 0, low] > 0) & (space - hop > 0)
        high_ok = (mask_ref[0, 0, high] > 0) & (space + hop + 1 < n_space)
        low_bias = jnp.where(low_ok, 0.0, MASKED).astype(F32)
        high_bias = jnp.where(high_ok, 0.0, MASKED).astype(F32)
        bias[NEAR + hop] = jnp.where(lane < TOK, low_bias, high_bias)

    loads[0].wait()
    square[...] = jnp.zeros((TOK, HD), F32)

    def add_squares(group, _):
        squares = square[...]
        for i in range(PER):
            values = buf[1, pl.ds(0, TOK), head_cols(group * PER + i)].astype(F32)
            squares = squares + values * values
        square[...] = squares
        return 0

    lax.fori_loop(0, GROUPS, add_squares, 0)
    col = root_scale()
    send_scale(0, col)
    for load in loads[1:3]:
        load.wait()
    for direction in range(2):
        ring_copy(direction, 0, True).wait_send()
        ring_copy(direction, 2, False).start()
    begin_heads(col)

    def phase_body(phase, _):
        first = phase == 0
        square[...] = jnp.zeros((TOK, HD), F32)

        def heads_of(part, count):
            return [part * count + i for i in range(count)]

        def arrive(hop, group, rounds=True):
            if rounds:
                @pl.when(first)
                def _():
                    ring_round(8 * hop + 2 * group)
                    ring_round(8 * hop + 2 * group + 1)

            wait_tile(phase, hop, group)

        @pl.when(first)
        def _():
            each_sibling(1, 1, lambda copy: copy.wait_recv())

        def stored(stage):
            def body(part, _):
                update(stage, phase, heads_of(part, BATCH))
                return 0

            lax.fori_loop(0, HEADS // BATCH, body, 0)

        stored(0)
        tile_left(phase, 0, 0)
        start_tile(phase, 0, 2)

        @pl.when(jnp.logical_not(first))
        def _():
            stored(1)
            stored(2)

        def near(part, _):
            arrive(0, 2 * part)

            @pl.when(part == 0)
            def _():
                take_scales(phase, 0)

            arrive(0, 2 * part + 1)
            update(NEAR, phase, heads_of(part, 2 * PER))
            return 0

        lax.fori_loop(0, GROUPS // 2, near, 0)

        @pl.when(first)
        def _():
            each_sibling(3, 4, lambda copy: copy.wait_recv())
            stored(1)

        arrive(1, 0)
        take_scales(phase, 1)
        arrive(1, 1)
        update(FAR, phase, heads_of(0, 2 * PER))
        arrive(1, 2)
        update(FAR, phase, heads_of(2, PER))

        @pl.when(first)
        def _():
            each_sibling(11, 3, lambda copy: copy.wait_recv())
            stored(2)

        lax.fori_loop(0, 3, finish, 0)
        arrive(1, 3, rounds=False)
        update(FAR, phase, heads_of(3, PER))
        finish(3, 0)

        @pl.when(first)
        def _():
            col = root_scale()
            step_size = steps_ref[0]
            square[...] = jnp.zeros((TOK, HD), F32)

            def move(group, _):
                squares = square[...]
                cols = [head_cols(group * PER + i) for i in range(PER)]
                moved = [
                    (buf[1, pl.ds(0, TOK), c].astype(F32) + step_size * (accum[:, c] * col)).astype(BF16)
                    for c in cols
                ]
                for c, values in zip(cols, moved):
                    buf[1, pl.ds(0, TOK), c] = values
                    wide = values.astype(F32)
                    squares = squares + wide * wide
                square[...] = squares

                @pl.when(group < 2)
                def _():
                    start_tile(1, 0, group)

                return 0

            lax.fori_loop(0, GROUPS, move, 0)
            col = root_scale()
            send_scale(1, col)
            begin_heads(col)

        return 0

    lax.fori_loop(0, STEPS, phase_body, 0)

    col = root_scale()
    last_size = steps_ref[STEPS - 1]

    def put(group, _):
        cols = [head_cols(group * PER + i) for i in range(PER)]
        velocities = [accum[:, c] * col for c in cols]
        moved = [buf[1, pl.ds(0, TOK), c].astype(F32) + last_size * v for c, v in zip(cols, velocities)]
        for c, velocity, denoised in zip(cols, velocities, moved):
            denoised_ref[0, :, c] = denoised.astype(BF16)
            velocity_ref[0, :, c] = velocity.astype(BF16)
        return 0

    lax.fori_loop(0, GROUPS, put, 0)

    for which in range(2):
        for half in range(2):
            sib_copy(which, half, 1, True).wait_send()
    each_sibling(3, 7, lambda copy: copy.wait_send())
    for phase in range(STEPS):
        for direction in range(2):
            for hop in range(2):
                @pl.when(sends[direction][hop])
                def _():
                    scale_copy(phase, direction, hop).wait_send()

        for group in range(2, GROUPS):
            tile_left(phase, 1, group)


PIECE = 16
PIECES = TOK // PIECE


def hand_over(denoised_in, velocity_in, denoised_out, velocity_out, sems):
    copies = [
        pltpu.make_async_copy(source.at[0, pl.ds(PIECE * i, PIECE)], target.at[0, pl.ds(PIECE * i, PIECE)], sems.at[which, i])
        for i in range(PIECES)
        for which, (source, target) in enumerate(((denoised_in, denoised_out), (velocity_in, velocity_out)))
    ]
    for copy in copies:
        copy.start()
    for copy in copies:
        copy.wait()


def per_device(latent, past_cache, neighbour_mask, gains, step_sizes):
    dma = pltpu.SemaphoreType.DMA
    hbm = pl.BlockSpec(memory_space=pltpu.HBM)
    vmem = pl.BlockSpec(memory_space=pltpu.VMEM)
    operands = [
        pltpu.with_memory_space_constraint(x, pltpu.HBM)
        for x in (latent, past_cache, neighbour_mask, gains, step_sizes)
    ]
    results = pl.pallas_call(
        kernel,
        out_shape=(pltpu.VMEM((1, TOK, HW), BF16),) * 2,
        in_specs=[hbm] * 5,
        out_specs=(vmem,) * 2,
        scratch_shapes=[
            pltpu.SMEM((1, 1, 4), jnp.int32),
            pltpu.VMEM((2, HW), F32),
            pltpu.SMEM((STEPS,), F32),
            pltpu.VMEM((2, ROWS, HW), BF16),
            pltpu.VMEM((TOK, HW), BF16),
            pltpu.VMEM((TOK, HW), F32),
            pltpu.VMEM((HEADS, TOK, HD), F32),
            pltpu.VMEM((HEADS, TOK, HD), F32),
            pltpu.VMEM((STEPS, 8, HD), F32),
            pltpu.VMEM((STEPS, 4, 8, HD), F32),
            pltpu.VMEM((4 * TOK, HD), F32),
            pltpu.VMEM((5, 8, HD), F32),
            pltpu.VMEM((TOK, HD), F32),
            dma((6,)),
            dma((2, RING)),
            dma((2, 16, 2)),
            dma((2, 16, 2)),
            dma((STEPS, 2, 2, GROUPS)),
            dma((STEPS, 4, GROUPS)),
            dma((STEPS, 2, 2)),
            dma((STEPS, 4)),
        ],
        compiler_params=pltpu.CompilerParams(
            collective_id=0, has_side_effects=True, vmem_limit_bytes=32 * 1024 * 1024
        ),
        cost_estimate=pl.CostEstimate(flops=760_000_000, bytes_accessed=1_200_000, transcendentals=1_600_000),
    )(*operands)
    return pl.pallas_call(
        hand_over,
        out_shape=(jax.ShapeDtypeStruct((1, TOK, HW), BF16),) * 2,
        in_specs=[vmem] * 2,
        out_specs=(hbm,) * 2,
        scratch_shapes=[dma((2, PIECES))],
    )(*(pltpu.with_memory_space_constraint(x, pltpu.VMEM) for x in results))


def solution(mesh):
    in_specs = (P("tm", "space", None), P(None, "tm", "space"), P("tm", "space", None), P(), P())
    out_specs = (P("tm", "space", None), P("tm", "space", None))
    return jax.shard_map(
        per_device, mesh=mesh, in_specs=in_specs, out_specs=out_specs, check_vma=False
    )
```

```python
import math

import jax
import jax.numpy as jnp
from jax import lax
from jax.experimental import pallas as pl
from jax.experimental.pallas import tpu as pltpu
from jax.sharding import PartitionSpec as P

HD = 128
HEADS = 20
HW = HD * HEADS
TOK = 64
STEPS = 2
SHARD = 16
GROUPS = 4
PER = HEADS // GROUPS
GW = PER * HD
BATCH = 20
EPS = 1e-6
SCORE_SCALE = math.log2(math.e) / math.sqrt(HD)
MASKED = -1e30
MESH = pl.DeviceIdType.MESH
F32 = jnp.float32
BF16 = jnp.bfloat16

STAGE = 128
NEAR, FAR = 3, 4
TILES = 3 * STAGE
ROWS = TILES + STEPS * 2 * STAGE
CHIP = TOK
RING = 14


def kernel(
    latent_hbm, cache_hbm, mask_hbm, gains_hbm, steps_hbm,
    denoised_ref, velocity_ref,
    mask_ref, gains_ref, steps_ref, buf, query, accum, peak, total, scale_own, scale_in, scale_col, bias, square,
    local_sem, ysend, ssend, yrecv, zsend, zrecv, rsend, rrecv,
):
    tm, space = lax.axis_index("tm"), lax.axis_index("space")
    n_tm, n_space = lax.axis_size("tm"), lax.axis_size("space")
    along_y = ((lax.rem(tm + 2, n_tm), space), (lax.rem(tm + n_tm - 2, n_tm), space))
    sibling = (tm + 1 - 2 * lax.rem(tm, 2), space)
    along_z = ((tm, lax.rem(space + 1, n_space)), (tm, lax.rem(space + n_space - 1, n_space)))
    has_low, has_high = space > 0, space < n_space - 1
    sends = ((has_high, has_low & has_high), (has_low, has_low & has_high))
    receives = ((has_low, space > 1), (has_high, space < n_space - 2))

    def remote(src, dst, send, recv, device):
        return pltpu.make_async_remote_copy(
            src_ref=src, dst_ref=dst, send_sem=send, recv_sem=recv, device_id=device, device_id_type=MESH
        )

    def half_cols(half):
        return pl.ds(pl.multiple_of(half * (HW // 2), HW // 2), HW // 2)

    def shard(which, index, half):
        rows = CHIP + SHARD * index + jnp.where(index >= 2, 2 * SHARD, 0)
        return buf.at[which, pl.ds(pl.multiple_of(rows, SHARD), SHARD), half_cols(half)]

    def slot(distance, direction):
        return 4 * distance - 2 + jnp.where(distance == 4, 0, 2 * direction)

    def ring_place(direction, number):
        which = lax.rem(number // 2 + direction, 2)
        return which, lax.rem(number, 2), number // 4 + 1

    def ring_copy(direction, number, own):
        which, half, distance = ring_place(direction, number)
        target = slot(distance, direction)
        if own:
            src = cache_hbm.at[which, :, half_cols(half)]
        else:
            src = shard(which, slot(distance - 1, direction), half)
        return remote(
            src, shard(which, target, half), ysend.at[direction, number], yrecv.at[which, target, half],
            along_y[direction],
        )

    def sib_copy(which, half, target, own=False):
        src = cache_hbm.at[which, :, half_cols(half)] if own else shard(which, target - 1, half)
        return remote(
            src, shard(which, target, half), ssend.at[which, target, half], yrecv.at[which, target, half], sibling
        )

    def ring_round(number):
        for direction in range(2):
            which, half, distance = ring_place(direction, number)
            ring_copy(direction, number, False).wait_recv()

            @pl.when(number + 4 < RING)
            def _():
                ring_copy(direction, number + 4, False).start()

            sib_copy(which, half, slot(distance, direction) + 1).start()

    def each_sibling(first, count, act):
        def body(i, _):
            act(sib_copy(lax.rem(i, 2), lax.rem(i // 2, 2), first + 2 * (i // 4)))
            return 0

        lax.fori_loop(0, 4 * count, body, 0)

    def columns(group):
        return pl.ds(pl.multiple_of(group * GW, GW), GW)

    def head_cols(head):
        return pl.ds(pl.multiple_of(head * HD, HD), HD)

    def tile_rows(phase, number):
        return pl.ds(pl.multiple_of(TILES + phase * 2 * STAGE + number * TOK, TOK), TOK)

    def tile_part(phase, number, cols):
        return buf.at[1, tile_rows(phase, number), cols]

    def tile_copy(phase, direction, hop, group):
        cols = columns(group)
        if hop == 1:
            src = tile_part(phase, direction, cols)
        elif isinstance(phase, int) and phase == 0:
            src = latent_hbm.at[0, :, cols]
        else:
            src = buf.at[1, pl.ds(0, TOK), cols]
        target = 2 * hop + direction
        return remote(
            src, tile_part(phase, target, cols), zsend.at[phase, direction, hop, group],
            zrecv.at[phase, target, group], along_z[direction],
        )

    def scale_copy(phase, direction, hop):
        src = scale_own.at[phase] if hop == 0 else scale_in.at[phase, direction]
        target = 2 * hop + direction
        return remote(
            src, scale_in.at[phase, target], rsend.at[phase, direction, hop], rrecv.at[phase, target], along_z[direction]
        )

    def start_tile(phase, hop, group):
        for direction in range(2):
            @pl.when(sends[direction][hop])
            def _():
                tile_copy(phase, direction, hop, group).start()

    def wait_tile(phase, hop, group):
        for direction in range(2):
            @pl.when(receives[direction][hop])
            def _():
                tile_copy(phase, direction, hop, group).wait_recv()

        if hop == 0:
            start_tile(phase, 1, group)

    diagonal = lax.broadcasted_iota(jnp.int32, (TOK, HD), 0) == lax.broadcasted_iota(jnp.int32, (TOK, HD), 1)

    def take_scales(phase, hop):
        for direction in range(2):
            target = 2 * hop + direction

            @pl.when(receives[direction][hop])
            def _():
                scale_copy(phase, direction, hop).wait_recv()

            if hop == 0:
                @pl.when(sends[direction][1])
                def _():
                    scale_copy(phase, direction, 1).start()

            row = jnp.broadcast_to(scale_in[phase, target, 0:1, :], (TOK, HD))
            col = jnp.sum(jnp.where(diagonal, row, 0.0), axis=1, keepdims=True)
            scale_col[pl.ds(target * TOK, TOK), :] = jnp.broadcast_to(col, (TOK, HD))

    def root_scale():
        mean = jnp.sum(square[...], axis=1, keepdims=True) * (1.0 / HW)
        return jnp.broadcast_to(lax.rsqrt(mean + EPS), (TOK, HD))

    def send_scale(phase, col):
        row = jnp.sum(jnp.where(diagonal, col, 0.0), axis=0, keepdims=True)
        scale_own[phase] = jnp.broadcast_to(row, (8, HD))
        for direction in range(2):
            @pl.when(sends[direction][0])
            def _():
                scale_copy(phase, direction, 0).start()

    def begin_heads(col):
        def body(group, _):
            heads = [group * PER + i for i in range(PER)]
            normals = [buf[1, pl.ds(0, TOK), head_cols(head)].astype(F32) * col for head in heads]
            for head, normal in zip(heads, normals):
                cols = head_cols(head)
                query[:, cols] = (normal * gains_ref[0:1, cols]).astype(BF16)
                buf[0, pl.ds(0, TOK), cols] = (normal * gains_ref[1:2, cols]).astype(BF16)
                peak[head] = jnp.full((TOK, HD), MASKED, F32)
                total[head] = jnp.zeros((TOK, HD), F32)
                accum[:, cols] = jnp.zeros((TOK, HD), F32)
            return 0

        lax.fori_loop(0, GROUPS, body, 0)

    def tile_keys(stage, phase, heads):
        scales = scale_col[pl.ds(pl.multiple_of((stage - NEAR) * STAGE, STAGE), STAGE), :]
        source = pl.ds(pl.multiple_of((stage + phase * 2) * STAGE, STAGE), STAGE)
        return [
            (buf[1, source, head_cols(head)].astype(F32) * scales * gains_ref[1:2, head_cols(head)]).astype(BF16)
            for head in heads
        ]

    def update(stage, phase, heads):
        cols = [head_cols(head) for head in heads]
        value_stage = stage + phase * 2 if stage >= NEAR else stage
        value_rows = pl.ds(pl.multiple_of(value_stage * STAGE, STAGE), STAGE)
        allowed = bias[stage, 0:1, :]
        if stage >= NEAR:
            keys = tile_keys(stage, phase, heads)
        else:
            keys = [buf[0, value_rows, c] for c in cols]
        queries = [query[:, c] for c in cols]
        old_peaks = [peak[head] for head in heads]
        scores = [
            lax.dot_general(q, k, (((1,), (1,)), ((), ())), preferred_element_type=F32) * SCORE_SCALE + allowed
            for q, k in zip(queries, keys)
        ]
        peaks = [
            jnp.maximum(old, jnp.broadcast_to(jnp.max(s, axis=1, keepdims=True), (TOK, HD)))
            for old, s in zip(old_peaks, scores)
        ]
        expos = [jnp.exp2(s - p) for s, p in zip(scores, peaks)]
        values = [buf[1, value_rows, c] for c in cols]
        mixed = [jnp.dot(e.astype(BF16), v, preferred_element_type=F32) for e, v in zip(expos, values)]
        factors = [jnp.exp2(old - new) for old, new in zip(old_peaks, peaks)]
        totals = [total[head] * f + e for head, f, e in zip(heads, factors, expos)]
        sums = [accum[:, c] * f + m for c, f, m in zip(cols, factors, mixed)]
        for i, head in enumerate(heads):
            peak[head] = peaks[i]
            total[head] = totals[i]
            accum[:, cols[i]] = sums[i]

    def finish(group, _):
        heads = [group * PER + i for i in range(PER)]
        squares = square[...]
        attended = [accum[:, head_cols(head)] / jnp.sum(total[head], axis=1, keepdims=True) for head in heads]
        for head, values in zip(heads, attended):
            accum[:, head_cols(head)] = values
            squares = squares + values * values
        square[...] = squares
        return 0

    loads = [
        pltpu.make_async_copy(latent_hbm.at[0], buf.at[1, pl.ds(0, TOK)], local_sem.at[0]),
        pltpu.make_async_copy(cache_hbm.at[0], buf.at[0, pl.ds(CHIP, SHARD)], local_sem.at[1]),
        pltpu.make_async_copy(cache_hbm.at[1], buf.at[1, pl.ds(CHIP, SHARD)], local_sem.at[2]),
        pltpu.make_async_copy(mask_hbm, mask_ref, local_sem.at[3]),
        pltpu.make_async_copy(gains_hbm, gains_ref, local_sem.at[4]),
        pltpu.make_async_copy(steps_hbm, steps_ref, local_sem.at[5]),
    ]
    for load in loads:
        load.start()
    barrier = pltpu.get_barrier_semaphore()
    for device in (*along_y, sibling):
        pl.semaphore_signal(barrier, inc=1, device_id=device, device_id_type=MESH)
    for direction in range(2):
        @pl.when(sends[direction][0])
        def _():
            pl.semaphore_signal(barrier, inc=1, device_id=along_z[direction], device_id_type=MESH)

    pl.semaphore_wait(barrier, 3 + lax.min(space, 1) + lax.min(n_space - 1 - space, 1))

    for number in range(2):
        for direction in range(2):
            ring_copy(direction, number, True).start()
    start_tile(0, 0, 0)
    for number in range(2, 4):
        for direction in range(2):
            ring_copy(direction, number, True).start()
    for which in range(2):
        for half in range(2):
            sib_copy(which, half, 1, True).start()

    for hop in range(2):
        for direction in range(2):
            @pl.when(jnp.logical_not(receives[direction][hop]))
            def _():
                for phase in range(STEPS):
                    buf[1, tile_rows(phase, 2 * hop + direction), :] = jnp.zeros((TOK, HW), BF16)
                    scale_in[phase, 2 * hop + direction] = jnp.zeros((8, HD), F32)

    for which in range(2):
        for stage in (0, 2):
            buf[which, pl.ds(stage * STAGE + 3 * STAGE // 4, STAGE // 4), :] = jnp.zeros((STAGE // 4, HW), BF16)

    for load in loads[3:]:
        load.wait()
    lane = lax.broadcasted_iota(jnp.int32, (8, HD), 1)
    for stage in (0, 2):
        bias[stage] = jnp.where(lane < 3 * STAGE // 4, 0.0, MASKED).astype(F32)
    bias[1] = jnp.zeros((8, HD), F32)
    for hop in range(2):
        low, high = (1, 2) if hop == 0 else (0, 3)
        low_ok = (mask_ref[0, 0, low] > 0) & (space - hop > 0)
        high_ok = (mask_ref[0, 0, high] > 0) & (space + hop + 1 < n_space)
        low_bias = jnp.where(low_ok, 0.0, MASKED).astype(F32)
        high_bias = jnp.where(high_ok, 0.0, MASKED).astype(F32)
        bias[NEAR + hop] = jnp.where(lane < TOK, low_bias, high_bias)

    loads[0].wait()
    square[...] = jnp.zeros((TOK, HD), F32)

    def add_squares(group, _):
        squares = square[...]
        for i in range(PER):
            values = buf[1, pl.ds(0, TOK), head_cols(group * PER + i)].astype(F32)
            squares = squares + values * values
        square[...] = squares
        return 0

    lax.fori_loop(0, GROUPS, add_squares, 0)
    col = root_scale()
    send_scale(0, col)
    for group in range(1, GROUPS):
        start_tile(0, 0, group)
    begin_heads(col)
    for load in loads[1:3]:
        load.wait()

    def phase_body(phase, _):
        first = phase == 0
        square[...] = jnp.zeros((TOK, HD), F32)

        def heads_of(part, count):
            return [part * count + i for i in range(count)]

        def rounds(start, count):
            @pl.when(first)
            def _():
                for number in range(count):
                    ring_round(start + number)

        @pl.when(first)
        def _():
            each_sibling(1, 1, lambda copy: copy.wait_recv())

        def stored(stage):
            def body(part, _):
                update(stage, phase, heads_of(part, BATCH))
                return 0

            lax.fori_loop(0, HEADS // BATCH, body, 0)

        stored(0)

        @pl.when(jnp.logical_not(first))
        def _():
            stored(1)
            stored(2)

        def near(part, _):
            for i in range(2):
                group = 2 * part + i
                rounds(2 * group, 2)
                wait_tile(phase, 0, group)

            @pl.when(part == 0)
            def _():
                take_scales(phase, 0)

            @pl.when(part == 1)
            def _():
                rounds(8, 2)

            update(NEAR, phase, heads_of(part, 2 * PER))
            return 0

        lax.fori_loop(0, GROUPS // 2, near, 0)

        @pl.when(first)
        def _():
            each_sibling(3, 4, lambda copy: copy.wait_recv())
            stored(1)

        rounds(10, 2)
        wait_tile(phase, 1, 0)
        wait_tile(phase, 1, 1)
        take_scales(phase, 1)
        update(FAR, phase, heads_of(0, 2 * PER))
        rounds(12, 2)
        wait_tile(phase, 1, 2)
        update(FAR, phase, heads_of(2, PER))

        @pl.when(first)
        def _():
            each_sibling(11, 3, lambda copy: copy.wait_recv())
            stored(2)

        lax.fori_loop(0, 3, finish, 0)
        wait_tile(phase, 1, 3)
        update(FAR, phase, heads_of(3, PER))
        finish(3, 0)

        @pl.when(first)
        def _():
            col = root_scale()
            step_size = steps_ref[0]
            square[...] = jnp.zeros((TOK, HD), F32)

            def move(group, _):
                squares = square[...]
                cols = [head_cols(group * PER + i) for i in range(PER)]
                moved = [
                    (buf[1, pl.ds(0, TOK), c].astype(F32) + step_size * (accum[:, c] * col)).astype(BF16)
                    for c in cols
                ]
                for c, values in zip(cols, moved):
                    buf[1, pl.ds(0, TOK), c] = values
                    wide = values.astype(F32)
                    squares = squares + wide * wide
                square[...] = squares

                @pl.when(group == 0)
                def _():
                    start_tile(1, 0, 0)

                return 0

            lax.fori_loop(0, GROUPS, move, 0)
            col = root_scale()
            send_scale(1, col)
            for group in range(1, GROUPS):
                start_tile(1, 0, group)
            begin_heads(col)

        return 0

    lax.fori_loop(0, STEPS, phase_body, 0)

    col = root_scale()
    last_size = steps_ref[STEPS - 1]

    def put(group, _):
        cols = [head_cols(group * PER + i) for i in range(PER)]
        velocities = [accum[:, c] * col for c in cols]
        moved = [buf[1, pl.ds(0, TOK), c].astype(F32) + last_size * v for c, v in zip(cols, velocities)]
        for c, velocity, denoised in zip(cols, velocities, moved):
            denoised_ref[0, :, c] = denoised.astype(BF16)
            velocity_ref[0, :, c] = velocity.astype(BF16)
        return 0

    lax.fori_loop(0, GROUPS, put, 0)

    def ring_left(number, _):
        for direction in range(2):
            ring_copy(direction, number, False).wait_send()
        return 0

    for number in range(4):
        for direction in range(2):
            ring_copy(direction, number, True).wait_send()
    lax.fori_loop(4, RING, ring_left, 0)
    for which in range(2):
        for half in range(2):
            sib_copy(which, half, 1, True).wait_send()
    each_sibling(3, 7, lambda copy: copy.wait_send())
    for direction in range(2):
        for hop in range(2):
            @pl.when(sends[direction][hop])
            def _():
                for phase in range(STEPS):
                    scale_copy(phase, direction, hop).wait_send()
                    for group in range(GROUPS):
                        tile_copy(phase, direction, hop, group).wait_send()


PIECE = 16
PIECES = TOK // PIECE


def hand_over(denoised_in, velocity_in, denoised_out, velocity_out, sems):
    copies = [
        pltpu.make_async_copy(source.at[0, pl.ds(PIECE * i, PIECE)], target.at[0, pl.ds(PIECE * i, PIECE)], sems.at[which, i])
        for i in range(PIECES)
        for which, (source, target) in enumerate(((denoised_in, denoised_out), (velocity_in, velocity_out)))
    ]
    for copy in copies:
        copy.start()
    for copy in copies:
        copy.wait()


def per_device(latent, past_cache, neighbour_mask, gains, step_sizes):
    dma = pltpu.SemaphoreType.DMA
    hbm = pl.BlockSpec(memory_space=pltpu.HBM)
    vmem = pl.BlockSpec(memory_space=pltpu.VMEM)
    operands = [
        pltpu.with_memory_space_constraint(x, pltpu.HBM)
        for x in (latent, past_cache, neighbour_mask, gains, step_sizes)
    ]
    results = pl.pallas_call(
        kernel,
        out_shape=(pltpu.VMEM((1, TOK, HW), BF16),) * 2,
        in_specs=[hbm] * 5,
        out_specs=(vmem,) * 2,
        scratch_shapes=[
            pltpu.SMEM((1, 1, 4), jnp.int32),
            pltpu.VMEM((2, HW), F32),
            pltpu.SMEM((STEPS,), F32),
            pltpu.VMEM((2, ROWS, HW), BF16),
            pltpu.VMEM((TOK, HW), BF16),
            pltpu.VMEM((TOK, HW), F32),
            pltpu.VMEM((HEADS, TOK, HD), F32),
            pltpu.VMEM((HEADS, TOK, HD), F32),
            pltpu.VMEM((STEPS, 8, HD), F32),
            pltpu.VMEM((STEPS, 4, 8, HD), F32),
            pltpu.VMEM((4 * TOK, HD), F32),
            pltpu.VMEM((5, 8, HD), F32),
            pltpu.VMEM((TOK, HD), F32),
            dma((6,)),
            dma((2, RING)),
            dma((2, 16, 2)),
            dma((2, 16, 2)),
            dma((STEPS, 2, 2, GROUPS)),
            dma((STEPS, 4, GROUPS)),
            dma((STEPS, 2, 2)),
            dma((STEPS, 4)),
        ],
        compiler_params=pltpu.CompilerParams(
            collective_id=0, has_side_effects=True, vmem_limit_bytes=32 * 1024 * 1024
        ),
        cost_estimate=pl.CostEstimate(flops=760_000_000, bytes_accessed=1_200_000, transcendentals=1_600_000),
    )(*operands)
    return pl.pallas_call(
        hand_over,
        out_shape=(jax.ShapeDtypeStruct((1, TOK, HW), BF16),) * 2,
        in_specs=[vmem] * 2,
        out_specs=(hbm,) * 2,
        scratch_shapes=[dma((2, PIECES))],
    )(*(pltpu.with_memory_space_constraint(x, pltpu.VMEM) for x in results))


def solution(mesh):
    in_specs = (P("tm", "space", None), P(None, "tm", "space"), P("tm", "space", None), P(), P())
    out_specs = (P("tm", "space", None), P("tm", "space", None))
    return jax.shard_map(
        per_device, mesh=mesh, in_specs=in_specs, out_specs=out_specs, check_vma=False
    )
```

```python
import math

import jax
import jax.numpy as jnp
from jax import lax
from jax.experimental import pallas as pl
from jax.experimental.pallas import tpu as pltpu
from jax.sharding import PartitionSpec as P

HD = 128
HEADS = 20
HW = HD * HEADS
TOK = 64
STEPS = 2
SHARD = 16
GROUPS = 4
PER = HEADS // GROUPS
GW = PER * HD
EPS = 1e-6
SCORE_SCALE = math.log2(math.e) / math.sqrt(HD)
MASKED = -1e30
MESH = pl.DeviceIdType.MESH
F32 = jnp.float32
BF16 = jnp.bfloat16

STAGE = 128
NEAR, FAR = 3, 4
TILES = 3 * STAGE
ROWS = TILES + STEPS * 2 * STAGE
CHIP = TOK
RING = 14


def kernel(
    latent_hbm, cache_hbm, mask_hbm, gains_hbm, steps_hbm,
    denoised_ref, velocity_ref,
    mask_ref, gains_ref, steps_ref, buf, query, accum, peak, total, scale_own, scale_in, scale_col, bias, square,
    local_sem, ysend, ssend, yrecv, zsend, zrecv, rsend, rrecv,
):
    tm, space = lax.axis_index("tm"), lax.axis_index("space")
    n_tm, n_space = lax.axis_size("tm"), lax.axis_size("space")
    along_y = ((lax.rem(tm + 2, n_tm), space), (lax.rem(tm + n_tm - 2, n_tm), space))
    sibling = (tm + 1 - 2 * lax.rem(tm, 2), space)
    along_z = ((tm, lax.rem(space + 1, n_space)), (tm, lax.rem(space + n_space - 1, n_space)))
    has_low, has_high = space > 0, space < n_space - 1
    sends = ((has_high, has_low & has_high), (has_low, has_low & has_high))
    receives = ((has_low, space > 1), (has_high, space < n_space - 2))

    def remote(src, dst, send, recv, device):
        return pltpu.make_async_remote_copy(
            src_ref=src, dst_ref=dst, send_sem=send, recv_sem=recv, device_id=device, device_id_type=MESH
        )

    def half_cols(half):
        return pl.ds(pl.multiple_of(half * (HW // 2), HW // 2), HW // 2)

    def shard(which, index, half):
        rows = CHIP + SHARD * index + jnp.where(index >= 2, 2 * SHARD, 0)
        return buf.at[which, pl.ds(pl.multiple_of(rows, SHARD), SHARD), half_cols(half)]

    def slot(distance, direction):
        return 4 * distance - 2 + jnp.where(distance == 4, 0, 2 * direction)

    def ring_place(direction, number):
        which = lax.rem(number // 2 + direction, 2)
        return which, lax.rem(number, 2), number // 4 + 1

    def ring_copy(direction, number, own):
        which, half, distance = ring_place(direction, number)
        target = slot(distance, direction)
        if own:
            src = cache_hbm.at[which, :, half_cols(half)]
        else:
            src = shard(which, slot(distance - 1, direction), half)
        return remote(
            src, shard(which, target, half), ysend.at[direction, number], yrecv.at[which, target, half],
            along_y[direction],
        )

    def sib_copy(which, half, target, own=False):
        src = cache_hbm.at[which, :, half_cols(half)] if own else shard(which, target - 1, half)
        return remote(
            src, shard(which, target, half), ssend.at[which, target, half], yrecv.at[which, target, half], sibling
        )

    def ring_round(number):
        for direction in range(2):
            which, half, distance = ring_place(direction, number)
            ring_copy(direction, number, False).wait_recv()

            @pl.when(number + 4 < RING)
            def _():
                ring_copy(direction, number + 4, False).start()

            sib_copy(which, half, slot(distance, direction) + 1).start()

    def each_sibling(first, count, act):
        def body(i, _):
            act(sib_copy(lax.rem(i, 2), lax.rem(i // 2, 2), first + 2 * (i // 4)))
            return 0

        lax.fori_loop(0, 4 * count, body, 0)

    def columns(group):
        return pl.ds(pl.multiple_of(group * GW, GW), GW)

    def head_cols(head):
        if isinstance(head, int):
            return pl.ds(head * HD, HD)
        return pl.ds(pl.multiple_of(head * HD, HD), HD)

    def tile_rows(phase, number):
        return pl.ds(pl.multiple_of(TILES + phase * 2 * STAGE + number * TOK, TOK), TOK)

    def tile_part(phase, number, cols):
        return buf.at[1, tile_rows(phase, number), cols]

    def tile_copy(phase, direction, hop, group):
        cols = columns(group)
        if hop == 1:
            src = tile_part(phase, direction, cols)
        elif isinstance(phase, int) and phase == 0:
            src = latent_hbm.at[0, :, cols]
        else:
            src = buf.at[1, pl.ds(0, TOK), cols]
        target = 2 * hop + direction
        return remote(
            src, tile_part(phase, target, cols), zsend.at[phase, direction, hop, group],
            zrecv.at[phase, target, group], along_z[direction],
        )

    def scale_copy(phase, direction, hop):
        src = scale_own.at[phase] if hop == 0 else scale_in.at[phase, direction]
        target = 2 * hop + direction
        return remote(
            src, scale_in.at[phase, target], rsend.at[phase, direction, hop], rrecv.at[phase, target], along_z[direction]
        )

    def start_tile(phase, hop, group):
        for direction in range(2):
            @pl.when(sends[direction][hop])
            def _():
                tile_copy(phase, direction, hop, group).start()

    def wait_tile(phase, hop, group):
        for direction in range(2):
            @pl.when(receives[direction][hop])
            def _():
                tile_copy(phase, direction, hop, group).wait_recv()

        if hop == 0:
            start_tile(phase, 1, group)

    diagonal = lax.broadcasted_iota(jnp.int32, (TOK, HD), 0) == lax.broadcasted_iota(jnp.int32, (TOK, HD), 1)

    def take_scales(phase, hop):
        for direction in range(2):
            target = 2 * hop + direction

            @pl.when(receives[direction][hop])
            def _():
                scale_copy(phase, direction, hop).wait_recv()

            if hop == 0:
                @pl.when(sends[direction][1])
                def _():
                    scale_copy(phase, direction, 1).start()

            row = jnp.broadcast_to(scale_in[phase, target, 0:1, :], (TOK, HD))
            col = jnp.sum(jnp.where(diagonal, row, 0.0), axis=1, keepdims=True)
            scale_col[pl.ds(target * TOK, TOK), :] = jnp.broadcast_to(col, (TOK, HD))

    def root_scale():
        mean = jnp.sum(square[...], axis=1, keepdims=True) * (1.0 / HW)
        return jnp.broadcast_to(lax.rsqrt(mean + EPS), (TOK, HD))

    def send_scale(phase, col):
        row = jnp.sum(jnp.where(diagonal, col, 0.0), axis=0, keepdims=True)
        scale_own[phase] = jnp.broadcast_to(row, (8, HD))
        for direction in range(2):
            @pl.when(sends[direction][0])
            def _():
                scale_copy(phase, direction, 0).start()

    def begin_heads(col):
        def body(group, _):
            heads = [group * PER + i for i in range(PER)]
            normals = [buf[1, pl.ds(0, TOK), head_cols(head)].astype(F32) * col for head in heads]
            for head, normal in zip(heads, normals):
                cols = head_cols(head)
                query[:, cols] = (normal * gains_ref[0:1, cols]).astype(BF16)
                buf[0, pl.ds(0, TOK), cols] = (normal * gains_ref[1:2, cols]).astype(BF16)
                peak[head] = jnp.full((TOK, HD), MASKED, F32)
                total[head] = jnp.zeros((TOK, HD), F32)
                accum[:, cols] = jnp.zeros((TOK, HD), F32)
            return 0

        lax.fori_loop(0, GROUPS, body, 0)

    def tile_keys(stage, phase, heads):
        scales = scale_col[pl.ds(pl.multiple_of((stage - NEAR) * STAGE, STAGE), STAGE), :]
        source = pl.ds(pl.multiple_of((stage + phase * 2) * STAGE, STAGE), STAGE)
        return [
            (buf[1, source, head_cols(head)].astype(F32) * scales * gains_ref[1:2, head_cols(head)]).astype(BF16)
            for head in heads
        ]

    def update(stage, phase, heads):
        cols = [head_cols(head) for head in heads]
        value_stage = stage + phase * 2 if stage >= NEAR else stage
        value_rows = pl.ds(pl.multiple_of(value_stage * STAGE, STAGE), STAGE)
        allowed = bias[stage, 0:1, :]
        if stage >= NEAR:
            keys = tile_keys(stage, phase, heads)
        else:
            keys = [buf[0, value_rows, c] for c in cols]
        queries = [query[:, c] for c in cols]
        old_peaks = [peak[head] for head in heads]
        scores = [
            lax.dot_general(q, k, (((1,), (1,)), ((), ())), preferred_element_type=F32) * SCORE_SCALE + allowed
            for q, k in zip(queries, keys)
        ]
        peaks = [
            jnp.maximum(old, jnp.broadcast_to(jnp.max(s, axis=1, keepdims=True), (TOK, HD)))
            for old, s in zip(old_peaks, scores)
        ]
        expos = [jnp.exp2(s - p) for s, p in zip(scores, peaks)]
        values = [buf[1, value_rows, c] for c in cols]
        mixed = [jnp.dot(e.astype(BF16), v, preferred_element_type=F32) for e, v in zip(expos, values)]
        factors = [jnp.exp2(old - new) for old, new in zip(old_peaks, peaks)]
        totals = [total[head] * f + e for head, f, e in zip(heads, factors, expos)]
        sums = [accum[:, c] * f + m for c, f, m in zip(cols, factors, mixed)]
        for i, head in enumerate(heads):
            peak[head] = peaks[i]
            total[head] = totals[i]
            accum[:, cols[i]] = sums[i]

    def finish(heads):
        attended = [accum[:, head_cols(head)] / jnp.sum(total[head], axis=1, keepdims=True) for head in heads]
        squares = square[...]
        for head, values in zip(heads, attended):
            accum[:, head_cols(head)] = values
            squares = squares + values * values
        square[...] = squares

    def tiles_left(phase, hop):
        for direction in range(2):
            @pl.when(sends[direction][hop])
            def _():
                scale_copy(phase, direction, hop).wait_send()

                def body(group, _):
                    tile_copy(phase, direction, hop, group).wait_send()
                    return 0

                lax.fori_loop(0, GROUPS, body, 0)

    def earlier_sends_left():
        def ring_left(number, _):
            for direction in range(2):
                ring_copy(direction, number, False).wait_send()
            return 0

        for number in range(4):
            for direction in range(2):
                ring_copy(direction, number, True).wait_send()
        lax.fori_loop(4, RING, ring_left, 0)
        for which in range(2):
            for half in range(2):
                sib_copy(which, half, 1, True).wait_send()
        each_sibling(3, 7, lambda copy: copy.wait_send())
        for hop in range(2):
            tiles_left(0, hop)

    loads = [
        pltpu.make_async_copy(latent_hbm.at[0], buf.at[1, pl.ds(0, TOK)], local_sem.at[0]),
        pltpu.make_async_copy(cache_hbm.at[0], buf.at[0, pl.ds(CHIP, SHARD)], local_sem.at[1]),
        pltpu.make_async_copy(cache_hbm.at[1], buf.at[1, pl.ds(CHIP, SHARD)], local_sem.at[2]),
        pltpu.make_async_copy(mask_hbm, mask_ref, local_sem.at[3]),
        pltpu.make_async_copy(gains_hbm, gains_ref, local_sem.at[4]),
        pltpu.make_async_copy(steps_hbm, steps_ref, local_sem.at[5]),
    ]
    for load in loads:
        load.start()
    barrier = pltpu.get_barrier_semaphore()
    for device in (*along_y, sibling):
        pl.semaphore_signal(barrier, inc=1, device_id=device, device_id_type=MESH)
    for direction in range(2):
        @pl.when(sends[direction][0])
        def _():
            pl.semaphore_signal(barrier, inc=1, device_id=along_z[direction], device_id_type=MESH)

    pl.semaphore_wait(barrier, 3 + lax.min(space, 1) + lax.min(n_space - 1 - space, 1))

    for number in range(2):
        for direction in range(2):
            ring_copy(direction, number, True).start()
    start_tile(0, 0, 0)
    for number in range(2, 4):
        for direction in range(2):
            ring_copy(direction, number, True).start()
    for which in range(2):
        for half in range(2):
            sib_copy(which, half, 1, True).start()

    for hop in range(2):
        for direction in range(2):
            @pl.when(jnp.logical_not(receives[direction][hop]))
            def _():
                for phase in range(STEPS):
                    buf[1, tile_rows(phase, 2 * hop + direction), :] = jnp.zeros((TOK, HW), BF16)
                    scale_in[phase, 2 * hop + direction] = jnp.zeros((8, HD), F32)

    for which in range(2):
        for stage in (0, 2):
            buf[which, pl.ds(stage * STAGE + 3 * STAGE // 4, STAGE // 4), :] = jnp.zeros((STAGE // 4, HW), BF16)

    for load in loads[3:]:
        load.wait()
    lane = lax.broadcasted_iota(jnp.int32, (8, HD), 1)
    for stage in (0, 2):
        bias[stage] = jnp.where(lane < 3 * STAGE // 4, 0.0, MASKED).astype(F32)
    bias[1] = jnp.zeros((8, HD), F32)
    for hop in range(2):
        low, high = (1, 2) if hop == 0 else (0, 3)
        low_ok = (mask_ref[0, 0, low] > 0) & (space - hop > 0)
        high_ok = (mask_ref[0, 0, high] > 0) & (space + hop + 1 < n_space)
        low_bias = jnp.where(low_ok, 0.0, MASKED).astype(F32)
        high_bias = jnp.where(high_ok, 0.0, MASKED).astype(F32)
        bias[NEAR + hop] = jnp.where(lane < TOK, low_bias, high_bias)

    loads[0].wait()
    square[...] = jnp.zeros((TOK, HD), F32)

    def add_squares(group, _):
        squares = square[...]
        for i in range(PER):
            values = buf[1, pl.ds(0, TOK), head_cols(group * PER + i)].astype(F32)
            squares = squares + values * values
        square[...] = squares
        return 0

    lax.fori_loop(0, GROUPS, add_squares, 0)
    col = root_scale()
    send_scale(0, col)
    for group in range(1, GROUPS):
        start_tile(0, 0, group)
    begin_heads(col)
    for load in loads[1:3]:
        load.wait()

    def phase_body(phase, _):
        first = phase == 0
        square[...] = jnp.zeros((TOK, HD), F32)

        def heads_of(part, count):
            return [part * count + i for i in range(count)]

        def rounds(start, count):
            @pl.when(first)
            def _():
                for number in range(count):
                    ring_round(start + number)

        @pl.when(first)
        def _():
            each_sibling(1, 1, lambda copy: copy.wait_recv())

        def stored(stage):
            update(stage, phase, heads_of(0, HEADS))

        stored(0)

        @pl.when(jnp.logical_not(first))
        def _():
            stored(1)
            stored(2)

        def near(part, _):
            for i in range(2):
                group = 2 * part + i
                rounds(2 * group, 2)
                wait_tile(phase, 0, group)

            @pl.when(part == 0)
            def _():
                take_scales(phase, 0)

            @pl.when(part == 1)
            def _():
                rounds(8, 2)

            update(NEAR, phase, heads_of(part, 2 * PER))
            return 0

        lax.fori_loop(0, GROUPS // 2, near, 0)

        @pl.when(first)
        def _():
            each_sibling(3, 4, lambda copy: copy.wait_recv())
            stored(1)

        @pl.when(jnp.logical_not(first))
        def _():
            earlier_sends_left()

        rounds(10, 2)
        wait_tile(phase, 1, 0)
        wait_tile(phase, 1, 1)
        take_scales(phase, 1)
        update(FAR, phase, heads_of(0, 2 * PER))
        rounds(12, 2)
        wait_tile(phase, 1, 2)
        update(FAR, phase, heads_of(2, PER))

        @pl.when(first)
        def _():
            for half in range(2):
                for target in (11, 13, 15):
                    for which in range(2):
                        sib_copy(which, half, target).wait_recv()
                update(2, phase, heads_of(half, HEADS // 2))

        finish(heads_of(0, 3 * PER))
        wait_tile(phase, 1, 3)
        update(FAR, phase, heads_of(3, PER))
        finish(heads_of(3, PER))

        @pl.when(first)
        def _():
            col = root_scale()
            step_size = steps_ref[0]
            square[...] = jnp.zeros((TOK, HD), F32)

            def move(group, _):
                squares = square[...]
                cols = [head_cols(group * PER + i) for i in range(PER)]
                moved = [
                    (buf[1, pl.ds(0, TOK), c].astype(F32) + step_size * (accum[:, c] * col)).astype(BF16)
                    for c in cols
                ]
                for c, values in zip(cols, moved):
                    buf[1, pl.ds(0, TOK), c] = values
                    wide = values.astype(F32)
                    squares = squares + wide * wide
                square[...] = squares

                @pl.when(group == 0)
                def _():
                    start_tile(1, 0, 0)

                return 0

            lax.fori_loop(0, GROUPS, move, 0)
            col = root_scale()
            send_scale(1, col)
            for group in range(1, GROUPS):
                start_tile(1, 0, group)
            begin_heads(col)

        return 0

    lax.fori_loop(0, STEPS, phase_body, 0)

    col = root_scale()
    last_size = steps_ref[STEPS - 1]

    cols = [head_cols(head) for head in range(HEADS)]
    velocities = [accum[:, c] * col for c in cols]
    moved = [buf[1, pl.ds(0, TOK), c].astype(F32) + last_size * v for c, v in zip(cols, velocities)]
    for c, velocity, denoised in zip(cols, velocities, moved):
        denoised_ref[0, :, c] = denoised.astype(BF16)
        velocity_ref[0, :, c] = velocity.astype(BF16)

    for hop in range(2):
        tiles_left(1, hop)


PIECE = 16
PIECES = TOK // PIECE


def hand_over(denoised_in, velocity_in, denoised_out, velocity_out, sems):
    copies = [
        pltpu.make_async_copy(source.at[0, pl.ds(PIECE * i, PIECE)], target.at[0, pl.ds(PIECE * i, PIECE)], sems.at[which, i])
        for i in range(PIECES)
        for which, (source, target) in enumerate(((denoised_in, denoised_out), (velocity_in, velocity_out)))
    ]
    for copy in copies:
        copy.start()
    for copy in copies:
        copy.wait()


def per_device(latent, past_cache, neighbour_mask, gains, step_sizes):
    dma = pltpu.SemaphoreType.DMA
    hbm = pl.BlockSpec(memory_space=pltpu.HBM)
    vmem = pl.BlockSpec(memory_space=pltpu.VMEM)
    operands = [
        pltpu.with_memory_space_constraint(x, pltpu.HBM)
        for x in (latent, past_cache, neighbour_mask, gains, step_sizes)
    ]
    results = pl.pallas_call(
        kernel,
        out_shape=(pltpu.VMEM((1, TOK, HW), BF16),) * 2,
        in_specs=[hbm] * 5,
        out_specs=(vmem,) * 2,
        scratch_shapes=[
            pltpu.SMEM((1, 1, 4), jnp.int32),
            pltpu.VMEM((2, HW), F32),
            pltpu.SMEM((STEPS,), F32),
            pltpu.VMEM((2, ROWS, HW), BF16),
            pltpu.VMEM((TOK, HW), BF16),
            pltpu.VMEM((TOK, HW), F32),
            pltpu.VMEM((HEADS, TOK, HD), F32),
            pltpu.VMEM((HEADS, TOK, HD), F32),
            pltpu.VMEM((STEPS, 8, HD), F32),
            pltpu.VMEM((STEPS, 4, 8, HD), F32),
            pltpu.VMEM((4 * TOK, HD), F32),
            pltpu.VMEM((5, 8, HD), F32),
            pltpu.VMEM((TOK, HD), F32),
            dma((6,)),
            dma((2, RING)),
            dma((2, 16, 2)),
            dma((2, 16, 2)),
            dma((STEPS, 2, 2, GROUPS)),
            dma((STEPS, 4, GROUPS)),
            dma((STEPS, 2, 2)),
            dma((STEPS, 4)),
        ],
        compiler_params=pltpu.CompilerParams(
            collective_id=0, has_side_effects=True, vmem_limit_bytes=32 * 1024 * 1024
        ),
        cost_estimate=pl.CostEstimate(flops=760_000_000, bytes_accessed=1_200_000, transcendentals=1_600_000),
    )(*operands)
    return pl.pallas_call(
        hand_over,
        out_shape=(jax.ShapeDtypeStruct((1, TOK, HW), BF16),) * 2,
        in_specs=[vmem] * 2,
        out_specs=(hbm,) * 2,
        scratch_shapes=[dma((2, PIECES))],
    )(*(pltpu.with_memory_space_constraint(x, pltpu.VMEM) for x in results))


def solution(mesh):
    in_specs = (P("tm", "space", None), P(None, "tm", "space"), P("tm", "space", None), P(), P())
    out_specs = (P("tm", "space", None), P("tm", "space", None))
    return jax.shard_map(
        per_device, mesh=mesh, in_specs=in_specs, out_specs=out_specs, check_vma=False
    )
```

```python
import functools
import math

import jax
import jax.numpy as jnp
from jax import lax
from jax.experimental import pallas as pl
from jax.experimental.pallas import tpu as pltpu
from jax.sharding import PartitionSpec as P

HD = 128
HEADS = 20
HW = HD * HEADS
TOK = 64
STEPS = 2
SHARD = 16
GROUPS = 4
PER = HEADS // GROUPS
GW = PER * HD
EPS = 1e-6
SCORE_SCALE = math.log2(math.e) / math.sqrt(HD)
MASKED = -1e30
MESH = pl.DeviceIdType.MESH
F32 = jnp.float32
BF16 = jnp.bfloat16

STAGE = 128
NEAR, FAR = 3, 4
TILES = 3 * STAGE
ROWS = TILES + STEPS * 2 * STAGE
CHIP = TOK
RING = 14


def kernel(
    latent_hbm, cache_hbm, mask_hbm, gains_hbm, steps_hbm,
    denoised_ref, velocity_ref,
    mask_ref, gains_ref, steps_ref, buf, query, accum, peak, total, scale_own, scale_in, scale_col, bias, square,
    local_sem, ysend, ssend, yrecv, zsend, zrecv, rsend, rrecv,
):
    tm, space = lax.axis_index("tm"), lax.axis_index("space")
    n_tm, n_space = lax.axis_size("tm"), lax.axis_size("space")
    along_y = ((lax.rem(tm + 2, n_tm), space), (lax.rem(tm + n_tm - 2, n_tm), space))
    sibling = (tm + 1 - 2 * lax.rem(tm, 2), space)
    along_z = ((tm, lax.rem(space + 1, n_space)), (tm, lax.rem(space + n_space - 1, n_space)))
    has_low, has_high = space > 0, space < n_space - 1
    sends = ((has_high, has_low & has_high), (has_low, has_low & has_high))
    receives = ((has_low, space > 1), (has_high, space < n_space - 2))

    def remote(src, dst, send, recv, device):
        return pltpu.make_async_remote_copy(
            src_ref=src, dst_ref=dst, send_sem=send, recv_sem=recv, device_id=device, device_id_type=MESH
        )

    def half_cols(half):
        return pl.ds(pl.multiple_of(half * (HW // 2), HW // 2), HW // 2)

    def shard(which, index, half):
        rows = CHIP + SHARD * index + jnp.where(index >= 2, 2 * SHARD, 0)
        return buf.at[which, pl.ds(pl.multiple_of(rows, SHARD), SHARD), half_cols(half)]

    def slot(distance, direction):
        return 4 * distance - 2 + jnp.where(distance == 4, 0, 2 * direction)

    def ring_place(direction, number):
        which = lax.rem(number // 2 + direction, 2)
        return which, lax.rem(number, 2), number // 4 + 1

    def ring_copy(direction, number, own):
        which, half, distance = ring_place(direction, number)
        target = slot(distance, direction)
        if own:
            src = cache_hbm.at[which, :, half_cols(half)]
        else:
            src = shard(which, slot(distance - 1, direction), half)
        return remote(
            src, shard(which, target, half), ysend.at[direction, number], yrecv.at[which, target, half],
            along_y[direction],
        )

    def sib_copy(which, half, target, own=False):
        src = cache_hbm.at[which, :, half_cols(half)] if own else shard(which, target - 1, half)
        return remote(
            src, shard(which, target, half), ssend.at[which, target, half], yrecv.at[which, target, half], sibling
        )

    def ring_round(number):
        for direction in range(2):
            which, half, distance = ring_place(direction, number)
            ring_copy(direction, number, False).wait_recv()

            @pl.when(number + 4 < RING)
            def _():
                ring_copy(direction, number + 4, False).start()

            sib_copy(which, half, slot(distance, direction) + 1).start()

    def each_sibling(first, count, act):
        def body(i, _):
            act(sib_copy(lax.rem(i, 2), lax.rem(i // 2, 2), first + 2 * (i // 4)))
            return 0

        lax.fori_loop(0, 4 * count, body, 0)

    def columns(group):
        return pl.ds(pl.multiple_of(group * GW, GW), GW)

    def head_cols(head):
        if isinstance(head, int):
            return pl.ds(head * HD, HD)
        return pl.ds(pl.multiple_of(head * HD, HD), HD)

    def tile_rows(phase, number):
        return pl.ds(pl.multiple_of(TILES + phase * 2 * STAGE + number * TOK, TOK), TOK)

    def tile_part(phase, number, cols):
        return buf.at[1, tile_rows(phase, number), cols]

    def tile_copy(phase, direction, hop, group):
        cols = columns(group)
        if hop == 1:
            src = tile_part(phase, direction, cols)
        elif isinstance(phase, int) and phase == 0:
            src = latent_hbm.at[0, :, cols]
        else:
            src = buf.at[1, pl.ds(0, TOK), cols]
        target = 2 * hop + direction
        return remote(
            src, tile_part(phase, target, cols), zsend.at[phase, direction, hop, group],
            zrecv.at[phase, target, group], along_z[direction],
        )

    def scale_copy(phase, direction, hop):
        src = scale_own.at[phase] if hop == 0 else scale_in.at[phase, direction]
        target = 2 * hop + direction
        return remote(
            src, scale_in.at[phase, target], rsend.at[phase, direction, hop], rrecv.at[phase, target], along_z[direction]
        )

    def start_tile(phase, hop, group):
        for direction in range(2):
            @pl.when(sends[direction][hop])
            def _():
                tile_copy(phase, direction, hop, group).start()

    def wait_tile(phase, hop, group):
        for direction in range(2):
            @pl.when(receives[direction][hop])
            def _():
                tile_copy(phase, direction, hop, group).wait_recv()

        if hop == 0:
            start_tile(phase, 1, group)

    diagonal = lax.broadcasted_iota(jnp.int32, (TOK, HD), 0) == lax.broadcasted_iota(jnp.int32, (TOK, HD), 1)

    def take_scales(phase, hop):
        for direction in range(2):
            target = 2 * hop + direction

            @pl.when(receives[direction][hop])
            def _():
                scale_copy(phase, direction, hop).wait_recv()

            if hop == 0:
                @pl.when(sends[direction][1])
                def _():
                    scale_copy(phase, direction, 1).start()

            row = jnp.broadcast_to(scale_in[phase, target, 0:1, :], (TOK, HD))
            col = jnp.sum(jnp.where(diagonal, row, 0.0), axis=1, keepdims=True)
            scale_col[pl.ds(target * TOK, TOK), :] = jnp.broadcast_to(col, (TOK, HD))

    def root_scale():
        mean = jnp.sum(square[...], axis=1, keepdims=True) * (1.0 / HW)
        return jnp.broadcast_to(lax.rsqrt(mean + EPS), (TOK, HD))

    def send_scale(phase, col):
        row = jnp.sum(jnp.where(diagonal, col, 0.0), axis=0, keepdims=True)
        scale_own[phase] = jnp.broadcast_to(row, (8, HD))
        for direction in range(2):
            @pl.when(sends[direction][0])
            def _():
                scale_copy(phase, direction, 0).start()

    def begin_heads(col):
        def body(group, _):
            heads = [group * PER + i for i in range(PER)]
            normals = [buf[1, pl.ds(0, TOK), head_cols(head)].astype(F32) * col for head in heads]
            for head, normal in zip(heads, normals):
                cols = head_cols(head)
                query[:, cols] = (normal * gains_ref[0:1, cols]).astype(BF16)
                buf[0, pl.ds(0, TOK), cols] = (normal * gains_ref[1:2, cols]).astype(BF16)
                peak[head] = jnp.full((TOK, HD), MASKED, F32)
                total[head] = jnp.zeros((TOK, HD), F32)
                accum[:, cols] = jnp.zeros((TOK, HD), F32)
            return 0

        lax.fori_loop(0, GROUPS, body, 0)

    def keys_values(head, stage, phase):
        cols = head_cols(head)
        if stage < NEAR:
            rows = pl.ds(stage * STAGE, STAGE)
            return buf[0, rows, cols], buf[1, rows, cols]
        values = buf[1, pl.ds(pl.multiple_of((stage + phase * 2) * STAGE, STAGE), STAGE), cols]
        scales = scale_col[pl.ds((stage - NEAR) * STAGE, STAGE), :]
        return (values.astype(F32) * scales * gains_ref[1:2, cols]).astype(BF16), values

    def update(phase, *parts):
        plan = [(head, stages) for heads, stages in parts for head in heads]
        cols = [head_cols(head) for head, _ in plan]
        tiles = [[keys_values(head, stage, phase) for stage in stages] for head, stages in plan]
        queries = [query[:, c] for c in cols]
        old_peaks = [peak[head] for head, _ in plan]
        scores = [
            [
                lax.dot_general(q, k, (((1,), (1,)), ((), ())), preferred_element_type=F32) * SCORE_SCALE
                + bias[stage, 0:1, :]
                for stage, (k, _) in zip(stages, pairs)
            ]
            for q, pairs, (_, stages) in zip(queries, tiles, plan)
        ]
        tops = [functools.reduce(jnp.maximum, each) for each in scores]
        peaks = [
            jnp.maximum(old, jnp.broadcast_to(jnp.max(top, axis=1, keepdims=True), (TOK, HD)))
            for old, top in zip(old_peaks, tops)
        ]
        expos = [[jnp.exp2(s - p) for s in each] for each, p in zip(scores, peaks)]
        mixed = [
            sum(jnp.dot(e.astype(BF16), v, preferred_element_type=F32) for e, (_, v) in zip(each, pairs))
            for each, pairs in zip(expos, tiles)
        ]
        factors = [jnp.exp2(old - new) for old, new in zip(old_peaks, peaks)]
        totals = [total[head] * f + sum(each) for (head, _), f, each in zip(plan, factors, expos)]
        sums = [accum[:, c] * f + m for c, f, m in zip(cols, factors, mixed)]
        for i, (head, _) in enumerate(plan):
            peak[head] = peaks[i]
            total[head] = totals[i]
            accum[:, cols[i]] = sums[i]

    def finish(heads):
        attended = [accum[:, head_cols(head)] / jnp.sum(total[head], axis=1, keepdims=True) for head in heads]
        squares = square[...]
        for head, values in zip(heads, attended):
            accum[:, head_cols(head)] = values
            squares = squares + values * values
        square[...] = squares

    def tiles_left(phase, hop):
        for direction in range(2):
            @pl.when(sends[direction][hop])
            def _():
                scale_copy(phase, direction, hop).wait_send()

                def body(group, _):
                    tile_copy(phase, direction, hop, group).wait_send()
                    return 0

                lax.fori_loop(0, GROUPS, body, 0)

    def earlier_sends_left():
        def ring_left(number, _):
            for direction in range(2):
                ring_copy(direction, number, False).wait_send()
            return 0

        for number in range(4):
            for direction in range(2):
                ring_copy(direction, number, True).wait_send()
        lax.fori_loop(4, RING, ring_left, 0)
        for which in range(2):
            for half in range(2):
                sib_copy(which, half, 1, True).wait_send()
        each_sibling(3, 7, lambda copy: copy.wait_send())
        for hop in range(2):
            tiles_left(0, hop)

    loads = [
        pltpu.make_async_copy(latent_hbm.at[0], buf.at[1, pl.ds(0, TOK)], local_sem.at[0]),
        pltpu.make_async_copy(cache_hbm.at[0], buf.at[0, pl.ds(CHIP, SHARD)], local_sem.at[1]),
        pltpu.make_async_copy(cache_hbm.at[1], buf.at[1, pl.ds(CHIP, SHARD)], local_sem.at[2]),
        pltpu.make_async_copy(mask_hbm, mask_ref, local_sem.at[3]),
        pltpu.make_async_copy(gains_hbm, gains_ref, local_sem.at[4]),
        pltpu.make_async_copy(steps_hbm, steps_ref, local_sem.at[5]),
    ]
    for load in loads:
        load.start()
    barrier = pltpu.get_barrier_semaphore()
    for device in (*along_y, sibling):
        pl.semaphore_signal(barrier, inc=1, device_id=device, device_id_type=MESH)
    for direction in range(2):
        @pl.when(sends[direction][0])
        def _():
            pl.semaphore_signal(barrier, inc=1, device_id=along_z[direction], device_id_type=MESH)

    pl.semaphore_wait(barrier, 3 + lax.min(space, 1) + lax.min(n_space - 1 - space, 1))

    for number in range(2):
        for direction in range(2):
            ring_copy(direction, number, True).start()
    start_tile(0, 0, 0)
    for number in range(2, 4):
        for direction in range(2):
            ring_copy(direction, number, True).start()
    for which in range(2):
        for half in range(2):
            sib_copy(which, half, 1, True).start()

    for hop in range(2):
        for direction in range(2):
            @pl.when(jnp.logical_not(receives[direction][hop]))
            def _():
                for phase in range(STEPS):
                    buf[1, tile_rows(phase, 2 * hop + direction), :] = jnp.zeros((TOK, HW), BF16)
                    scale_in[phase, 2 * hop + direction] = jnp.zeros((8, HD), F32)

    for which in range(2):
        for stage in (0, 2):
            buf[which, pl.ds(stage * STAGE + 3 * STAGE // 4, STAGE // 4), :] = jnp.zeros((STAGE // 4, HW), BF16)

    for load in loads[3:]:
        load.wait()
    lane = lax.broadcasted_iota(jnp.int32, (8, HD), 1)
    for stage in (0, 2):
        bias[stage] = jnp.where(lane < 3 * STAGE // 4, 0.0, MASKED).astype(F32)
    bias[1] = jnp.zeros((8, HD), F32)
    for hop in range(2):
        low, high = (1, 2) if hop == 0 else (0, 3)
        low_ok = (mask_ref[0, 0, low] > 0) & (space - hop > 0)
        high_ok = (mask_ref[0, 0, high] > 0) & (space + hop + 1 < n_space)
        low_bias = jnp.where(low_ok, 0.0, MASKED).astype(F32)
        high_bias = jnp.where(high_ok, 0.0, MASKED).astype(F32)
        bias[NEAR + hop] = jnp.where(lane < TOK, low_bias, high_bias)

    loads[0].wait()
    square[...] = jnp.zeros((TOK, HD), F32)

    def add_squares(group, _):
        squares = square[...]
        for i in range(PER):
            values = buf[1, pl.ds(0, TOK), head_cols(group * PER + i)].astype(F32)
            squares = squares + values * values
        square[...] = squares
        return 0

    lax.fori_loop(0, GROUPS, add_squares, 0)
    col = root_scale()
    send_scale(0, col)
    for group in range(1, GROUPS):
        start_tile(0, 0, group)
    begin_heads(col)
    for load in loads[1:3]:
        load.wait()

    def phase_body(phase, _):
        first = phase == 0
        square[...] = jnp.zeros((TOK, HD), F32)

        def rounds(start, count):
            @pl.when(first)
            def _():
                for number in range(start, start + count):
                    ring_round(number)

        def last_shards(half):
            for target in (11, 13, 15):
                for which in range(2):
                    sib_copy(which, half, target).wait_recv()

        every = range(HEADS)

        @pl.when(first)
        def _():
            each_sibling(1, 1, lambda copy: copy.wait_recv())

        update(phase, (every, (0,)))

        @pl.when(jnp.logical_not(first))
        def _():
            update(phase, (every, (1,)))
            update(phase, (every, (2,)))

        for group in range(GROUPS):
            rounds(2 * group, 2)
            wait_tile(phase, 0, group)
        rounds(8, 2)
        take_scales(phase, 0)
        update(phase, (every, (NEAR,)))

        @pl.when(first)
        def _():
            each_sibling(3, 4, lambda copy: copy.wait_recv())
            update(phase, (every, (1,)))

        @pl.when(jnp.logical_not(first))
        def _():
            earlier_sends_left()

        rounds(10, 2)
        wait_tile(phase, 1, 0)
        wait_tile(phase, 1, 1)
        take_scales(phase, 1)
        update(phase, (every[:2 * PER], (FAR,)))
        rounds(12, 2)
        wait_tile(phase, 1, 2)
        update(phase, (every[2 * PER : 3 * PER], (FAR,)))

        @pl.when(first)
        def _():
            last_shards(0)
            update(phase, (every[: 2 * PER], (2,)))
            finish(every[: 2 * PER])
            last_shards(1)
            wait_tile(phase, 1, 3)
            update(phase, (every[2 * PER : 3 * PER], (2,)), (every[3 * PER :], (2, FAR)))
            finish(every[2 * PER :])

        @pl.when(jnp.logical_not(first))
        def _():
            finish(every[: 3 * PER])
            wait_tile(phase, 1, 3)
            update(phase, (every[3 * PER :], (FAR,)))
            finish(every[3 * PER :])

        @pl.when(first)
        def _():
            col = root_scale()
            step_size = steps_ref[0]
            square[...] = jnp.zeros((TOK, HD), F32)

            def move(group, _):
                squares = square[...]
                cols = [head_cols(group * PER + i) for i in range(PER)]
                moved = [
                    (buf[1, pl.ds(0, TOK), c].astype(F32) + step_size * (accum[:, c] * col)).astype(BF16)
                    for c in cols
                ]
                for c, values in zip(cols, moved):
                    buf[1, pl.ds(0, TOK), c] = values
                    wide = values.astype(F32)
                    squares = squares + wide * wide
                square[...] = squares

                @pl.when(group == 0)
                def _():
                    start_tile(1, 0, 0)

                return 0

            lax.fori_loop(0, GROUPS, move, 0)
            col = root_scale()
            send_scale(1, col)
            for group in range(1, GROUPS):
                start_tile(1, 0, group)
            begin_heads(col)

        return 0

    lax.fori_loop(0, STEPS, phase_body, 0)

    col = root_scale()
    last_size = steps_ref[STEPS - 1]

    cols = [head_cols(head) for head in range(HEADS)]
    velocities = [accum[:, c] * col for c in cols]
    moved = [buf[1, pl.ds(0, TOK), c].astype(F32) + last_size * v for c, v in zip(cols, velocities)]
    for c, velocity, denoised in zip(cols, velocities, moved):
        denoised_ref[0, :, c] = denoised.astype(BF16)
        velocity_ref[0, :, c] = velocity.astype(BF16)

    for hop in range(2):
        tiles_left(1, hop)


PIECE = 16
PIECES = TOK // PIECE


def hand_over(denoised_in, velocity_in, denoised_out, velocity_out, sems):
    copies = [
        pltpu.make_async_copy(source.at[0, pl.ds(PIECE * i, PIECE)], target.at[0, pl.ds(PIECE * i, PIECE)], sems.at[which, i])
        for i in range(PIECES)
        for which, (source, target) in enumerate(((denoised_in, denoised_out), (velocity_in, velocity_out)))
    ]
    for copy in copies:
        copy.start()
    for copy in copies:
        copy.wait()


def per_device(latent, past_cache, neighbour_mask, gains, step_sizes):
    dma = pltpu.SemaphoreType.DMA
    hbm = pl.BlockSpec(memory_space=pltpu.HBM)
    vmem = pl.BlockSpec(memory_space=pltpu.VMEM)
    operands = [
        pltpu.with_memory_space_constraint(x, pltpu.HBM)
        for x in (latent, past_cache, neighbour_mask, gains, step_sizes)
    ]
    results = pl.pallas_call(
        kernel,
        out_shape=(pltpu.VMEM((1, TOK, HW), BF16),) * 2,
        in_specs=[hbm] * 5,
        out_specs=(vmem,) * 2,
        scratch_shapes=[
            pltpu.SMEM((1, 1, 4), jnp.int32),
            pltpu.VMEM((2, HW), F32),
            pltpu.SMEM((STEPS,), F32),
            pltpu.VMEM((2, ROWS, HW), BF16),
            pltpu.VMEM((TOK, HW), BF16),
            pltpu.VMEM((TOK, HW), F32),
            pltpu.VMEM((HEADS, TOK, HD), F32),
            pltpu.VMEM((HEADS, TOK, HD), F32),
            pltpu.VMEM((STEPS, 8, HD), F32),
            pltpu.VMEM((STEPS, 4, 8, HD), F32),
            pltpu.VMEM((4 * TOK, HD), F32),
            pltpu.VMEM((5, 8, HD), F32),
            pltpu.VMEM((TOK, HD), F32),
            dma((6,)),
            dma((2, RING)),
            dma((2, 16, 2)),
            dma((2, 16, 2)),
            dma((STEPS, 2, 2, GROUPS)),
            dma((STEPS, 4, GROUPS)),
            dma((STEPS, 2, 2)),
            dma((STEPS, 4)),
        ],
        compiler_params=pltpu.CompilerParams(
            collective_id=0, has_side_effects=True, vmem_limit_bytes=32 * 1024 * 1024
        ),
        cost_estimate=pl.CostEstimate(flops=760_000_000, bytes_accessed=1_200_000, transcendentals=1_600_000),
    )(*operands)
    return pl.pallas_call(
        hand_over,
        out_shape=(jax.ShapeDtypeStruct((1, TOK, HW), BF16),) * 2,
        in_specs=[vmem] * 2,
        out_specs=(hbm,) * 2,
        scratch_shapes=[dma((2, PIECES))],
    )(*(pltpu.with_memory_space_constraint(x, pltpu.VMEM) for x in results))


def solution(mesh):
    in_specs = (P("tm", "space", None), P(None, "tm", "space"), P("tm", "space", None), P(), P())
    out_specs = (P("tm", "space", None), P("tm", "space", None))
    return jax.shard_map(
        per_device, mesh=mesh, in_specs=in_specs, out_specs=out_specs, check_vma=False
    )
```

```python
import functools
import math

import jax
import jax.numpy as jnp
from jax import lax
from jax.experimental import pallas as pl
from jax.experimental.pallas import tpu as pltpu
from jax.sharding import PartitionSpec as P

HD = 128
HEADS = 20
HW = HD * HEADS
TOK = 64
STEPS = 2
SHARD = 16
GROUPS = 4
PER = HEADS // GROUPS
GW = PER * HD
EPS = 1e-6
SCORE_SCALE = math.log2(math.e) / math.sqrt(HD)
MASKED = -1e30
MESH = pl.DeviceIdType.MESH
F32 = jnp.float32
BF16 = jnp.bfloat16

STAGE = 128
NEAR, FAR = 3, 4
TILES = 3 * STAGE
ROWS = TILES + STEPS * 2 * STAGE
CHIP = TOK
RING = 14


def kernel(
    latent_hbm, cache_hbm, mask_hbm, gains_hbm, steps_hbm,
    denoised_ref, velocity_ref,
    mask_ref, gains_ref, steps_ref, buf, query, accum, peak, total, scale_own, scale_in, scale_col, bias, square,
    local_sem, ysend, ssend, yrecv, zsend, zrecv, rsend, rrecv,
):
    tm, space = lax.axis_index("tm"), lax.axis_index("space")
    n_tm, n_space = lax.axis_size("tm"), lax.axis_size("space")
    along_y = ((lax.rem(tm + 2, n_tm), space), (lax.rem(tm + n_tm - 2, n_tm), space))
    sibling = (tm + 1 - 2 * lax.rem(tm, 2), space)
    along_z = ((tm, lax.rem(space + 1, n_space)), (tm, lax.rem(space + n_space - 1, n_space)))
    has_low, has_high = space > 0, space < n_space - 1
    sends = ((has_high, has_low & has_high), (has_low, has_low & has_high))
    receives = ((has_low, space > 1), (has_high, space < n_space - 2))

    def remote(src, dst, send, recv, device):
        return pltpu.make_async_remote_copy(
            src_ref=src, dst_ref=dst, send_sem=send, recv_sem=recv, device_id=device, device_id_type=MESH
        )

    def half_cols(half):
        return pl.ds(pl.multiple_of(half * (HW // 2), HW // 2), HW // 2)

    def shard(which, index, half):
        rows = CHIP + SHARD * index + jnp.where(index >= 2, 2 * SHARD, 0)
        return buf.at[which, pl.ds(pl.multiple_of(rows, SHARD), SHARD), half_cols(half)]

    def slot(distance, direction):
        return 4 * distance - 2 + jnp.where(distance == 4, 0, 2 * direction)

    def ring_place(direction, number):
        which = lax.rem(number // 2 + direction, 2)
        return which, lax.rem(number, 2), number // 4 + 1

    def ring_copy(direction, number, own):
        which, half, distance = ring_place(direction, number)
        target = slot(distance, direction)
        if own:
            src = cache_hbm.at[which, :, half_cols(half)]
        else:
            src = shard(which, slot(distance - 1, direction), half)
        return remote(
            src, shard(which, target, half), ysend.at[direction, number], yrecv.at[which, target, half],
            along_y[direction],
        )

    def sib_copy(which, half, target, own=False):
        src = cache_hbm.at[which, :, half_cols(half)] if own else shard(which, target - 1, half)
        return remote(
            src, shard(which, target, half), ssend.at[which, target, half], yrecv.at[which, target, half], sibling
        )

    def ring_round(number):
        for direction in range(2):
            which, half, distance = ring_place(direction, number)
            ring_copy(direction, number, False).wait_recv()

            @pl.when(number + 4 < RING)
            def _():
                ring_copy(direction, number + 4, False).start()

            sib_copy(which, half, slot(distance, direction) + 1).start()

    def each_sibling(first, count, act):
        def body(i, _):
            act(sib_copy(lax.rem(i, 2), lax.rem(i // 2, 2), first + 2 * (i // 4)))
            return 0

        lax.fori_loop(0, 4 * count, body, 0)

    def columns(group):
        return pl.ds(pl.multiple_of(group * GW, GW), GW)

    def head_cols(head):
        if isinstance(head, int):
            return pl.ds(head * HD, HD)
        return pl.ds(pl.multiple_of(head * HD, HD), HD)

    def tile_rows(phase, number):
        return pl.ds(pl.multiple_of(TILES + phase * 2 * STAGE + number * TOK, TOK), TOK)

    def tile_part(phase, number, cols):
        return buf.at[1, tile_rows(phase, number), cols]

    def tile_copy(phase, direction, hop, group):
        cols = columns(group)
        if hop == 1:
            src = tile_part(phase, direction, cols)
        elif isinstance(phase, int) and phase == 0:
            src = latent_hbm.at[0, :, cols]
        else:
            src = buf.at[1, pl.ds(0, TOK), cols]
        target = 2 * hop + direction
        return remote(
            src, tile_part(phase, target, cols), zsend.at[phase, direction, hop, group],
            zrecv.at[phase, target, group], along_z[direction],
        )

    def scale_copy(phase, direction, hop):
        src = scale_own.at[phase] if hop == 0 else scale_in.at[phase, direction]
        target = 2 * hop + direction
        return remote(
            src, scale_in.at[phase, target], rsend.at[phase, direction, hop], rrecv.at[phase, target], along_z[direction]
        )

    def start_tile(phase, hop, group):
        for direction in range(2):
            @pl.when(sends[direction][hop])
            def _():
                tile_copy(phase, direction, hop, group).start()

    def wait_tile(phase, hop, group):
        for direction in range(2):
            @pl.when(receives[direction][hop])
            def _():
                tile_copy(phase, direction, hop, group).wait_recv()

        if hop == 0:
            start_tile(phase, 1, group)

    diagonal = lax.broadcasted_iota(jnp.int32, (TOK, HD), 0) == lax.broadcasted_iota(jnp.int32, (TOK, HD), 1)

    def take_scales(phase, hop):
        for direction in range(2):
            target = 2 * hop + direction

            @pl.when(receives[direction][hop])
            def _():
                scale_copy(phase, direction, hop).wait_recv()

            if hop == 0:
                @pl.when(sends[direction][1])
                def _():
                    scale_copy(phase, direction, 1).start()

            row = jnp.broadcast_to(scale_in[phase, target, 0:1, :], (TOK, HD))
            col = jnp.sum(jnp.where(diagonal, row, 0.0), axis=1, keepdims=True)
            scale_col[pl.ds(target * TOK, TOK), :] = jnp.broadcast_to(col, (TOK, HD))

    def root_scale():
        mean = jnp.sum(square[...], axis=1, keepdims=True) * (1.0 / HW)
        return jnp.broadcast_to(lax.rsqrt(mean + EPS), (TOK, HD))

    def send_scale(phase, col):
        row = jnp.sum(jnp.where(diagonal, col, 0.0), axis=0, keepdims=True)
        scale_own[phase] = jnp.broadcast_to(row, (8, HD))
        for direction in range(2):
            @pl.when(sends[direction][0])
            def _():
                scale_copy(phase, direction, 0).start()

    def begin_heads(col):
        def body(group, _):
            heads = [group * PER + i for i in range(PER)]
            normals = [buf[1, pl.ds(0, TOK), head_cols(head)].astype(F32) * col for head in heads]
            for head, normal in zip(heads, normals):
                cols = head_cols(head)
                query[:, cols] = (normal * gains_ref[0:1, cols]).astype(BF16)
                buf[0, pl.ds(0, TOK), cols] = (normal * gains_ref[1:2, cols]).astype(BF16)
                peak[head] = jnp.full((TOK, HD), MASKED, F32)
                total[head] = jnp.zeros((TOK, HD), F32)
                accum[:, cols] = jnp.zeros((TOK, HD), F32)
            return 0

        lax.fori_loop(0, GROUPS, body, 0)

    def value_rows(stage, count, phase):
        start = (stage + phase * 2) * STAGE if stage >= NEAR else stage * STAGE
        return pl.ds(pl.multiple_of(start, STAGE), count * STAGE)

    def keys_of(head, stage, count, phase):
        cols = head_cols(head)
        rows = value_rows(stage, count, phase)
        if stage < NEAR:
            return buf[0, rows, cols]
        scales = scale_col[pl.ds((stage - NEAR) * STAGE, STAGE), :]
        return (buf[1, rows, cols].astype(F32) * scales * gains_ref[1:2, cols]).astype(BF16)

    def mix(plan, weights, phase):
        mixed = []
        at = 0
        while at < len(plan):
            head, spans = plan[at]
            pair = 2 if at + 1 < len(plan) and plan[at + 1] == (head + 1, spans) else 1
            cols = pl.ds(head * HD, pair * HD)
            sums = None
            for i, (stage, count) in enumerate(spans):
                stacked = jnp.concatenate([weights[at + j][i] for j in range(pair)], axis=0)
                product = jnp.dot(stacked, buf[1, value_rows(stage, count, phase), cols], preferred_element_type=F32)
                sums = product if sums is None else sums + product
            mixed += [sums[j * TOK : (j + 1) * TOK, j * HD : (j + 1) * HD] for j in range(pair)]
            at += pair
        return mixed

    def update(phase, *parts):
        plan = [(head, spans) for heads, spans in parts for head in heads]
        cols = [head_cols(head) for head, _ in plan]
        keys = [[keys_of(head, stage, count, phase) for stage, count in spans] for head, spans in plan]
        queries = [query[:, c] for c in cols]
        old_peaks = [peak[head] for head, _ in plan]
        scores = []
        for q, each, (_, spans) in zip(queries, keys, plan):
            pieces = []
            for k, (stage, count) in zip(each, spans):
                raw = lax.dot_general(q, k, (((1,), (1,)), ((), ())), preferred_element_type=F32)
                pieces.append([
                    raw[:, i * STAGE : (i + 1) * STAGE] * SCORE_SCALE + bias[stage + i, 0:1, :] for i in range(count)
                ])
            scores.append(pieces)
        tops = [functools.reduce(jnp.maximum, sum(pieces, [])) for pieces in scores]
        peaks = [
            jnp.maximum(old, jnp.broadcast_to(jnp.max(top, axis=1, keepdims=True), (TOK, HD)))
            for old, top in zip(old_peaks, tops)
        ]
        expos = [[[jnp.exp2(s - p) for s in span] for span in pieces] for pieces, p in zip(scores, peaks)]
        weights = [[jnp.concatenate([e.astype(BF16) for e in span], axis=1) for span in each] for each in expos]
        mixed = mix(plan, weights, phase)
        factors = [jnp.exp2(old - new) for old, new in zip(old_peaks, peaks)]
        totals = [
            total[head] * f + functools.reduce(jnp.add, sum(each, []))
            for (head, _), f, each in zip(plan, factors, expos)
        ]
        sums = [accum[:, c] * f + m for c, f, m in zip(cols, factors, mixed)]
        for i, (head, _) in enumerate(plan):
            peak[head] = peaks[i]
            total[head] = totals[i]
            accum[:, cols[i]] = sums[i]

    def finish(heads):
        attended = [accum[:, head_cols(head)] / jnp.sum(total[head], axis=1, keepdims=True) for head in heads]
        squares = square[...]
        for head, values in zip(heads, attended):
            accum[:, head_cols(head)] = values
            squares = squares + values * values
        square[...] = squares

    def tiles_left(phase, hop):
        for direction in range(2):
            @pl.when(sends[direction][hop])
            def _():
                scale_copy(phase, direction, hop).wait_send()

                def body(group, _):
                    tile_copy(phase, direction, hop, group).wait_send()
                    return 0

                lax.fori_loop(0, GROUPS, body, 0)

    def earlier_sends_left():
        def ring_left(number, _):
            for direction in range(2):
                ring_copy(direction, number, False).wait_send()
            return 0

        for number in range(4):
            for direction in range(2):
                ring_copy(direction, number, True).wait_send()
        lax.fori_loop(4, RING, ring_left, 0)
        for which in range(2):
            for half in range(2):
                sib_copy(which, half, 1, True).wait_send()
        each_sibling(3, 7, lambda copy: copy.wait_send())
        for hop in range(2):
            tiles_left(0, hop)

    loads = [
        pltpu.make_async_copy(latent_hbm.at[0], buf.at[1, pl.ds(0, TOK)], local_sem.at[0]),
        pltpu.make_async_copy(cache_hbm.at[0], buf.at[0, pl.ds(CHIP, SHARD)], local_sem.at[1]),
        pltpu.make_async_copy(cache_hbm.at[1], buf.at[1, pl.ds(CHIP, SHARD)], local_sem.at[2]),
        pltpu.make_async_copy(mask_hbm, mask_ref, local_sem.at[3]),
        pltpu.make_async_copy(gains_hbm, gains_ref, local_sem.at[4]),
        pltpu.make_async_copy(steps_hbm, steps_ref, local_sem.at[5]),
    ]
    for load in loads:
        load.start()
    barrier = pltpu.get_barrier_semaphore()
    for device in (*along_y, sibling):
        pl.semaphore_signal(barrier, inc=1, device_id=device, device_id_type=MESH)
    for direction in range(2):
        @pl.when(sends[direction][0])
        def _():
            pl.semaphore_signal(barrier, inc=1, device_id=along_z[direction], device_id_type=MESH)

    pl.semaphore_wait(barrier, 3 + lax.min(space, 1) + lax.min(n_space - 1 - space, 1))

    for number in range(2):
        for direction in range(2):
            ring_copy(direction, number, True).start()
    start_tile(0, 0, 0)
    for number in range(2, 4):
        for direction in range(2):
            ring_copy(direction, number, True).start()
    for which in range(2):
        for half in range(2):
            sib_copy(which, half, 1, True).start()

    for hop in range(2):
        for direction in range(2):
            @pl.when(jnp.logical_not(receives[direction][hop]))
            def _():
                for phase in range(STEPS):
                    buf[1, tile_rows(phase, 2 * hop + direction), :] = jnp.zeros((TOK, HW), BF16)
                    scale_in[phase, 2 * hop + direction] = jnp.zeros((8, HD), F32)

    for which in range(2):
        for stage in (0, 2):
            buf[which, pl.ds(stage * STAGE + 3 * STAGE // 4, STAGE // 4), :] = jnp.zeros((STAGE // 4, HW), BF16)

    for load in loads[3:]:
        load.wait()
    lane = lax.broadcasted_iota(jnp.int32, (8, HD), 1)
    for stage in (0, 2):
        bias[stage] = jnp.where(lane < 3 * STAGE // 4, 0.0, MASKED).astype(F32)
    bias[1] = jnp.zeros((8, HD), F32)
    for hop in range(2):
        low, high = (1, 2) if hop == 0 else (0, 3)
        low_ok = (mask_ref[0, 0, low] > 0) & (space - hop > 0)
        high_ok = (mask_ref[0, 0, high] > 0) & (space + hop + 1 < n_space)
        low_bias = jnp.where(low_ok, 0.0, MASKED).astype(F32)
        high_bias = jnp.where(high_ok, 0.0, MASKED).astype(F32)
        bias[NEAR + hop] = jnp.where(lane < TOK, low_bias, high_bias)

    loads[0].wait()
    square[...] = jnp.zeros((TOK, HD), F32)

    def add_squares(group, _):
        squares = square[...]
        for i in range(PER):
            values = buf[1, pl.ds(0, TOK), head_cols(group * PER + i)].astype(F32)
            squares = squares + values * values
        square[...] = squares
        return 0

    lax.fori_loop(0, GROUPS, add_squares, 0)
    col = root_scale()
    send_scale(0, col)
    for group in range(1, GROUPS):
        start_tile(0, 0, group)
    begin_heads(col)
    for load in loads[1:3]:
        load.wait()

    def phase_body(phase, _):
        first = phase == 0
        square[...] = jnp.zeros((TOK, HD), F32)

        def rounds(start, count):
            @pl.when(first)
            def _():
                for number in range(start, start + count):
                    ring_round(number)

        def last_shards(half):
            for target in (11, 13, 15):
                for which in range(2):
                    sib_copy(which, half, target).wait_recv()

        every = range(HEADS)

        @pl.when(first)
        def _():
            each_sibling(1, 1, lambda copy: copy.wait_recv())

        @pl.when(first)
        def _():
            update(phase, (every, ((0, 1),)))

        @pl.when(jnp.logical_not(first))
        def _():
            update(phase, (every[: 2 * PER], ((0, 3),)))
            update(phase, (every[2 * PER :], ((0, 3),)))

        near, far = ((NEAR, 1),), ((FAR, 1),)
        for group in range(2):
            rounds(2 * group, 2)
            wait_tile(phase, 0, group)
        take_scales(phase, 0)
        update(phase, (every[: 2 * PER], near))
        rounds(4, 2)
        wait_tile(phase, 0, 2)
        update(phase, (every[2 * PER : 3 * PER], near))
        rounds(6, 2)
        wait_tile(phase, 0, 3)
        rounds(8, 2)
        update(phase, (every[3 * PER :], near))

        @pl.when(first)
        def _():
            each_sibling(3, 4, lambda copy: copy.wait_recv())
            update(phase, (every, ((1, 1),)))

        @pl.when(jnp.logical_not(first))
        def _():
            earlier_sends_left()

        rounds(10, 2)
        wait_tile(phase, 1, 0)
        wait_tile(phase, 1, 1)
        take_scales(phase, 1)
        update(phase, (every[: 2 * PER], far))
        rounds(12, 2)
        wait_tile(phase, 1, 2)
        update(phase, (every[2 * PER : 3 * PER], far))

        @pl.when(first)
        def _():
            last_shards(0)
            update(phase, (every[: 2 * PER], ((2, 1),)))
            finish(every[: 2 * PER])
            last_shards(1)
            wait_tile(phase, 1, 3)
            update(phase, (every[2 * PER : 3 * PER], ((2, 1),)), (every[3 * PER :], ((2, 1), (FAR, 1))))
            finish(every[2 * PER :])

        @pl.when(jnp.logical_not(first))
        def _():
            finish(every[: 3 * PER])
            wait_tile(phase, 1, 3)
            update(phase, (every[3 * PER :], far))
            finish(every[3 * PER :])

        @pl.when(first)
        def _():
            col = root_scale()
            step_size = steps_ref[0]
            square[...] = jnp.zeros((TOK, HD), F32)

            def move(group, _):
                squares = square[...]
                cols = [head_cols(group * PER + i) for i in range(PER)]
                moved = [
                    (buf[1, pl.ds(0, TOK), c].astype(F32) + step_size * (accum[:, c] * col)).astype(BF16)
                    for c in cols
                ]
                for c, values in zip(cols, moved):
                    buf[1, pl.ds(0, TOK), c] = values
                    wide = values.astype(F32)
                    squares = squares + wide * wide
                square[...] = squares

                @pl.when(group == 0)
                def _():
                    start_tile(1, 0, 0)

                return 0

            lax.fori_loop(0, GROUPS, move, 0)
            col = root_scale()
            send_scale(1, col)
            for group in range(1, GROUPS):
                start_tile(1, 0, group)
            begin_heads(col)

        return 0

    lax.fori_loop(0, STEPS, phase_body, 0)

    col = root_scale()
    last_size = steps_ref[STEPS - 1]

    cols = [head_cols(head) for head in range(HEADS)]
    velocities = [accum[:, c] * col for c in cols]
    moved = [buf[1, pl.ds(0, TOK), c].astype(F32) + last_size * v for c, v in zip(cols, velocities)]
    for c, velocity, denoised in zip(cols, velocities, moved):
        denoised_ref[0, :, c] = denoised.astype(BF16)
        velocity_ref[0, :, c] = velocity.astype(BF16)

    for hop in range(2):
        tiles_left(1, hop)


PIECE = 16
PIECES = TOK // PIECE


def hand_over(denoised_in, velocity_in, denoised_out, velocity_out, sems):
    copies = [
        pltpu.make_async_copy(source.at[0, pl.ds(PIECE * i, PIECE)], target.at[0, pl.ds(PIECE * i, PIECE)], sems.at[which, i])
        for i in range(PIECES)
        for which, (source, target) in enumerate(((denoised_in, denoised_out), (velocity_in, velocity_out)))
    ]
    for copy in copies:
        copy.start()
    for copy in copies:
        copy.wait()


def per_device(latent, past_cache, neighbour_mask, gains, step_sizes):
    dma = pltpu.SemaphoreType.DMA
    hbm = pl.BlockSpec(memory_space=pltpu.HBM)
    vmem = pl.BlockSpec(memory_space=pltpu.VMEM)
    operands = [
        pltpu.with_memory_space_constraint(x, pltpu.HBM)
        for x in (latent, past_cache, neighbour_mask, gains, step_sizes)
    ]
    results = pl.pallas_call(
        kernel,
        out_shape=(pltpu.VMEM((1, TOK, HW), BF16),) * 2,
        in_specs=[hbm] * 5,
        out_specs=(vmem,) * 2,
        scratch_shapes=[
            pltpu.SMEM((1, 1, 4), jnp.int32),
            pltpu.VMEM((2, HW), F32),
            pltpu.SMEM((STEPS,), F32),
            pltpu.VMEM((2, ROWS, HW), BF16),
            pltpu.VMEM((TOK, HW), BF16),
            pltpu.VMEM((TOK, HW), F32),
            pltpu.VMEM((HEADS, TOK, HD), F32),
            pltpu.VMEM((HEADS, TOK, HD), F32),
            pltpu.VMEM((STEPS, 8, HD), F32),
            pltpu.VMEM((STEPS, 4, 8, HD), F32),
            pltpu.VMEM((4 * TOK, HD), F32),
            pltpu.VMEM((5, 8, HD), F32),
            pltpu.VMEM((TOK, HD), F32),
            dma((6,)),
            dma((2, RING)),
            dma((2, 16, 2)),
            dma((2, 16, 2)),
            dma((STEPS, 2, 2, GROUPS)),
            dma((STEPS, 4, GROUPS)),
            dma((STEPS, 2, 2)),
            dma((STEPS, 4)),
        ],
        compiler_params=pltpu.CompilerParams(
            collective_id=0, has_side_effects=True, vmem_limit_bytes=32 * 1024 * 1024
        ),
        cost_estimate=pl.CostEstimate(flops=760_000_000, bytes_accessed=1_200_000, transcendentals=1_600_000),
    )(*operands)
    return pl.pallas_call(
        hand_over,
        out_shape=(jax.ShapeDtypeStruct((1, TOK, HW), BF16),) * 2,
        in_specs=[vmem] * 2,
        out_specs=(hbm,) * 2,
        scratch_shapes=[dma((2, PIECES))],
    )(*(pltpu.with_memory_space_constraint(x, pltpu.VMEM) for x in results))


def solution(mesh):
    in_specs = (P("tm", "space", None), P(None, "tm", "space"), P("tm", "space", None), P(), P())
    out_specs = (P("tm", "space", None), P("tm", "space", None))
    return jax.shard_map(
        per_device, mesh=mesh, in_specs=in_specs, out_specs=out_specs, check_vma=False
    )
```

```python
import functools
import math

import jax
import jax.numpy as jnp
from jax import lax
from jax.experimental import pallas as pl
from jax.experimental.pallas import tpu as pltpu
from jax.sharding import PartitionSpec as P

HD = 128
HEADS = 20
HW = HD * HEADS
TOK = 64
STEPS = 2
SHARD = 16
GROUPS = 4
PER = HEADS // GROUPS
GW = PER * HD
EPS = 1e-6
SCORE_SCALE = math.log2(math.e) / math.sqrt(HD)
MASKED = -1e30
MESH = pl.DeviceIdType.MESH
F32 = jnp.float32
BF16 = jnp.bfloat16

STAGE = 128
NEAR, FAR = 3, 4
TILES = 3 * STAGE
ROWS = TILES + STEPS * 2 * STAGE
CHIP = TOK
RING = 14


def kernel(
    latent_hbm, cache_hbm, mask_hbm, gains_hbm, steps_hbm,
    denoised_ref, velocity_ref,
    mask_ref, gains_ref, steps_ref, buf, query, accum, peak, total, scale_own, scale_in, scale_col, bias, square,
    local_sem, ysend, ssend, yrecv, zsend, zrecv, rsend, rrecv,
):
    tm, space = lax.axis_index("tm"), lax.axis_index("space")
    n_tm, n_space = lax.axis_size("tm"), lax.axis_size("space")
    along_y = ((lax.rem(tm + 2, n_tm), space), (lax.rem(tm + n_tm - 2, n_tm), space))
    sibling = (tm + 1 - 2 * lax.rem(tm, 2), space)
    along_z = ((tm, lax.rem(space + 1, n_space)), (tm, lax.rem(space + n_space - 1, n_space)))
    has_low, has_high = space > 0, space < n_space - 1
    sends = ((has_high, has_low & has_high), (has_low, has_low & has_high))
    receives = ((has_low, space > 1), (has_high, space < n_space - 2))

    def remote(src, dst, send, recv, device):
        return pltpu.make_async_remote_copy(
            src_ref=src, dst_ref=dst, send_sem=send, recv_sem=recv, device_id=device, device_id_type=MESH
        )

    def half_cols(half):
        return pl.ds(pl.multiple_of(half * (HW // 2), HW // 2), HW // 2)

    def shard(which, index, half):
        rows = CHIP + SHARD * index + jnp.where(index >= 2, 2 * SHARD, 0)
        return buf.at[which, pl.ds(pl.multiple_of(rows, SHARD), SHARD), half_cols(half)]

    def slot(distance, direction):
        return 4 * distance - 2 + jnp.where(distance == 4, 0, 2 * direction)

    def ring_place(direction, number):
        which = lax.rem(number // 2 + direction, 2)
        return which, lax.rem(number, 2), number // 4 + 1

    def ring_copy(direction, number, own):
        which, half, distance = ring_place(direction, number)
        target = slot(distance, direction)
        if own:
            src = cache_hbm.at[which, :, half_cols(half)]
        else:
            src = shard(which, slot(distance - 1, direction), half)
        return remote(
            src, shard(which, target, half), ysend.at[direction, number], yrecv.at[which, target, half],
            along_y[direction],
        )

    def sib_copy(which, half, target, own=False):
        src = cache_hbm.at[which, :, half_cols(half)] if own else shard(which, target - 1, half)
        return remote(
            src, shard(which, target, half), ssend.at[which, target, half], yrecv.at[which, target, half], sibling
        )

    def ring_round(number):
        for direction in range(2):
            which, half, distance = ring_place(direction, number)
            ring_copy(direction, number, False).wait_recv()

            @pl.when(number + 4 < RING)
            def _():
                ring_copy(direction, number + 4, False).start()

            sib_copy(which, half, slot(distance, direction) + 1).start()

    def each_sibling(first, count, act):
        def body(i, _):
            act(sib_copy(lax.rem(i, 2), lax.rem(i // 2, 2), first + 2 * (i // 4)))
            return 0

        lax.fori_loop(0, 4 * count, body, 0)

    def columns(group):
        return pl.ds(pl.multiple_of(group * GW, GW), GW)

    def head_cols(head):
        if isinstance(head, int):
            return pl.ds(head * HD, HD)
        return pl.ds(pl.multiple_of(head * HD, HD), HD)

    def tile_rows(phase, number):
        return pl.ds(pl.multiple_of(TILES + phase * 2 * STAGE + number * TOK, TOK), TOK)

    def tile_part(phase, number, cols):
        return buf.at[1, tile_rows(phase, number), cols]

    def tile_copy(phase, direction, hop, group):
        cols = columns(group)
        if hop == 1:
            src = tile_part(phase, direction, cols)
        elif isinstance(phase, int) and phase == 0:
            src = latent_hbm.at[0, :, cols]
        else:
            src = buf.at[1, pl.ds(0, TOK), cols]
        target = 2 * hop + direction
        return remote(
            src, tile_part(phase, target, cols), zsend.at[phase, direction, hop, group],
            zrecv.at[phase, target, group], along_z[direction],
        )

    def scale_copy(phase, direction, hop):
        src = scale_own.at[phase] if hop == 0 else scale_in.at[phase, direction]
        target = 2 * hop + direction
        return remote(
            src, scale_in.at[phase, target], rsend.at[phase, direction, hop], rrecv.at[phase, target], along_z[direction]
        )

    def start_tile(phase, hop, group):
        for direction in range(2):
            @pl.when(sends[direction][hop])
            def _():
                tile_copy(phase, direction, hop, group).start()

    def wait_tile(phase, hop, group):
        for direction in range(2):
            @pl.when(receives[direction][hop])
            def _():
                tile_copy(phase, direction, hop, group).wait_recv()

        if hop == 0:
            start_tile(phase, 1, group)

    diagonal = lax.broadcasted_iota(jnp.int32, (TOK, HD), 0) == lax.broadcasted_iota(jnp.int32, (TOK, HD), 1)

    def take_scales(phase, hop):
        for direction in range(2):
            target = 2 * hop + direction

            @pl.when(receives[direction][hop])
            def _():
                scale_copy(phase, direction, hop).wait_recv()

            if hop == 0:
                @pl.when(sends[direction][1])
                def _():
                    scale_copy(phase, direction, 1).start()

            row = jnp.broadcast_to(scale_in[phase, target, 0:1, :], (TOK, HD))
            col = jnp.sum(jnp.where(diagonal, row, 0.0), axis=1, keepdims=True)
            scale_col[pl.ds(target * TOK, TOK), :] = jnp.broadcast_to(col, (TOK, HD))

    def root_scale():
        mean = jnp.sum(square[...], axis=1, keepdims=True) * (1.0 / HW)
        return jnp.broadcast_to(lax.rsqrt(mean + EPS), (TOK, HD))

    def send_scale(phase, col):
        row = jnp.sum(jnp.where(diagonal, col, 0.0), axis=0, keepdims=True)
        scale_own[phase] = jnp.broadcast_to(row, (8, HD))
        for direction in range(2):
            @pl.when(sends[direction][0])
            def _():
                scale_copy(phase, direction, 0).start()

    def begin_heads(col):
        def body(group, _):
            heads = [group * PER + i for i in range(PER)]
            normals = [buf[1, pl.ds(0, TOK), head_cols(head)].astype(F32) * col for head in heads]
            for head, normal in zip(heads, normals):
                cols = head_cols(head)
                query[:, cols] = (normal * gains_ref[0:1, cols]).astype(BF16)
                buf[0, pl.ds(0, TOK), cols] = (normal * gains_ref[1:2, cols]).astype(BF16)
                peak[head] = jnp.full((TOK, HD), MASKED, F32)
                total[head] = jnp.zeros((TOK, HD), F32)
                accum[:, cols] = jnp.zeros((TOK, HD), F32)
            return 0

        lax.fori_loop(0, GROUPS, body, 0)

    def value_rows(stage, count, phase):
        start = (stage + phase * 2) * STAGE if stage >= NEAR else stage * STAGE
        return pl.ds(pl.multiple_of(start, STAGE), count * STAGE)

    def keys_of(head, stage, count, phase):
        cols = head_cols(head)
        rows = value_rows(stage, count, phase)
        if stage < NEAR:
            return buf[0, rows, cols]
        scales = scale_col[pl.ds((stage - NEAR) * STAGE, STAGE), :]
        return (buf[1, rows, cols].astype(F32) * scales * gains_ref[1:2, cols]).astype(BF16)

    def mix(plan, weights, phase):
        mixed = []
        at = 0
        while at < len(plan):
            head, spans = plan[at]
            pair = 2 if at + 1 < len(plan) and plan[at + 1] == (head + 1, spans) else 1
            cols = pl.ds(head * HD, pair * HD)
            sums = None
            for i, (stage, count) in enumerate(spans):
                stacked = jnp.concatenate([weights[at + j][i] for j in range(pair)], axis=0)
                product = jnp.dot(stacked, buf[1, value_rows(stage, count, phase), cols], preferred_element_type=F32)
                sums = product if sums is None else sums + product
            mixed += [sums[j * TOK : (j + 1) * TOK, j * HD : (j + 1) * HD] for j in range(pair)]
            at += pair
        return mixed

    def update(phase, *parts):
        plan = [(head, spans) for heads, spans in parts for head in heads]
        cols = [head_cols(head) for head, _ in plan]
        keys = [[keys_of(head, stage, count, phase) for stage, count in spans] for head, spans in plan]
        queries = [query[:, c] for c in cols]
        old_peaks = [peak[head] for head, _ in plan]
        scores = []
        for q, each, (_, spans) in zip(queries, keys, plan):
            pieces = []
            for k, (stage, count) in zip(each, spans):
                raw = lax.dot_general(q, k, (((1,), (1,)), ((), ())), preferred_element_type=F32)
                pieces.append([
                    raw[:, i * STAGE : (i + 1) * STAGE] * SCORE_SCALE + bias[stage + i, 0:1, :] for i in range(count)
                ])
            scores.append(pieces)
        tops = [functools.reduce(jnp.maximum, sum(pieces, [])) for pieces in scores]
        peaks = [
            jnp.maximum(old, jnp.broadcast_to(jnp.max(top, axis=1, keepdims=True), (TOK, HD)))
            for old, top in zip(old_peaks, tops)
        ]
        expos = [[[jnp.exp2(s - p) for s in span] for span in pieces] for pieces, p in zip(scores, peaks)]
        weights = [[jnp.concatenate([e.astype(BF16) for e in span], axis=1) for span in each] for each in expos]
        mixed = mix(plan, weights, phase)
        factors = [jnp.exp2(old - new) for old, new in zip(old_peaks, peaks)]
        totals = [
            total[head] * f + functools.reduce(jnp.add, sum(each, []))
            for (head, _), f, each in zip(plan, factors, expos)
        ]
        sums = [accum[:, c] * f + m for c, f, m in zip(cols, factors, mixed)]
        for i, (head, _) in enumerate(plan):
            peak[head] = peaks[i]
            total[head] = totals[i]
            accum[:, cols[i]] = sums[i]

    def finish(heads):
        attended = [accum[:, head_cols(head)] / jnp.sum(total[head], axis=1, keepdims=True) for head in heads]
        squares = square[...]
        for head, values in zip(heads, attended):
            accum[:, head_cols(head)] = values
            squares = squares + values * values
        square[...] = squares

    def tiles_left(phase, hop):
        for direction in range(2):
            @pl.when(sends[direction][hop])
            def _():
                scale_copy(phase, direction, hop).wait_send()

                def body(group, _):
                    tile_copy(phase, direction, hop, group).wait_send()
                    return 0

                lax.fori_loop(0, GROUPS, body, 0)

    def earlier_sends_left():
        def ring_left(number, _):
            for direction in range(2):
                ring_copy(direction, number, False).wait_send()
            return 0

        for number in range(4):
            for direction in range(2):
                ring_copy(direction, number, True).wait_send()
        lax.fori_loop(4, RING, ring_left, 0)
        for which in range(2):
            for half in range(2):
                sib_copy(which, half, 1, True).wait_send()
        each_sibling(3, 7, lambda copy: copy.wait_send())
        for hop in range(2):
            tiles_left(0, hop)

    loads = [
        pltpu.make_async_copy(latent_hbm.at[0], buf.at[1, pl.ds(0, TOK)], local_sem.at[0]),
        pltpu.make_async_copy(cache_hbm.at[0], buf.at[0, pl.ds(CHIP, SHARD)], local_sem.at[1]),
        pltpu.make_async_copy(cache_hbm.at[1], buf.at[1, pl.ds(CHIP, SHARD)], local_sem.at[2]),
        pltpu.make_async_copy(mask_hbm, mask_ref, local_sem.at[3]),
        pltpu.make_async_copy(gains_hbm, gains_ref, local_sem.at[4]),
        pltpu.make_async_copy(steps_hbm, steps_ref, local_sem.at[5]),
    ]
    barrier = pltpu.get_barrier_semaphore()
    for device in (*along_y, sibling):
        pl.semaphore_signal(barrier, inc=1, device_id=device, device_id_type=MESH)
    for direction in range(2):
        @pl.when(sends[direction][0])
        def _():
            pl.semaphore_signal(barrier, inc=1, device_id=along_z[direction], device_id_type=MESH)

    for load in loads:
        load.start()
    pl.semaphore_wait(barrier, 3 + lax.min(space, 1) + lax.min(n_space - 1 - space, 1))

    start_tile(0, 0, 0)
    for number in range(4):
        for direction in range(2):
            ring_copy(direction, number, True).start()
    for which in range(2):
        for half in range(2):
            sib_copy(which, half, 1, True).start()

    for hop in range(2):
        for direction in range(2):
            @pl.when(jnp.logical_not(receives[direction][hop]))
            def _():
                for phase in range(STEPS):
                    buf[1, tile_rows(phase, 2 * hop + direction), :] = jnp.zeros((TOK, HW), BF16)
                    scale_in[phase, 2 * hop + direction] = jnp.zeros((8, HD), F32)

    for which in range(2):
        for stage in (0, 2):
            buf[which, pl.ds(stage * STAGE + 3 * STAGE // 4, STAGE // 4), :] = jnp.zeros((STAGE // 4, HW), BF16)

    for load in loads[3:]:
        load.wait()
    lane = lax.broadcasted_iota(jnp.int32, (8, HD), 1)
    for stage in (0, 2):
        bias[stage] = jnp.where(lane < 3 * STAGE // 4, 0.0, MASKED).astype(F32)
    bias[1] = jnp.zeros((8, HD), F32)
    for hop in range(2):
        low, high = (1, 2) if hop == 0 else (0, 3)
        low_ok = (mask_ref[0, 0, low] > 0) & (space - hop > 0)
        high_ok = (mask_ref[0, 0, high] > 0) & (space + hop + 1 < n_space)
        low_bias = jnp.where(low_ok, 0.0, MASKED).astype(F32)
        high_bias = jnp.where(high_ok, 0.0, MASKED).astype(F32)
        bias[NEAR + hop] = jnp.where(lane < TOK, low_bias, high_bias)

    loads[0].wait()
    square[...] = jnp.zeros((TOK, HD), F32)

    def add_squares(group, _):
        squares = square[...]
        for i in range(PER):
            values = buf[1, pl.ds(0, TOK), head_cols(group * PER + i)].astype(F32)
            squares = squares + values * values
        square[...] = squares
        return 0

    lax.fori_loop(0, GROUPS, add_squares, 0)
    col = root_scale()
    send_scale(0, col)
    for group in range(1, GROUPS):
        start_tile(0, 0, group)
    begin_heads(col)
    for load in loads[1:3]:
        load.wait()

    def phase_body(phase, _):
        first = phase == 0
        square[...] = jnp.zeros((TOK, HD), F32)

        def rounds(start, count):
            @pl.when(first)
            def _():
                for number in range(start, start + count):
                    ring_round(number)

        def last_shards(half):
            for target in (11, 13, 15):
                for which in range(2):
                    sib_copy(which, half, target).wait_recv()

        every = range(HEADS)

        @pl.when(first)
        def _():
            each_sibling(1, 1, lambda copy: copy.wait_recv())

        @pl.when(first)
        def _():
            update(phase, (every, ((0, 1),)))

        @pl.when(jnp.logical_not(first))
        def _():
            update(phase, (every[: 2 * PER], ((0, 3),)))
            update(phase, (every[2 * PER :], ((0, 3),)))

        near, far = ((NEAR, 1),), ((FAR, 1),)
        for group in range(GROUPS):
            rounds(2 * group, 2)
            wait_tile(phase, 0, group)
            if group == 0:
                take_scales(phase, 0)
            update(phase, (every[group * PER : (group + 1) * PER], near))
        rounds(8, 2)

        @pl.when(first)
        def _():
            each_sibling(3, 4, lambda copy: copy.wait_recv())
            update(phase, (every, ((1, 1),)))

        @pl.when(jnp.logical_not(first))
        def _():
            earlier_sends_left()

        rounds(10, 2)
        wait_tile(phase, 1, 0)
        wait_tile(phase, 1, 1)
        take_scales(phase, 1)
        update(phase, (every[: 2 * PER], far))
        rounds(12, 2)
        wait_tile(phase, 1, 2)
        update(phase, (every[2 * PER : 3 * PER], far))

        @pl.when(first)
        def _():
            last_shards(0)
            update(phase, (every[: 2 * PER], ((2, 1),)))
            last_shards(1)
            wait_tile(phase, 1, 3)
            update(phase, (every[2 * PER : 3 * PER], ((2, 1),)), (every[3 * PER :], ((2, 1), (FAR, 1))))
            finish(every)

        @pl.when(jnp.logical_not(first))
        def _():
            finish(every[: 3 * PER])
            wait_tile(phase, 1, 3)
            update(phase, (every[3 * PER :], far))
            finish(every[3 * PER :])

        @pl.when(first)
        def _():
            col = root_scale()
            step_size = steps_ref[0]
            square[...] = jnp.zeros((TOK, HD), F32)

            def move(group, _):
                squares = square[...]
                cols = [head_cols(group * PER + i) for i in range(PER)]
                moved = [
                    (buf[1, pl.ds(0, TOK), c].astype(F32) + step_size * (accum[:, c] * col)).astype(BF16)
                    for c in cols
                ]
                for c, values in zip(cols, moved):
                    buf[1, pl.ds(0, TOK), c] = values
                    wide = values.astype(F32)
                    squares = squares + wide * wide
                square[...] = squares

                @pl.when(group == 0)
                def _():
                    start_tile(1, 0, 0)

                return 0

            lax.fori_loop(0, GROUPS, move, 0)
            col = root_scale()
            send_scale(1, col)
            for group in range(1, GROUPS):
                start_tile(1, 0, group)
            begin_heads(col)

        return 0

    lax.fori_loop(0, STEPS, phase_body, 0)

    col = root_scale()
    last_size = steps_ref[STEPS - 1]

    cols = [head_cols(head) for head in range(HEADS)]
    velocities = [accum[:, c] * col for c in cols]
    moved = [buf[1, pl.ds(0, TOK), c].astype(F32) + last_size * v for c, v in zip(cols, velocities)]
    for c, velocity, denoised in zip(cols, velocities, moved):
        denoised_ref[0, :, c] = denoised.astype(BF16)
        velocity_ref[0, :, c] = velocity.astype(BF16)

    for hop in range(2):
        tiles_left(1, hop)


PIECE = 16
PIECES = TOK // PIECE


def hand_over(denoised_in, velocity_in, denoised_out, velocity_out, sems):
    copies = [
        pltpu.make_async_copy(source.at[0, pl.ds(PIECE * i, PIECE)], target.at[0, pl.ds(PIECE * i, PIECE)], sems.at[which, i])
        for i in range(PIECES)
        for which, (source, target) in enumerate(((denoised_in, denoised_out), (velocity_in, velocity_out)))
    ]
    for copy in copies:
        copy.start()
    for copy in copies:
        copy.wait()


def per_device(latent, past_cache, neighbour_mask, gains, step_sizes):
    dma = pltpu.SemaphoreType.DMA
    hbm = pl.BlockSpec(memory_space=pltpu.HBM)
    vmem = pl.BlockSpec(memory_space=pltpu.VMEM)
    operands = [
        pltpu.with_memory_space_constraint(x, pltpu.HBM)
        for x in (latent, past_cache, neighbour_mask, gains, step_sizes)
    ]
    results = pl.pallas_call(
        kernel,
        out_shape=(pltpu.VMEM((1, TOK, HW), BF16),) * 2,
        in_specs=[hbm] * 5,
        out_specs=(vmem,) * 2,
        scratch_shapes=[
            pltpu.SMEM((1, 1, 4), jnp.int32),
            pltpu.VMEM((2, HW), F32),
            pltpu.SMEM((STEPS,), F32),
            pltpu.VMEM((2, ROWS, HW), BF16),
            pltpu.VMEM((TOK, HW), BF16),
            pltpu.VMEM((TOK, HW), F32),
            pltpu.VMEM((HEADS, TOK, HD), F32),
            pltpu.VMEM((HEADS, TOK, HD), F32),
            pltpu.VMEM((STEPS, 8, HD), F32),
            pltpu.VMEM((STEPS, 4, 8, HD), F32),
            pltpu.VMEM((4 * TOK, HD), F32),
            pltpu.VMEM((5, 8, HD), F32),
            pltpu.VMEM((TOK, HD), F32),
            dma((6,)),
            dma((2, RING)),
            dma((2, 16, 2)),
            dma((2, 16, 2)),
            dma((STEPS, 2, 2, GROUPS)),
            dma((STEPS, 4, GROUPS)),
            dma((STEPS, 2, 2)),
            dma((STEPS, 4)),
        ],
        compiler_params=pltpu.CompilerParams(
            collective_id=0, has_side_effects=True, vmem_limit_bytes=32 * 1024 * 1024
        ),
        cost_estimate=pl.CostEstimate(flops=760_000_000, bytes_accessed=1_200_000, transcendentals=1_600_000),
    )(*operands)
    return pl.pallas_call(
        hand_over,
        out_shape=(jax.ShapeDtypeStruct((1, TOK, HW), BF16),) * 2,
        in_specs=[vmem] * 2,
        out_specs=(hbm,) * 2,
        scratch_shapes=[dma((2, PIECES))],
    )(*(pltpu.with_memory_space_constraint(x, pltpu.VMEM) for x in results))


def solution(mesh):
    in_specs = (P("tm", "space", None), P(None, "tm", "space"), P("tm", "space", None), P(), P())
    out_specs = (P("tm", "space", None), P("tm", "space", None))
    return jax.shard_map(
        per_device, mesh=mesh, in_specs=in_specs, out_specs=out_specs, check_vma=False
    )
```

```python
import functools
import math

import jax
import jax.numpy as jnp
from jax import lax
from jax.experimental import pallas as pl
from jax.experimental.pallas import tpu as pltpu
from jax.sharding import PartitionSpec as P

HD = 128
HEADS = 20
HW = HD * HEADS
TOK = 64
STEPS = 2
SHARD = 16
GROUPS = 4
PER = HEADS // GROUPS
GW = PER * HD
EPS = 1e-6
SCORE_SCALE = math.log2(math.e) / math.sqrt(HD)
MASKED = -1e30
MESH = pl.DeviceIdType.MESH
F32 = jnp.float32
BF16 = jnp.bfloat16

STAGE = 128
NEAR, FAR = 3, 4
TILES = 3 * STAGE
ROWS = TILES + STEPS * 2 * STAGE
CHIP = TOK
RING = 14


def kernel(
    latent_hbm, cache_hbm, mask_hbm, gains_hbm, steps_hbm,
    denoised_ref, velocity_ref,
    mask_ref, gains_ref, steps_ref, buf, query, accum, peak, total, scale_own, scale_in, scale_col, bias, square,
    local_sem, ysend, ssend, yrecv, zsend, zrecv, rsend, rrecv,
):
    tm, space = lax.axis_index("tm"), lax.axis_index("space")
    n_tm, n_space = lax.axis_size("tm"), lax.axis_size("space")
    along_y = ((lax.rem(tm + 2, n_tm), space), (lax.rem(tm + n_tm - 2, n_tm), space))
    sibling = (tm + 1 - 2 * lax.rem(tm, 2), space)
    along_z = ((tm, lax.rem(space + 1, n_space)), (tm, lax.rem(space + n_space - 1, n_space)))
    has_low, has_high = space > 0, space < n_space - 1
    sends = ((has_high, has_low & has_high), (has_low, has_low & has_high))
    receives = ((has_low, space > 1), (has_high, space < n_space - 2))

    def remote(src, dst, send, recv, device):
        return pltpu.make_async_remote_copy(
            src_ref=src, dst_ref=dst, send_sem=send, recv_sem=recv, device_id=device, device_id_type=MESH
        )

    def half_cols(half):
        return pl.ds(pl.multiple_of(half * (HW // 2), HW // 2), HW // 2)

    def shard(which, index, half):
        rows = CHIP + SHARD * index + jnp.where(index >= 2, 2 * SHARD, 0)
        return buf.at[which, pl.ds(pl.multiple_of(rows, SHARD), SHARD), half_cols(half)]

    def slot(distance, direction):
        return 4 * distance - 2 + jnp.where(distance == 4, 0, 2 * direction)

    def ring_place(direction, number):
        which = lax.rem(number // 2 + direction, 2)
        return which, lax.rem(number, 2), number // 4 + 1

    def ring_copy(direction, number, own):
        which, half, distance = ring_place(direction, number)
        target = slot(distance, direction)
        if own:
            src = cache_hbm.at[which, :, half_cols(half)]
        else:
            src = shard(which, slot(distance - 1, direction), half)
        return remote(
            src, shard(which, target, half), ysend.at[direction, number], yrecv.at[which, target, half],
            along_y[direction],
        )

    def sib_copy(which, half, target, own=False):
        src = cache_hbm.at[which, :, half_cols(half)] if own else shard(which, target - 1, half)
        return remote(
            src, shard(which, target, half), ssend.at[which, target, half], yrecv.at[which, target, half], sibling
        )

    def ring_round(number):
        for direction in range(2):
            which, half, distance = ring_place(direction, number)
            ring_copy(direction, number, False).wait_recv()

            @pl.when(number + 4 < RING)
            def _():
                ring_copy(direction, number + 4, False).start()

            sib_copy(which, half, slot(distance, direction) + 1).start()

    def each_sibling(first, count, act):
        def body(i, _):
            act(sib_copy(lax.rem(i, 2), lax.rem(i // 2, 2), first + 2 * (i // 4)))
            return 0

        lax.fori_loop(0, 4 * count, body, 0)

    def columns(group):
        return pl.ds(pl.multiple_of(group * GW, GW), GW)

    def head_cols(head):
        if isinstance(head, int):
            return pl.ds(head * HD, HD)
        return pl.ds(pl.multiple_of(head * HD, HD), HD)

    def tile_rows(phase, number):
        return pl.ds(pl.multiple_of(TILES + phase * 2 * STAGE + number * TOK, TOK), TOK)

    def tile_part(phase, number, cols):
        return buf.at[1, tile_rows(phase, number), cols]

    def tile_copy(phase, direction, hop, group):
        cols = columns(group)
        if hop == 1:
            src = tile_part(phase, direction, cols)
        elif isinstance(phase, int) and phase == 0:
            src = latent_hbm.at[0, :, cols]
        else:
            src = buf.at[1, pl.ds(0, TOK), cols]
        target = 2 * hop + direction
        return remote(
            src, tile_part(phase, target, cols), zsend.at[phase, direction, hop, group],
            zrecv.at[phase, target, group], along_z[direction],
        )

    def scale_copy(phase, direction, hop):
        src = scale_own.at[phase] if hop == 0 else scale_in.at[phase, direction]
        target = 2 * hop + direction
        return remote(
            src, scale_in.at[phase, target], rsend.at[phase, direction, hop], rrecv.at[phase, target], along_z[direction]
        )

    def start_tile(phase, hop, group):
        for direction in range(2):
            @pl.when(sends[direction][hop])
            def _():
                tile_copy(phase, direction, hop, group).start()

    def wait_tile(phase, hop, group):
        for direction in range(2):
            @pl.when(receives[direction][hop])
            def _():
                tile_copy(phase, direction, hop, group).wait_recv()

        if hop == 0:
            start_tile(phase, 1, group)

    diagonal = lax.broadcasted_iota(jnp.int32, (TOK, HD), 0) == lax.broadcasted_iota(jnp.int32, (TOK, HD), 1)

    def take_scales(phase, hop):
        for direction in range(2):
            target = 2 * hop + direction

            @pl.when(receives[direction][hop])
            def _():
                scale_copy(phase, direction, hop).wait_recv()

            if hop == 0:
                @pl.when(sends[direction][1])
                def _():
                    scale_copy(phase, direction, 1).start()

            row = jnp.broadcast_to(scale_in[phase, target, 0:1, :], (TOK, HD))
            col = jnp.sum(jnp.where(diagonal, row, 0.0), axis=1, keepdims=True)
            scale_col[pl.ds(target * TOK, TOK), :] = jnp.broadcast_to(col, (TOK, HD))

    def root_scale():
        mean = jnp.sum(square[...], axis=1, keepdims=True) * (1.0 / HW)
        return jnp.broadcast_to(lax.rsqrt(mean + EPS), (TOK, HD))

    def send_scale(phase, col):
        row = jnp.sum(jnp.where(diagonal, col, 0.0), axis=0, keepdims=True)
        scale_own[phase] = jnp.broadcast_to(row, (8, HD))
        for direction in range(2):
            @pl.when(sends[direction][0])
            def _():
                scale_copy(phase, direction, 0).start()

    def begin_heads(col):
        def body(group, _):
            heads = [group * PER + i for i in range(PER)]
            normals = [buf[1, pl.ds(0, TOK), head_cols(head)].astype(F32) * col for head in heads]
            for head, normal in zip(heads, normals):
                cols = head_cols(head)
                query[:, cols] = (normal * gains_ref[0:1, cols]).astype(BF16)
                buf[0, pl.ds(0, TOK), cols] = (normal * gains_ref[1:2, cols]).astype(BF16)
                peak[head] = jnp.full((TOK, HD), MASKED, F32)
                total[head] = jnp.zeros((TOK, HD), F32)
                accum[:, cols] = jnp.zeros((TOK, HD), F32)
            return 0

        lax.fori_loop(0, GROUPS, body, 0)

    def value_rows(stage, count, phase):
        start = (stage + phase * 2) * STAGE if stage >= NEAR else stage * STAGE
        return pl.ds(pl.multiple_of(start, STAGE), count * STAGE)

    def keys_of(head, stage, count, phase):
        cols = head_cols(head)
        rows = value_rows(stage, count, phase)
        if stage < NEAR:
            return buf[0, rows, cols]
        scales = scale_col[pl.ds((stage - NEAR) * STAGE, STAGE), :]
        return (buf[1, rows, cols].astype(F32) * scales * gains_ref[1:2, cols]).astype(BF16)

    def update(phase, *parts):
        plan = [(head, spans) for heads, spans in parts for head in heads]
        units = []
        while plan:
            head, spans = plan[0]
            pair = 2 if len(plan) > 1 and plan[1] == (head + 1, spans) else 1
            units.append((range(head, head + pair), spans))
            plan = plan[pair:]

        def score(unit, held):
            heads, spans = unit
            held["scores"] = []
            for head in heads:
                q = query[:, head_cols(head)]
                pieces = []
                for stage, count in spans:
                    k = keys_of(head, stage, count, phase)
                    raw = lax.dot_general(q, k, (((1,), (1,)), ((), ())), preferred_element_type=F32)
                    pieces.append([
                        raw[:, i * STAGE : (i + 1) * STAGE] * SCORE_SCALE + bias[stage + i, 0:1, :]
                        for i in range(count)
                    ])
                held["scores"].append(pieces)

        def top(unit, held):
            heads, _ = unit
            held["old"] = [peak[head] for head in heads]
            tops = [functools.reduce(jnp.maximum, sum(pieces, [])) for pieces in held["scores"]]
            held["peaks"] = [
                jnp.maximum(old, jnp.broadcast_to(jnp.max(t, axis=1, keepdims=True), (TOK, HD)))
                for old, t in zip(held["old"], tops)
            ]

        def mix(unit, held):
            heads, spans = unit
            held["expos"] = [
                [[jnp.exp2(s - p) for s in span] for span in pieces] for pieces, p in zip(held["scores"], held["peaks"])
            ]
            cols = pl.ds(heads[0] * HD, len(heads) * HD)
            product = None
            for i, (stage, count) in enumerate(spans):
                weights = jnp.concatenate(
                    [jnp.concatenate([e.astype(BF16) for e in each[i]], axis=1) for each in held["expos"]], axis=0
                )
                values = buf[1, value_rows(stage, count, phase), cols]
                part = jnp.dot(weights, values, preferred_element_type=F32)
                product = part if product is None else product + part
            held["mixed"] = [product[j * TOK : (j + 1) * TOK, j * HD : (j + 1) * HD] for j in range(len(heads))]

        def keep(unit, held):
            for i, head in enumerate(unit[0]):
                factor = jnp.exp2(held["old"][i] - held["peaks"][i])
                added = functools.reduce(jnp.add, sum(held["expos"][i], []))
                peak[head] = held["peaks"][i]
                total[head] = total[head] * factor + added
                accum[:, head_cols(head)] = accum[:, head_cols(head)] * factor + held["mixed"][i]
            held.clear()

        steps = (score, top, mix, keep)
        held = [{} for _ in units]
        for at in range(len(units) + len(steps) - 1):
            for behind in reversed(range(len(steps))):
                if 0 <= at - behind < len(units):
                    steps[behind](units[at - behind], held[at - behind])

    def finish(heads):
        attended = [accum[:, head_cols(head)] / jnp.sum(total[head], axis=1, keepdims=True) for head in heads]
        squares = square[...]
        for head, values in zip(heads, attended):
            accum[:, head_cols(head)] = values
            squares = squares + values * values
        square[...] = squares

    def tiles_left(phase, hop):
        for direction in range(2):
            @pl.when(sends[direction][hop])
            def _():
                scale_copy(phase, direction, hop).wait_send()

                def body(group, _):
                    tile_copy(phase, direction, hop, group).wait_send()
                    return 0

                lax.fori_loop(0, GROUPS, body, 0)

    def earlier_sends_left():
        def ring_left(number, _):
            for direction in range(2):
                ring_copy(direction, number, False).wait_send()
            return 0

        for number in range(4):
            for direction in range(2):
                ring_copy(direction, number, True).wait_send()
        lax.fori_loop(4, RING, ring_left, 0)
        for which in range(2):
            for half in range(2):
                sib_copy(which, half, 1, True).wait_send()
        each_sibling(3, 7, lambda copy: copy.wait_send())
        for hop in range(2):
            tiles_left(0, hop)

    loads = [
        pltpu.make_async_copy(latent_hbm.at[0], buf.at[1, pl.ds(0, TOK)], local_sem.at[0]),
        pltpu.make_async_copy(cache_hbm.at[0], buf.at[0, pl.ds(CHIP, SHARD)], local_sem.at[1]),
        pltpu.make_async_copy(cache_hbm.at[1], buf.at[1, pl.ds(CHIP, SHARD)], local_sem.at[2]),
        pltpu.make_async_copy(mask_hbm, mask_ref, local_sem.at[3]),
        pltpu.make_async_copy(gains_hbm, gains_ref, local_sem.at[4]),
        pltpu.make_async_copy(steps_hbm, steps_ref, local_sem.at[5]),
    ]
    barrier = pltpu.get_barrier_semaphore()
    for device in (*along_y, sibling):
        pl.semaphore_signal(barrier, inc=1, device_id=device, device_id_type=MESH)
    for direction in range(2):
        @pl.when(sends[direction][0])
        def _():
            pl.semaphore_signal(barrier, inc=1, device_id=along_z[direction], device_id_type=MESH)

    for load in loads:
        load.start()
    pl.semaphore_wait(barrier, 3 + lax.min(space, 1) + lax.min(n_space - 1 - space, 1))

    start_tile(0, 0, 0)
    for number in range(4):
        for direction in range(2):
            ring_copy(direction, number, True).start()
    for which in range(2):
        for half in range(2):
            sib_copy(which, half, 1, True).start()

    for hop in range(2):
        for direction in range(2):
            @pl.when(jnp.logical_not(receives[direction][hop]))
            def _():
                for phase in range(STEPS):
                    buf[1, tile_rows(phase, 2 * hop + direction), :] = jnp.zeros((TOK, HW), BF16)
                    scale_in[phase, 2 * hop + direction] = jnp.zeros((8, HD), F32)

    for which in range(2):
        for stage in (0, 2):
            buf[which, pl.ds(stage * STAGE + 3 * STAGE // 4, STAGE // 4), :] = jnp.zeros((STAGE // 4, HW), BF16)

    for load in loads[3:]:
        load.wait()
    lane = lax.broadcasted_iota(jnp.int32, (8, HD), 1)
    for stage in (0, 2):
        bias[stage] = jnp.where(lane < 3 * STAGE // 4, 0.0, MASKED).astype(F32)
    bias[1] = jnp.zeros((8, HD), F32)
    for hop in range(2):
        low, high = (1, 2) if hop == 0 else (0, 3)
        low_ok = (mask_ref[0, 0, low] > 0) & (space - hop > 0)
        high_ok = (mask_ref[0, 0, high] > 0) & (space + hop + 1 < n_space)
        low_bias = jnp.where(low_ok, 0.0, MASKED).astype(F32)
        high_bias = jnp.where(high_ok, 0.0, MASKED).astype(F32)
        bias[NEAR + hop] = jnp.where(lane < TOK, low_bias, high_bias)

    loads[0].wait()
    square[...] = jnp.zeros((TOK, HD), F32)

    def add_squares(group, _):
        squares = square[...]
        for i in range(PER):
            values = buf[1, pl.ds(0, TOK), head_cols(group * PER + i)].astype(F32)
            squares = squares + values * values
        square[...] = squares
        return 0

    lax.fori_loop(0, GROUPS, add_squares, 0)
    col = root_scale()
    send_scale(0, col)
    for group in range(1, GROUPS):
        start_tile(0, 0, group)
    begin_heads(col)
    for load in loads[1:3]:
        load.wait()

    def phase_body(phase, _):
        first = phase == 0
        square[...] = jnp.zeros((TOK, HD), F32)

        def rounds(start, count):
            @pl.when(first)
            def _():
                for number in range(start, start + count):
                    ring_round(number)

        def last_shards(half):
            for target in (11, 13, 15):
                for which in range(2):
                    sib_copy(which, half, target).wait_recv()

        every = range(HEADS)

        @pl.when(first)
        def _():
            each_sibling(1, 1, lambda copy: copy.wait_recv())

        @pl.when(first)
        def _():
            update(phase, (every, ((0, 1),)))

        @pl.when(jnp.logical_not(first))
        def _():
            update(phase, (every[: 2 * PER], ((0, 3),)))
            update(phase, (every[2 * PER :], ((0, 3),)))

        near, far = ((NEAR, 1),), ((FAR, 1),)
        for group in range(GROUPS):
            rounds(2 * group, 2)
            wait_tile(phase, 0, group)
            if group == 0:
                take_scales(phase, 0)
            update(phase, (every[group * PER : (group + 1) * PER], near))
        rounds(8, 2)

        @pl.when(first)
        def _():
            each_sibling(3, 4, lambda copy: copy.wait_recv())
            update(phase, (every, ((1, 1),)))

        @pl.when(jnp.logical_not(first))
        def _():
            earlier_sends_left()

        rounds(10, 2)
        wait_tile(phase, 1, 0)
        wait_tile(phase, 1, 1)
        take_scales(phase, 1)
        update(phase, (every[: 2 * PER], far))
        rounds(12, 2)
        wait_tile(phase, 1, 2)
        update(phase, (every[2 * PER : 3 * PER], far))

        @pl.when(first)
        def _():
            last_shards(0)
            update(phase, (every[: 2 * PER], ((2, 1),)))
            last_shards(1)
            wait_tile(phase, 1, 3)
            update(phase, (every[2 * PER : 3 * PER], ((2, 1),)), (every[3 * PER :], ((2, 1), (FAR, 1))))
            finish(every)

        @pl.when(jnp.logical_not(first))
        def _():
            finish(every[: 3 * PER])
            wait_tile(phase, 1, 3)
            update(phase, (every[3 * PER :], far))
            finish(every[3 * PER :])

        @pl.when(first)
        def _():
            col = root_scale()
            step_size = steps_ref[0]
            square[...] = jnp.zeros((TOK, HD), F32)

            def move(group, _):
                squares = square[...]
                cols = [head_cols(group * PER + i) for i in range(PER)]
                moved = [
                    (buf[1, pl.ds(0, TOK), c].astype(F32) + step_size * (accum[:, c] * col)).astype(BF16)
                    for c in cols
                ]
                for c, values in zip(cols, moved):
                    buf[1, pl.ds(0, TOK), c] = values
                    wide = values.astype(F32)
                    squares = squares + wide * wide
                square[...] = squares

                @pl.when(group == 0)
                def _():
                    start_tile(1, 0, 0)

                return 0

            lax.fori_loop(0, GROUPS, move, 0)
            col = root_scale()
            send_scale(1, col)
            for group in range(1, GROUPS):
                start_tile(1, 0, group)
            begin_heads(col)

        return 0

    lax.fori_loop(0, STEPS, phase_body, 0)

    col = root_scale()
    last_size = steps_ref[STEPS - 1]

    cols = [head_cols(head) for head in range(HEADS)]
    velocities = [accum[:, c] * col for c in cols]
    moved = [buf[1, pl.ds(0, TOK), c].astype(F32) + last_size * v for c, v in zip(cols, velocities)]
    for c, velocity, denoised in zip(cols, velocities, moved):
        denoised_ref[0, :, c] = denoised.astype(BF16)
        velocity_ref[0, :, c] = velocity.astype(BF16)

    for hop in range(2):
        tiles_left(1, hop)


PIECE = 16
PIECES = TOK // PIECE


def hand_over(denoised_in, velocity_in, denoised_out, velocity_out, sems):
    copies = [
        pltpu.make_async_copy(source.at[0, pl.ds(PIECE * i, PIECE)], target.at[0, pl.ds(PIECE * i, PIECE)], sems.at[which, i])
        for i in range(PIECES)
        for which, (source, target) in enumerate(((denoised_in, denoised_out), (velocity_in, velocity_out)))
    ]
    for copy in copies:
        copy.start()
    for copy in copies:
        copy.wait()


def per_device(latent, past_cache, neighbour_mask, gains, step_sizes):
    dma = pltpu.SemaphoreType.DMA
    hbm = pl.BlockSpec(memory_space=pltpu.HBM)
    vmem = pl.BlockSpec(memory_space=pltpu.VMEM)
    operands = [
        pltpu.with_memory_space_constraint(x, pltpu.HBM)
        for x in (latent, past_cache, neighbour_mask, gains, step_sizes)
    ]
    results = pl.pallas_call(
        kernel,
        out_shape=(pltpu.VMEM((1, TOK, HW), BF16),) * 2,
        in_specs=[hbm] * 5,
        out_specs=(vmem,) * 2,
        scratch_shapes=[
            pltpu.SMEM((1, 1, 4), jnp.int32),
            pltpu.VMEM((2, HW), F32),
            pltpu.SMEM((STEPS,), F32),
            pltpu.VMEM((2, ROWS, HW), BF16),
            pltpu.VMEM((TOK, HW), BF16),
            pltpu.VMEM((TOK, HW), F32),
            pltpu.VMEM((HEADS, TOK, HD), F32),
            pltpu.VMEM((HEADS, TOK, HD), F32),
            pltpu.VMEM((STEPS, 8, HD), F32),
            pltpu.VMEM((STEPS, 4, 8, HD), F32),
            pltpu.VMEM((4 * TOK, HD), F32),
            pltpu.VMEM((5, 8, HD), F32),
            pltpu.VMEM((TOK, HD), F32),
            dma((6,)),
            dma((2, RING)),
            dma((2, 16, 2)),
            dma((2, 16, 2)),
            dma((STEPS, 2, 2, GROUPS)),
            dma((STEPS, 4, GROUPS)),
            dma((STEPS, 2, 2)),
            dma((STEPS, 4)),
        ],
        compiler_params=pltpu.CompilerParams(
            collective_id=0, has_side_effects=True, vmem_limit_bytes=32 * 1024 * 1024
        ),
        cost_estimate=pl.CostEstimate(flops=760_000_000, bytes_accessed=1_200_000, transcendentals=1_600_000),
    )(*operands)
    return pl.pallas_call(
        hand_over,
        out_shape=(jax.ShapeDtypeStruct((1, TOK, HW), BF16),) * 2,
        in_specs=[vmem] * 2,
        out_specs=(hbm,) * 2,
        scratch_shapes=[dma((2, PIECES))],
    )(*(pltpu.with_memory_space_constraint(x, pltpu.VMEM) for x in results))


def solution(mesh):
    in_specs = (P("tm", "space", None), P(None, "tm", "space"), P("tm", "space", None), P(), P())
    out_specs = (P("tm", "space", None), P("tm", "space", None))
    return jax.shard_map(
        per_device, mesh=mesh, in_specs=in_specs, out_specs=out_specs, check_vma=False
    )
```

```python
import functools
import math

import jax
import jax.numpy as jnp
from jax import lax
from jax.experimental import pallas as pl
from jax.experimental.pallas import tpu as pltpu
from jax.sharding import PartitionSpec as P

HD = 128
HEADS = 20
HW = HD * HEADS
TOK = 64
STEPS = 2
SHARD = 16
GROUPS = 4
PER = HEADS // GROUPS
GW = PER * HD
EPS = 1e-6
SCORE_SCALE = math.log2(math.e) / math.sqrt(HD)
MASKED = -1e30
MESH = pl.DeviceIdType.MESH
F32 = jnp.float32
BF16 = jnp.bfloat16

STAGE = 128
NEAR, FAR = 3, 4
TILES = 3 * STAGE
ROWS = TILES + STEPS * 2 * STAGE
CHIP = TOK
RING = 14
LAST = 15


def kernel(
    latent_hbm, cache_hbm, mask_hbm, gains_hbm, steps_hbm,
    denoised_ref, velocity_ref,
    mask_ref, gains_ref, steps_ref, buf, query, accum, peak, total, scale_own, scale_in, scale_col, bias, square,
    local_sem, ysend, ssend, yrecv, srecv, zsend, zrecv, rsend, rrecv,
):
    tm, space = lax.axis_index("tm"), lax.axis_index("space")
    n_tm, n_space = lax.axis_size("tm"), lax.axis_size("space")
    along_y = ((lax.rem(tm + 2, n_tm), space), (lax.rem(tm + n_tm - 2, n_tm), space))
    sibling = (tm + 1 - 2 * lax.rem(tm, 2), space)
    along_z = ((tm, lax.rem(space + 1, n_space)), (tm, lax.rem(space + n_space - 1, n_space)))
    has_low, has_high = space > 0, space < n_space - 1
    sends = ((has_high, has_low & has_high), (has_low, has_low & has_high))
    receives = ((has_low, space > 1), (has_high, space < n_space - 2))

    def remote(src, dst, send, recv, device):
        return pltpu.make_async_remote_copy(
            src_ref=src, dst_ref=dst, send_sem=send, recv_sem=recv, device_id=device, device_id_type=MESH
        )

    def half_cols(half):
        return pl.ds(half * (HW // 2), HW // 2)

    def shard(which, index, half=None):
        rows = CHIP + SHARD * index + (2 * SHARD if index >= 2 else 0)
        if half is None:
            return buf.at[which, pl.ds(rows, SHARD)]
        return buf.at[which, pl.ds(rows, SHARD), half_cols(half)]

    def slot(distance, direction):
        return 4 * distance - 2 + (0 if distance == 4 else 2 * direction)

    def ring_place(direction, number):
        return (number // 2 + direction) % 2, number % 2, number // 4 + 1

    def ring_copy(direction, number, own):
        which, half, distance = ring_place(direction, number)
        target = slot(distance, direction)
        if own:
            src = cache_hbm.at[which, :, half_cols(half)]
        else:
            src = shard(which, slot(distance - 1, direction) if distance > 1 else 0, half)
        return remote(
            src, shard(which, target, half), ysend.at[direction, number], yrecv.at[which, target, half],
            along_y[direction],
        )

    def sib_copy(which, target, half=None, own=False):
        if own:
            src, dst = cache_hbm.at[which], shard(which, target)
        else:
            src, dst = shard(which, target - 1, half), shard(which, target, half)
        sem = 0 if half is None else half
        return remote(src, dst, ssend.at[which, target, sem], srecv.at[which, target, sem], sibling)

    def ring_round(number):
        for direction in range(2):
            ring_copy(direction, number, False).wait_recv()
            if number + 4 < RING:
                ring_copy(direction, number + 4, False).start()
        for direction in range(2):
            which, half, distance = ring_place(direction, number)
            if distance == 4:
                sib_copy(which, LAST, half).start()
            elif half == 1:
                sib_copy(which, slot(distance, direction) + 1).start()

    def each_sibling(targets, act):
        for target in targets:
            for which in range(2):
                if target == LAST:
                    for half in range(2):
                        act(sib_copy(which, target, half))
                else:
                    act(sib_copy(which, target))

    def columns(group):
        return pl.ds(pl.multiple_of(group * GW, GW), GW)

    def head_cols(head):
        if isinstance(head, int):
            return pl.ds(head * HD, HD)
        return pl.ds(pl.multiple_of(head * HD, HD), HD)

    def tile_rows(phase, number):
        return pl.ds(pl.multiple_of(TILES + phase * 2 * STAGE + number * TOK, TOK), TOK)

    def tile_part(phase, number, cols):
        return buf.at[1, tile_rows(phase, number), cols]

    def tile_copy(phase, direction, hop, group):
        cols = columns(group)
        if hop == 1:
            src = tile_part(phase, direction, cols)
        elif isinstance(phase, int) and phase == 0:
            src = latent_hbm.at[0, :, cols]
        else:
            src = buf.at[1, pl.ds(0, TOK), cols]
        target = 2 * hop + direction
        return remote(
            src, tile_part(phase, target, cols), zsend.at[phase, direction, hop, group],
            zrecv.at[phase, target, group], along_z[direction],
        )

    def scale_copy(phase, direction, hop):
        src = scale_own.at[phase] if hop == 0 else scale_in.at[phase, direction]
        target = 2 * hop + direction
        return remote(
            src, scale_in.at[phase, target], rsend.at[phase, direction, hop], rrecv.at[phase, target], along_z[direction]
        )

    def start_tile(phase, hop, group):
        for direction in range(2):
            @pl.when(sends[direction][hop])
            def _():
                tile_copy(phase, direction, hop, group).start()

    def wait_tile(phase, hop, group):
        for direction in range(2):
            @pl.when(receives[direction][hop])
            def _():
                tile_copy(phase, direction, hop, group).wait_recv()

        if hop == 0:
            start_tile(phase, 1, group)

    diagonal = lax.broadcasted_iota(jnp.int32, (TOK, HD), 0) == lax.broadcasted_iota(jnp.int32, (TOK, HD), 1)

    def take_scales(phase, hop):
        for direction in range(2):
            target = 2 * hop + direction

            @pl.when(receives[direction][hop])
            def _():
                scale_copy(phase, direction, hop).wait_recv()

            if hop == 0:
                @pl.when(sends[direction][1])
                def _():
                    scale_copy(phase, direction, 1).start()

            row = jnp.broadcast_to(scale_in[phase, target, 0:1, :], (TOK, HD))
            col = jnp.sum(jnp.where(diagonal, row, 0.0), axis=1, keepdims=True)
            scale_col[pl.ds(target * TOK, TOK), :] = jnp.broadcast_to(col, (TOK, HD))

    def root_scale():
        mean = jnp.sum(square[...], axis=1, keepdims=True) * (1.0 / HW)
        return jnp.broadcast_to(lax.rsqrt(mean + EPS), (TOK, HD))

    def send_scale(phase, col):
        row = jnp.sum(jnp.where(diagonal, col, 0.0), axis=0, keepdims=True)
        scale_own[phase] = jnp.broadcast_to(row, (8, HD))
        for direction in range(2):
            @pl.when(sends[direction][0])
            def _():
                scale_copy(phase, direction, 0).start()

    def begin_heads(col):
        def body(group, _):
            heads = [group * PER + i for i in range(PER)]
            normals = [buf[1, pl.ds(0, TOK), head_cols(head)].astype(F32) * col for head in heads]
            for head, normal in zip(heads, normals):
                cols = head_cols(head)
                query[:, cols] = (normal * gains_ref[0:1, cols]).astype(BF16)
                buf[0, pl.ds(0, TOK), cols] = (normal * gains_ref[1:2, cols]).astype(BF16)
                peak[head] = jnp.full((TOK, HD), MASKED, F32)
                total[head] = jnp.zeros((TOK, HD), F32)
                accum[:, cols] = jnp.zeros((TOK, HD), F32)
            return 0

        lax.fori_loop(0, GROUPS, body, 0)

    def value_rows(stage, count, phase):
        start = (stage + phase * 2) * STAGE if stage >= NEAR else stage * STAGE
        return pl.ds(pl.multiple_of(start, STAGE), count * STAGE)

    def keys_of(head, stage, count, phase):
        cols = head_cols(head)
        rows = value_rows(stage, count, phase)
        if stage < NEAR:
            return buf[0, rows, cols]
        scales = scale_col[pl.ds((stage - NEAR) * STAGE, STAGE), :]
        return (buf[1, rows, cols].astype(F32) * scales * gains_ref[1:2, cols]).astype(BF16)

    def mix(plan, weights, phase):
        mixed = []
        at = 0
        while at < len(plan):
            head, spans = plan[at]
            pair = 2 if at + 1 < len(plan) and plan[at + 1] == (head + 1, spans) else 1
            cols = pl.ds(head * HD, pair * HD)
            sums = None
            for i, (stage, count) in enumerate(spans):
                stacked = jnp.concatenate([weights[at + j][i] for j in range(pair)], axis=0)
                product = jnp.dot(stacked, buf[1, value_rows(stage, count, phase), cols], preferred_element_type=F32)
                sums = product if sums is None else sums + product
            mixed += [sums[j * TOK : (j + 1) * TOK, j * HD : (j + 1) * HD] for j in range(pair)]
            at += pair
        return mixed

    def update(phase, *parts):
        plan = [(head, spans) for heads, spans in parts for head in heads]
        cols = [head_cols(head) for head, _ in plan]
        keys = [[keys_of(head, stage, count, phase) for stage, count in spans] for head, spans in plan]
        queries = [query[:, c] for c in cols]
        old_peaks = [peak[head] for head, _ in plan]
        scores = []
        for q, each, (_, spans) in zip(queries, keys, plan):
            pieces = []
            for k, (stage, count) in zip(each, spans):
                raw = lax.dot_general(q, k, (((1,), (1,)), ((), ())), preferred_element_type=F32)
                pieces.append([
                    raw[:, i * STAGE : (i + 1) * STAGE] * SCORE_SCALE + bias[stage + i, 0:1, :] for i in range(count)
                ])
            scores.append(pieces)
        tops = [functools.reduce(jnp.maximum, sum(pieces, [])) for pieces in scores]
        peaks = [
            jnp.maximum(old, jnp.broadcast_to(jnp.max(top, axis=1, keepdims=True), (TOK, HD)))
            for old, top in zip(old_peaks, tops)
        ]
        expos = [[[jnp.exp2(s - p) for s in span] for span in pieces] for pieces, p in zip(scores, peaks)]
        weights = [[jnp.concatenate([e.astype(BF16) for e in span], axis=1) for span in each] for each in expos]
        mixed = mix(plan, weights, phase)
        factors = [jnp.exp2(old - new) for old, new in zip(old_peaks, peaks)]
        totals = [
            total[head] * f + functools.reduce(jnp.add, sum(each, []))
            for (head, _), f, each in zip(plan, factors, expos)
        ]
        sums = [accum[:, c] * f + m for c, f, m in zip(cols, factors, mixed)]
        for i, (head, _) in enumerate(plan):
            peak[head] = peaks[i]
            total[head] = totals[i]
            accum[:, cols[i]] = sums[i]

    def finish(heads):
        attended = [accum[:, head_cols(head)] / jnp.sum(total[head], axis=1, keepdims=True) for head in heads]
        squares = square[...]
        for head, values in zip(heads, attended):
            accum[:, head_cols(head)] = values
            squares = squares + values * values
        square[...] = squares

    def tiles_left(phase, hop):
        for direction in range(2):
            @pl.when(sends[direction][hop])
            def _():
                scale_copy(phase, direction, hop).wait_send()

                def body(group, _):
                    tile_copy(phase, direction, hop, group).wait_send()
                    return 0

                lax.fori_loop(0, GROUPS, body, 0)

    def earlier_sends_left():
        for number in range(RING):
            for direction in range(2):
                ring_copy(direction, number, number < 4).wait_send()
        each_sibling(range(1, LAST + 1, 2), lambda copy: copy.wait_send())
        for hop in range(2):
            tiles_left(0, hop)

    loads = [
        pltpu.make_async_copy(latent_hbm.at[0], buf.at[1, pl.ds(0, TOK)], local_sem.at[0]),
        pltpu.make_async_copy(cache_hbm.at[0], buf.at[0, pl.ds(CHIP, SHARD)], local_sem.at[1]),
        pltpu.make_async_copy(cache_hbm.at[1], buf.at[1, pl.ds(CHIP, SHARD)], local_sem.at[2]),
        pltpu.make_async_copy(mask_hbm, mask_ref, local_sem.at[3]),
        pltpu.make_async_copy(gains_hbm, gains_ref, local_sem.at[4]),
        pltpu.make_async_copy(steps_hbm, steps_ref, local_sem.at[5]),
    ]
    barrier = pltpu.get_barrier_semaphore()
    for device in (*along_y, sibling):
        pl.semaphore_signal(barrier, inc=1, device_id=device, device_id_type=MESH)
    for direction in range(2):
        @pl.when(sends[direction][0])
        def _():
            pl.semaphore_signal(barrier, inc=1, device_id=along_z[direction], device_id_type=MESH)

    for load in loads:
        load.start()
    pl.semaphore_wait(barrier, 3 + lax.min(space, 1) + lax.min(n_space - 1 - space, 1))

    start_tile(0, 0, 0)
    for number in range(4):
        for direction in range(2):
            ring_copy(direction, number, True).start()
    for which in range(2):
        sib_copy(which, 1, own=True).start()

    for hop in range(2):
        for direction in range(2):
            @pl.when(jnp.logical_not(receives[direction][hop]))
            def _():
                for phase in range(STEPS):
                    buf[1, tile_rows(phase, 2 * hop + direction), :] = jnp.zeros((TOK, HW), BF16)
                    scale_in[phase, 2 * hop + direction] = jnp.zeros((8, HD), F32)

    for which in range(2):
        for stage in (0, 2):
            buf[which, pl.ds(stage * STAGE + 3 * STAGE // 4, STAGE // 4), :] = jnp.zeros((STAGE // 4, HW), BF16)

    for load in loads[3:]:
        load.wait()
    lane = lax.broadcasted_iota(jnp.int32, (8, HD), 1)
    for stage in (0, 2):
        bias[stage] = jnp.where(lane < 3 * STAGE // 4, 0.0, MASKED).astype(F32)
    bias[1] = jnp.zeros((8, HD), F32)
    for hop in range(2):
        low, high = (1, 2) if hop == 0 else (0, 3)
        low_ok = (mask_ref[0, 0, low] > 0) & (space - hop > 0)
        high_ok = (mask_ref[0, 0, high] > 0) & (space + hop + 1 < n_space)
        low_bias = jnp.where(low_ok, 0.0, MASKED).astype(F32)
        high_bias = jnp.where(high_ok, 0.0, MASKED).astype(F32)
        bias[NEAR + hop] = jnp.where(lane < TOK, low_bias, high_bias)

    loads[0].wait()
    square[...] = jnp.zeros((TOK, HD), F32)

    def add_squares(group, _):
        squares = square[...]
        for i in range(PER):
            values = buf[1, pl.ds(0, TOK), head_cols(group * PER + i)].astype(F32)
            squares = squares + values * values
        square[...] = squares
        return 0

    lax.fori_loop(0, GROUPS, add_squares, 0)
    col = root_scale()
    send_scale(0, col)
    for group in range(1, GROUPS):
        start_tile(0, 0, group)
    begin_heads(col)
    for load in loads[1:3]:
        load.wait()

    def phase_body(phase, _):
        first = phase == 0
        square[...] = jnp.zeros((TOK, HD), F32)

        def rounds(start, count):
            @pl.when(first)
            def _():
                for number in range(start, start + count):
                    ring_round(number)

        def last_shards(half):
            if half == 0:
                each_sibling((11, 13), lambda copy: copy.wait_recv())
            for which in range(2):
                sib_copy(which, LAST, half).wait_recv()

        every = range(HEADS)

        @pl.when(first)
        def _():
            each_sibling((1,), lambda copy: copy.wait_recv())

        @pl.when(first)
        def _():
            update(phase, (every, ((0, 1),)))

        @pl.when(jnp.logical_not(first))
        def _():
            update(phase, (every[: 2 * PER], ((0, 3),)))
            update(phase, (every[2 * PER :], ((0, 3),)))

        near, far = ((NEAR, 1),), ((FAR, 1),)
        for group in range(GROUPS):
            rounds(2 * group, 2)
            wait_tile(phase, 0, group)
            if group == 0:
                take_scales(phase, 0)
            update(phase, (every[group * PER : (group + 1) * PER], near))
        rounds(8, 2)

        @pl.when(first)
        def _():
            each_sibling((3, 5, 7, 9), lambda copy: copy.wait_recv())
            update(phase, (every, ((1, 1),)))

        @pl.when(jnp.logical_not(first))
        def _():
            earlier_sends_left()

        rounds(10, 2)
        wait_tile(phase, 1, 0)
        wait_tile(phase, 1, 1)
        take_scales(phase, 1)
        update(phase, (every[: 2 * PER], far))
        rounds(12, 2)
        wait_tile(phase, 1, 2)
        update(phase, (every[2 * PER : 3 * PER], far))

        @pl.when(first)
        def _():
            last_shards(0)
            update(phase, (every[: 2 * PER], ((2, 1),)))
            last_shards(1)
            wait_tile(phase, 1, 3)
            update(phase, (every[2 * PER : 3 * PER], ((2, 1),)), (every[3 * PER :], ((2, 1), (FAR, 1))))
            finish(every)

        @pl.when(jnp.logical_not(first))
        def _():
            finish(every[: 3 * PER])
            tiles_left(1, 0)
            wait_tile(phase, 1, 3)
            update(phase, (every[3 * PER :], far))
            finish(every[3 * PER :])

        @pl.when(first)
        def _():
            col = root_scale()
            step_size = steps_ref[0]
            square[...] = jnp.zeros((TOK, HD), F32)

            def move(group, _):
                squares = square[...]
                cols = [head_cols(group * PER + i) for i in range(PER)]
                moved = [
                    (buf[1, pl.ds(0, TOK), c].astype(F32) + step_size * (accum[:, c] * col)).astype(BF16)
                    for c in cols
                ]
                for c, values in zip(cols, moved):
                    buf[1, pl.ds(0, TOK), c] = values
                    wide = values.astype(F32)
                    squares = squares + wide * wide
                square[...] = squares

                @pl.when(group == 0)
                def _():
                    start_tile(1, 0, 0)

                return 0

            lax.fori_loop(0, GROUPS, move, 0)
            col = root_scale()
            send_scale(1, col)
            for group in range(1, GROUPS):
                start_tile(1, 0, group)
            begin_heads(col)

        return 0

    lax.fori_loop(0, STEPS, phase_body, 0)

    col = root_scale()
    last_size = steps_ref[STEPS - 1]

    cols = [head_cols(head) for head in range(HEADS)]
    velocities = [accum[:, c] * col for c in cols]
    moved = [buf[1, pl.ds(0, TOK), c].astype(F32) + last_size * v for c, v in zip(cols, velocities)]
    for c, velocity, denoised in zip(cols, velocities, moved):
        denoised_ref[0, :, c] = denoised.astype(BF16)
        velocity_ref[0, :, c] = velocity.astype(BF16)

    tiles_left(1, 1)


PIECE = 16
PIECES = TOK // PIECE


def hand_over(denoised_in, velocity_in, denoised_out, velocity_out, sems):
    copies = [
        pltpu.make_async_copy(source.at[0, pl.ds(PIECE * i, PIECE)], target.at[0, pl.ds(PIECE * i, PIECE)], sems.at[which, i])
        for i in range(PIECES)
        for which, (source, target) in enumerate(((denoised_in, denoised_out), (velocity_in, velocity_out)))
    ]
    for copy in copies:
        copy.start()
    for copy in copies:
        copy.wait()


def per_device(latent, past_cache, neighbour_mask, gains, step_sizes):
    dma = pltpu.SemaphoreType.DMA
    hbm = pl.BlockSpec(memory_space=pltpu.HBM)
    vmem = pl.BlockSpec(memory_space=pltpu.VMEM)
    operands = [
        pltpu.with_memory_space_constraint(x, pltpu.HBM)
        for x in (latent, past_cache, neighbour_mask, gains, step_sizes)
    ]
    results = pl.pallas_call(
        kernel,
        out_shape=(pltpu.VMEM((1, TOK, HW), BF16),) * 2,
        in_specs=[hbm] * 5,
        out_specs=(vmem,) * 2,
        scratch_shapes=[
            pltpu.SMEM((1, 1, 4), jnp.int32),
            pltpu.VMEM((2, HW), F32),
            pltpu.SMEM((STEPS,), F32),
            pltpu.VMEM((2, ROWS, HW), BF16),
            pltpu.VMEM((TOK, HW), BF16),
            pltpu.VMEM((TOK, HW), F32),
            pltpu.VMEM((HEADS, TOK, HD), F32),
            pltpu.VMEM((HEADS, TOK, HD), F32),
            pltpu.VMEM((STEPS, 8, HD), F32),
            pltpu.VMEM((STEPS, 4, 8, HD), F32),
            pltpu.VMEM((4 * TOK, HD), F32),
            pltpu.VMEM((5, 8, HD), F32),
            pltpu.VMEM((TOK, HD), F32),
            dma((6,)),
            dma((2, RING)),
            dma((2, 16, 2)),
            dma((2, 16, 2)),
            dma((2, 16, 2)),
            dma((STEPS, 2, 2, GROUPS)),
            dma((STEPS, 4, GROUPS)),
            dma((STEPS, 2, 2)),
            dma((STEPS, 4)),
        ],
        compiler_params=pltpu.CompilerParams(
            collective_id=0, has_side_effects=True, vmem_limit_bytes=32 * 1024 * 1024
        ),
        cost_estimate=pl.CostEstimate(flops=760_000_000, bytes_accessed=1_200_000, transcendentals=1_600_000),
    )(*operands)
    return pl.pallas_call(
        hand_over,
        out_shape=(jax.ShapeDtypeStruct((1, TOK, HW), BF16),) * 2,
        in_specs=[vmem] * 2,
        out_specs=(hbm,) * 2,
        scratch_shapes=[dma((2, PIECES))],
    )(*(pltpu.with_memory_space_constraint(x, pltpu.VMEM) for x in results))


def solution(mesh):
    in_specs = (P("tm", "space", None), P(None, "tm", "space"), P("tm", "space", None), P(), P())
    out_specs = (P("tm", "space", None), P("tm", "space", None))
    return jax.shard_map(
        per_device, mesh=mesh, in_specs=in_specs, out_specs=out_specs, check_vma=False
    )
```

```python
import functools
import math

import jax
import jax.numpy as jnp
from jax import lax
from jax.experimental import pallas as pl
from jax.experimental.pallas import tpu as pltpu
from jax.sharding import PartitionSpec as P

HD = 128
HEADS = 20
HW = HD * HEADS
TOK = 64
STEPS = 2
SHARD = 16
GROUPS = 4
PER = HEADS // GROUPS
GW = PER * HD
EPS = 1e-6
SCORE_SCALE = math.log2(math.e) / math.sqrt(HD)
MASKED = -1e30
MESH = pl.DeviceIdType.MESH
F32 = jnp.float32
BF16 = jnp.bfloat16

STAGE = 128
NEAR, FAR = 3, 4
TILES = 3 * STAGE
ROWS = TILES + STEPS * 2 * STAGE
CHIP = TOK
RING = 14


def kernel(
    latent_hbm, cache_hbm, mask_hbm, gains_hbm, steps_hbm,
    denoised_ref, velocity_ref,
    mask_ref, gains_ref, steps_ref, buf, query, accum, peak, total, scale_own, scale_in, scale_col, bias, square,
    local_sem, ysend, ssend, yrecv, zsend, zrecv, rsend, rrecv,
):
    tm, space = lax.axis_index("tm"), lax.axis_index("space")
    n_tm, n_space = lax.axis_size("tm"), lax.axis_size("space")
    along_y = ((lax.rem(tm + 2, n_tm), space), (lax.rem(tm + n_tm - 2, n_tm), space))
    sibling = (tm + 1 - 2 * lax.rem(tm, 2), space)
    along_z = ((tm, lax.rem(space + 1, n_space)), (tm, lax.rem(space + n_space - 1, n_space)))
    has_low, has_high = space > 0, space < n_space - 1
    sends = ((has_high, has_low & has_high), (has_low, has_low & has_high))
    receives = ((has_low, space > 1), (has_high, space < n_space - 2))

    def remote(src, dst, send, recv, device):
        return pltpu.make_async_remote_copy(
            src_ref=src, dst_ref=dst, send_sem=send, recv_sem=recv, device_id=device, device_id_type=MESH
        )

    def half_cols(half):
        return pl.ds(pl.multiple_of(half * (HW // 2), HW // 2), HW // 2)

    def shard(which, index, half):
        rows = CHIP + SHARD * index + jnp.where(index >= 2, 2 * SHARD, 0)
        return buf.at[which, pl.ds(pl.multiple_of(rows, SHARD), SHARD), half_cols(half)]

    def slot(distance, direction):
        return 4 * distance - 2 + jnp.where(distance == 4, 0, 2 * direction)

    def ring_place(direction, number):
        which = lax.rem(number // 2 + direction, 2)
        return which, lax.rem(number, 2), number // 4 + 1

    def ring_copy(direction, number, own):
        which, half, distance = ring_place(direction, number)
        target = slot(distance, direction)
        if own:
            src = cache_hbm.at[which, :, half_cols(half)]
        else:
            src = shard(which, slot(distance - 1, direction), half)
        return remote(
            src, shard(which, target, half), ysend.at[direction, number], yrecv.at[which, target, half],
            along_y[direction],
        )

    def sib_copy(which, half, target, own=False):
        src = cache_hbm.at[which, :, half_cols(half)] if own else shard(which, target - 1, half)
        return remote(
            src, shard(which, target, half), ssend.at[which, target, half], yrecv.at[which, target, half], sibling
        )

    def ring_round(number):
        for direction in range(2):
            which, half, distance = ring_place(direction, number)
            ring_copy(direction, number, False).wait_recv()

            @pl.when(number + 4 < RING)
            def _():
                ring_copy(direction, number + 4, False).start()

            sib_copy(which, half, slot(distance, direction) + 1).start()

    def each_sibling(first, count, act):
        def body(i, _):
            act(sib_copy(lax.rem(i, 2), lax.rem(i // 2, 2), first + 2 * (i // 4)))
            return 0

        lax.fori_loop(0, 4 * count, body, 0)

    def columns(group):
        return pl.ds(pl.multiple_of(group * GW, GW), GW)

    def head_cols(head):
        if isinstance(head, int):
            return pl.ds(head * HD, HD)
        return pl.ds(pl.multiple_of(head * HD, HD), HD)

    def tile_rows(phase, number):
        return pl.ds(pl.multiple_of(TILES + phase * 2 * STAGE + number * TOK, TOK), TOK)

    def tile_part(phase, number, cols):
        return buf.at[1, tile_rows(phase, number), cols]

    def tile_copy(phase, direction, hop, group):
        cols = columns(group)
        if hop == 1:
            src = tile_part(phase, direction, cols)
        elif isinstance(phase, int) and phase == 0:
            src = latent_hbm.at[0, :, cols]
        else:
            src = buf.at[1, pl.ds(0, TOK), cols]
        target = 2 * hop + direction
        return remote(
            src, tile_part(phase, target, cols), zsend.at[phase, direction, hop, group],
            zrecv.at[phase, target, group], along_z[direction],
        )

    def scale_copy(phase, direction, hop):
        src = scale_own.at[phase] if hop == 0 else scale_in.at[phase, direction]
        target = 2 * hop + direction
        return remote(
            src, scale_in.at[phase, target], rsend.at[phase, direction, hop], rrecv.at[phase, target], along_z[direction]
        )

    def start_tile(phase, hop, group):
        for direction in range(2):
            @pl.when(sends[direction][hop])
            def _():
                tile_copy(phase, direction, hop, group).start()

    def wait_tile(phase, hop, group):
        for direction in range(2):
            @pl.when(receives[direction][hop])
            def _():
                tile_copy(phase, direction, hop, group).wait_recv()

        if hop == 0:
            start_tile(phase, 1, group)

    diagonal = lax.broadcasted_iota(jnp.int32, (TOK, HD), 0) == lax.broadcasted_iota(jnp.int32, (TOK, HD), 1)

    def take_scales(phase, hop):
        for direction in range(2):
            target = 2 * hop + direction

            @pl.when(receives[direction][hop])
            def _():
                scale_copy(phase, direction, hop).wait_recv()

            if hop == 0:
                @pl.when(sends[direction][1])
                def _():
                    scale_copy(phase, direction, 1).start()

            row = jnp.broadcast_to(scale_in[phase, target, 0:1, :], (TOK, HD))
            col = jnp.sum(jnp.where(diagonal, row, 0.0), axis=1, keepdims=True)
            scale_col[pl.ds(target * TOK, TOK), :] = jnp.broadcast_to(col, (TOK, HD))

    def root_scale():
        mean = jnp.sum(square[...], axis=1, keepdims=True) * (1.0 / HW)
        return jnp.broadcast_to(lax.rsqrt(mean + EPS), (TOK, HD))

    def send_scale(phase, col):
        row = jnp.sum(jnp.where(diagonal, col, 0.0), axis=0, keepdims=True)
        scale_own[phase] = jnp.broadcast_to(row, (8, HD))
        for direction in range(2):
            @pl.when(sends[direction][0])
            def _():
                scale_copy(phase, direction, 0).start()

    def begin_heads(col):
        def body(group, _):
            heads = [group * PER + i for i in range(PER)]
            normals = [buf[1, pl.ds(0, TOK), head_cols(head)].astype(F32) * col for head in heads]
            for head, normal in zip(heads, normals):
                cols = head_cols(head)
                query[:, cols] = (normal * gains_ref[0:1, cols]).astype(BF16)
                buf[0, pl.ds(0, TOK), cols] = (normal * gains_ref[1:2, cols]).astype(BF16)
                peak[head] = jnp.full((TOK, HD), MASKED, F32)
                total[head] = jnp.zeros((TOK, HD), F32)
                accum[:, cols] = jnp.zeros((TOK, HD), F32)
            return 0

        lax.fori_loop(0, GROUPS, body, 0)

    def value_rows(stage, count, phase):
        start = (stage + phase * 2) * STAGE if stage >= NEAR else stage * STAGE
        return pl.ds(pl.multiple_of(start, STAGE), count * STAGE)

    def keys_of(head, stage, count, phase):
        cols = head_cols(head)
        rows = value_rows(stage, count, phase)
        if stage < NEAR:
            return buf[0, rows, cols]
        scales = scale_col[pl.ds((stage - NEAR) * STAGE, STAGE), :]
        return (buf[1, rows, cols].astype(F32) * scales * gains_ref[1:2, cols]).astype(BF16)

    def mix(plan, weights, phase):
        mixed = []
        at = 0
        while at < len(plan):
            head, spans = plan[at]
            pair = 2 if at + 1 < len(plan) and plan[at + 1] == (head + 1, spans) else 1
            cols = pl.ds(head * HD, pair * HD)
            sums = None
            for i, (stage, count) in enumerate(spans):
                stacked = jnp.concatenate([weights[at + j][i] for j in range(pair)], axis=0)
                product = jnp.dot(stacked, buf[1, value_rows(stage, count, phase), cols], preferred_element_type=F32)
                sums = product if sums is None else sums + product
            mixed += [sums[j * TOK : (j + 1) * TOK, j * HD : (j + 1) * HD] for j in range(pair)]
            at += pair
        return mixed

    def update(phase, *parts):
        plan = [(head, spans) for heads, spans in parts for head in heads]
        cols = [head_cols(head) for head, _ in plan]
        keys = [[keys_of(head, stage, count, phase) for stage, count in spans] for head, spans in plan]
        queries = [query[:, c] for c in cols]
        old_peaks = [peak[head] for head, _ in plan]
        scores = []
        for q, each, (_, spans) in zip(queries, keys, plan):
            pieces = []
            for k, (stage, count) in zip(each, spans):
                raw = lax.dot_general(q, k, (((1,), (1,)), ((), ())), preferred_element_type=F32)
                pieces.append([
                    raw[:, i * STAGE : (i + 1) * STAGE] * SCORE_SCALE + bias[stage + i, 0:1, :] for i in range(count)
                ])
            scores.append(pieces)
        tops = [functools.reduce(jnp.maximum, sum(pieces, [])) for pieces in scores]
        peaks = [
            jnp.maximum(old, jnp.broadcast_to(jnp.max(top, axis=1, keepdims=True), (TOK, HD)))
            for old, top in zip(old_peaks, tops)
        ]
        expos = [[[jnp.exp2(s - p) for s in span] for span in pieces] for pieces, p in zip(scores, peaks)]
        weights = [[jnp.concatenate([e.astype(BF16) for e in span], axis=1) for span in each] for each in expos]
        mixed = mix(plan, weights, phase)
        factors = [jnp.exp2(old - new) for old, new in zip(old_peaks, peaks)]
        totals = [
            total[head] * f + functools.reduce(jnp.add, sum(each, []))
            for (head, _), f, each in zip(plan, factors, expos)
        ]
        sums = [accum[:, c] * f + m for c, f, m in zip(cols, factors, mixed)]
        for i, (head, _) in enumerate(plan):
            peak[head] = peaks[i]
            total[head] = totals[i]
            accum[:, cols[i]] = sums[i]

    def tile_update(phase, hop, group):
        heads = [group * PER + i for i in range(PER)]
        cols = [head_cols(head) for head in heads]
        rows = pl.ds(pl.multiple_of((NEAR + hop + phase * 2) * STAGE, STAGE), STAGE)
        scales = scale_col[pl.ds(pl.multiple_of(hop * STAGE, STAGE), STAGE), :]
        allowed = bias[NEAR + hop, 0:1, :]
        old_peaks = [peak[head] for head in heads]
        values = [buf[1, rows, c] for c in cols]
        keys = [(v.astype(F32) * scales * gains_ref[1:2, c]).astype(BF16) for v, c in zip(values, cols)]
        scores = [
            lax.dot_general(query[:, c], k, (((1,), (1,)), ((), ())), preferred_element_type=F32) * SCORE_SCALE + allowed
            for c, k in zip(cols, keys)
        ]
        peaks = [
            jnp.maximum(old, jnp.broadcast_to(jnp.max(s, axis=1, keepdims=True), (TOK, HD)))
            for old, s in zip(old_peaks, scores)
        ]
        expos = [jnp.exp2(s - p) for s, p in zip(scores, peaks)]
        mixed = [jnp.dot(e.astype(BF16), v, preferred_element_type=F32) for e, v in zip(expos, values)]
        factors = [jnp.exp2(old - new) for old, new in zip(old_peaks, peaks)]
        totals = [total[head] * f + e for head, f, e in zip(heads, factors, expos)]
        sums = [accum[:, c] * f + m for c, f, m in zip(cols, factors, mixed)]
        for i, head in enumerate(heads):
            peak[head] = peaks[i]
            total[head] = totals[i]
            accum[:, cols[i]] = sums[i]

    def finish(heads):
        attended = [accum[:, head_cols(head)] / jnp.sum(total[head], axis=1, keepdims=True) for head in heads]
        squares = square[...]
        for head, values in zip(heads, attended):
            accum[:, head_cols(head)] = values
            squares = squares + values * values
        square[...] = squares

    def tiles_left(phase, hop):
        for direction in range(2):
            @pl.when(sends[direction][hop])
            def _():
                scale_copy(phase, direction, hop).wait_send()

                def body(group, _):
                    tile_copy(phase, direction, hop, group).wait_send()
                    return 0

                lax.fori_loop(0, GROUPS, body, 0)

    def earlier_sends_left():
        def ring_left(number, _):
            for direction in range(2):
                ring_copy(direction, number, False).wait_send()
            return 0

        for number in range(4):
            for direction in range(2):
                ring_copy(direction, number, True).wait_send()
        lax.fori_loop(4, RING, ring_left, 0)
        for which in range(2):
            for half in range(2):
                sib_copy(which, half, 1, True).wait_send()
        each_sibling(3, 7, lambda copy: copy.wait_send())
        for hop in range(2):
            tiles_left(0, hop)

    loads = [
        pltpu.make_async_copy(latent_hbm.at[0], buf.at[1, pl.ds(0, TOK)], local_sem.at[0]),
        pltpu.make_async_copy(cache_hbm.at[0], buf.at[0, pl.ds(CHIP, SHARD)], local_sem.at[1]),
        pltpu.make_async_copy(cache_hbm.at[1], buf.at[1, pl.ds(CHIP, SHARD)], local_sem.at[2]),
        pltpu.make_async_copy(mask_hbm, mask_ref, local_sem.at[3]),
        pltpu.make_async_copy(gains_hbm, gains_ref, local_sem.at[4]),
        pltpu.make_async_copy(steps_hbm, steps_ref, local_sem.at[5]),
    ]
    barrier = pltpu.get_barrier_semaphore()
    for device in (*along_y, sibling):
        pl.semaphore_signal(barrier, inc=1, device_id=device, device_id_type=MESH)
    for direction in range(2):
        @pl.when(sends[direction][0])
        def _():
            pl.semaphore_signal(barrier, inc=1, device_id=along_z[direction], device_id_type=MESH)

    for load in loads:
        load.start()
    pl.semaphore_wait(barrier, 3 + lax.min(space, 1) + lax.min(n_space - 1 - space, 1))

    start_tile(0, 0, 0)
    for number in range(4):
        for direction in range(2):
            ring_copy(direction, number, True).start()
    for which in range(2):
        for half in range(2):
            sib_copy(which, half, 1, True).start()

    for hop in range(2):
        for direction in range(2):
            @pl.when(jnp.logical_not(receives[direction][hop]))
            def _():
                for phase in range(STEPS):
                    buf[1, tile_rows(phase, 2 * hop + direction), :] = jnp.zeros((TOK, HW), BF16)
                    scale_in[phase, 2 * hop + direction] = jnp.zeros((8, HD), F32)

    for which in range(2):
        for stage in (0, 2):
            buf[which, pl.ds(stage * STAGE + 3 * STAGE // 4, STAGE // 4), :] = jnp.zeros((STAGE // 4, HW), BF16)

    for load in loads[3:]:
        load.wait()
    lane = lax.broadcasted_iota(jnp.int32, (8, HD), 1)
    for stage in (0, 2):
        bias[stage] = jnp.where(lane < 3 * STAGE // 4, 0.0, MASKED).astype(F32)
    bias[1] = jnp.zeros((8, HD), F32)
    for hop in range(2):
        low, high = (1, 2) if hop == 0 else (0, 3)
        low_ok = (mask_ref[0, 0, low] > 0) & (space - hop > 0)
        high_ok = (mask_ref[0, 0, high] > 0) & (space + hop + 1 < n_space)
        low_bias = jnp.where(low_ok, 0.0, MASKED).astype(F32)
        high_bias = jnp.where(high_ok, 0.0, MASKED).astype(F32)
        bias[NEAR + hop] = jnp.where(lane < TOK, low_bias, high_bias)

    loads[0].wait()
    square[...] = jnp.zeros((TOK, HD), F32)

    def add_squares(group, _):
        squares = square[...]
        for i in range(PER):
            values = buf[1, pl.ds(0, TOK), head_cols(group * PER + i)].astype(F32)
            squares = squares + values * values
        square[...] = squares
        return 0

    lax.fori_loop(0, GROUPS, add_squares, 0)
    col = root_scale()
    send_scale(0, col)
    for group in range(1, GROUPS):
        start_tile(0, 0, group)
    begin_heads(col)
    for load in loads[1:3]:
        load.wait()

    def phase_body(phase, _):
        first = phase == 0
        square[...] = jnp.zeros((TOK, HD), F32)

        def rounds(start, count):
            @pl.when(first)
            def _():
                for number in range(start, start + count):
                    ring_round(number)

        def last_shards(half):
            for target in (11, 13, 15):
                for which in range(2):
                    sib_copy(which, half, target).wait_recv()

        every = range(HEADS)

        @pl.when(first)
        def _():
            each_sibling(1, 1, lambda copy: copy.wait_recv())

        @pl.when(first)
        def _():
            update(phase, (every, ((0, 1),)))

        @pl.when(jnp.logical_not(first))
        def _():
            update(phase, (every[: 2 * PER], ((0, 3),)))
            update(phase, (every[2 * PER :], ((0, 3),)))

        def tile_part_step(number, _):
            hop, group = number // GROUPS, lax.rem(number, GROUPS)

            @pl.when(first & (number < 7))
            def _():
                ring_round(2 * number)
                ring_round(2 * number + 1)

            @pl.when(first & (number == GROUPS))
            def _():
                each_sibling(3, 4, lambda copy: copy.wait_recv())
                update(phase, (every, ((1, 1),)))

            @pl.when(jnp.logical_not(first) & (number == GROUPS))
            def _():
                earlier_sends_left()

            @pl.when(number == 2 * GROUPS - 1)
            def _():
                @pl.when(first)
                def _():
                    last_shards(0)
                    update(phase, (every[: 2 * PER], ((2, 1),)))
                    last_shards(1)
                    update(phase, (every[2 * PER :], ((2, 1),)))

                finish(every[: 3 * PER])

            @pl.when(hop == 0)
            def _():
                wait_tile(phase, 0, group)

            @pl.when(hop == 1)
            def _():
                wait_tile(phase, 1, group)

            @pl.when(number == 0)
            def _():
                take_scales(phase, 0)

            @pl.when(number == GROUPS)
            def _():
                take_scales(phase, 1)

            tile_update(phase, hop, group)
            return 0

        lax.fori_loop(0, 2 * GROUPS, tile_part_step, 0)
        finish(every[3 * PER :])

        @pl.when(first)
        def _():
            col = root_scale()
            step_size = steps_ref[0]
            square[...] = jnp.zeros((TOK, HD), F32)

            def move(group, _):
                squares = square[...]
                cols = [head_cols(group * PER + i) for i in range(PER)]
                moved = [
                    (buf[1, pl.ds(0, TOK), c].astype(F32) + step_size * (accum[:, c] * col)).astype(BF16)
                    for c in cols
                ]
                for c, values in zip(cols, moved):
                    buf[1, pl.ds(0, TOK), c] = values
                    wide = values.astype(F32)
                    squares = squares + wide * wide
                square[...] = squares

                @pl.when(group == 0)
                def _():
                    start_tile(1, 0, 0)

                return 0

            lax.fori_loop(0, GROUPS, move, 0)
            col = root_scale()
            send_scale(1, col)
            for group in range(1, GROUPS):
                start_tile(1, 0, group)
            begin_heads(col)

        return 0

    lax.fori_loop(0, STEPS, phase_body, 0)

    col = root_scale()
    last_size = steps_ref[STEPS - 1]

    cols = [head_cols(head) for head in range(HEADS)]
    velocities = [accum[:, c] * col for c in cols]
    moved = [buf[1, pl.ds(0, TOK), c].astype(F32) + last_size * v for c, v in zip(cols, velocities)]
    for c, velocity, denoised in zip(cols, velocities, moved):
        denoised_ref[0, :, c] = denoised.astype(BF16)
        velocity_ref[0, :, c] = velocity.astype(BF16)

    for hop in range(2):
        tiles_left(1, hop)


PIECE = 16
PIECES = TOK // PIECE


def hand_over(denoised_in, velocity_in, denoised_out, velocity_out, sems):
    copies = [
        pltpu.make_async_copy(source.at[0, pl.ds(PIECE * i, PIECE)], target.at[0, pl.ds(PIECE * i, PIECE)], sems.at[which, i])
        for i in range(PIECES)
        for which, (source, target) in enumerate(((denoised_in, denoised_out), (velocity_in, velocity_out)))
    ]
    for copy in copies:
        copy.start()
    for copy in copies:
        copy.wait()


def per_device(latent, past_cache, neighbour_mask, gains, step_sizes):
    dma = pltpu.SemaphoreType.DMA
    hbm = pl.BlockSpec(memory_space=pltpu.HBM)
    vmem = pl.BlockSpec(memory_space=pltpu.VMEM)
    operands = [
        pltpu.with_memory_space_constraint(x, pltpu.HBM)
        for x in (latent, past_cache, neighbour_mask, gains, step_sizes)
    ]
    results = pl.pallas_call(
        kernel,
        out_shape=(pltpu.VMEM((1, TOK, HW), BF16),) * 2,
        in_specs=[hbm] * 5,
        out_specs=(vmem,) * 2,
        scratch_shapes=[
            pltpu.SMEM((1, 1, 4), jnp.int32),
            pltpu.VMEM((2, HW), F32),
            pltpu.SMEM((STEPS,), F32),
            pltpu.VMEM((2, ROWS, HW), BF16),
            pltpu.VMEM((TOK, HW), BF16),
            pltpu.VMEM((TOK, HW), F32),
            pltpu.VMEM((HEADS, TOK, HD), F32),
            pltpu.VMEM((HEADS, TOK, HD), F32),
            pltpu.VMEM((STEPS, 8, HD), F32),
            pltpu.VMEM((STEPS, 4, 8, HD), F32),
            pltpu.VMEM((4 * TOK, HD), F32),
            pltpu.VMEM((5, 8, HD), F32),
            pltpu.VMEM((TOK, HD), F32),
            dma((6,)),
            dma((2, RING)),
            dma((2, 16, 2)),
            dma((2, 16, 2)),
            dma((STEPS, 2, 2, GROUPS)),
            dma((STEPS, 4, GROUPS)),
            dma((STEPS, 2, 2)),
            dma((STEPS, 4)),
        ],
        compiler_params=pltpu.CompilerParams(
            collective_id=0, has_side_effects=True, vmem_limit_bytes=32 * 1024 * 1024
        ),
        cost_estimate=pl.CostEstimate(flops=760_000_000, bytes_accessed=1_200_000, transcendentals=1_600_000),
    )(*operands)
    return pl.pallas_call(
        hand_over,
        out_shape=(jax.ShapeDtypeStruct((1, TOK, HW), BF16),) * 2,
        in_specs=[vmem] * 2,
        out_specs=(hbm,) * 2,
        scratch_shapes=[dma((2, PIECES))],
    )(*(pltpu.with_memory_space_constraint(x, pltpu.VMEM) for x in results))


def solution(mesh):
    in_specs = (P("tm", "space", None), P(None, "tm", "space"), P("tm", "space", None), P(), P())
    out_specs = (P("tm", "space", None), P("tm", "space", None))
    return jax.shard_map(
        per_device, mesh=mesh, in_specs=in_specs, out_specs=out_specs, check_vma=False
    )
```

```python
import functools
import math

import jax
import jax.numpy as jnp
from jax import lax
from jax.experimental import pallas as pl
from jax.experimental.pallas import tpu as pltpu
from jax.sharding import PartitionSpec as P

HD = 128
HEADS = 20
HW = HD * HEADS
TOK = 64
STEPS = 2
SHARD = 16
GROUPS = 5
PER = HEADS // GROUPS
GW = PER * HD
EPS = 1e-6
SCORE_SCALE = math.log2(math.e) / math.sqrt(HD)
MASKED = -1e30
MESH = pl.DeviceIdType.MESH
F32 = jnp.float32
BF16 = jnp.bfloat16

STAGE = 128
NEAR, FAR = 3, 4
TILES = 3 * STAGE
ROWS = TILES + STEPS * 2 * STAGE
CHIP = TOK
RING = 14


def kernel(
    latent_hbm, cache_hbm, mask_hbm, gains_hbm, steps_hbm,
    denoised_ref, velocity_ref,
    mask_ref, gains_ref, steps_ref, buf, query, accum, peak, total, scale_own, scale_in, scale_col, bias, square,
    local_sem, ysend, ssend, yrecv, zsend, zrecv, rsend, rrecv,
):
    tm, space = lax.axis_index("tm"), lax.axis_index("space")
    n_tm, n_space = lax.axis_size("tm"), lax.axis_size("space")
    along_y = ((lax.rem(tm + 2, n_tm), space), (lax.rem(tm + n_tm - 2, n_tm), space))
    sibling = (tm + 1 - 2 * lax.rem(tm, 2), space)
    along_z = ((tm, lax.rem(space + 1, n_space)), (tm, lax.rem(space + n_space - 1, n_space)))
    has_low, has_high = space > 0, space < n_space - 1
    sends = ((has_high, has_low & has_high), (has_low, has_low & has_high))
    receives = ((has_low, space > 1), (has_high, space < n_space - 2))

    def remote(src, dst, send, recv, device):
        return pltpu.make_async_remote_copy(
            src_ref=src, dst_ref=dst, send_sem=send, recv_sem=recv, device_id=device, device_id_type=MESH
        )

    def half_cols(half):
        return pl.ds(pl.multiple_of(half * (HW // 2), HW // 2), HW // 2)

    def shard(which, index, half):
        rows = CHIP + SHARD * index + jnp.where(index >= 2, 2 * SHARD, 0)
        return buf.at[which, pl.ds(pl.multiple_of(rows, SHARD), SHARD), half_cols(half)]

    def slot(distance, direction):
        return 4 * distance - 2 + jnp.where(distance == 4, 0, 2 * direction)

    def ring_place(direction, number):
        which = lax.rem(number // 2 + direction, 2)
        return which, lax.rem(number, 2), number // 4 + 1

    def ring_copy(direction, number, own):
        which, half, distance = ring_place(direction, number)
        target = slot(distance, direction)
        if own:
            src = cache_hbm.at[which, :, half_cols(half)]
        else:
            src = shard(which, slot(distance - 1, direction), half)
        return remote(
            src, shard(which, target, half), ysend.at[direction, number], yrecv.at[which, target, half],
            along_y[direction],
        )

    def sib_copy(which, half, target, own=False):
        src = cache_hbm.at[which, :, half_cols(half)] if own else shard(which, target - 1, half)
        return remote(
            src, shard(which, target, half), ssend.at[which, target, half], yrecv.at[which, target, half], sibling
        )

    def ring_round(number):
        for direction in range(2):
            which, half, distance = ring_place(direction, number)
            ring_copy(direction, number, False).wait_recv()

            @pl.when(number + 4 < RING)
            def _():
                ring_copy(direction, number + 4, False).start()

            sib_copy(which, half, slot(distance, direction) + 1).start()

    def each_sibling(first, count, act):
        def body(i, _):
            act(sib_copy(lax.rem(i, 2), lax.rem(i // 2, 2), first + 2 * (i // 4)))
            return 0

        lax.fori_loop(0, 4 * count, body, 0)

    def columns(group):
        return pl.ds(pl.multiple_of(group * GW, GW), GW)

    def head_cols(head):
        if isinstance(head, int):
            return pl.ds(head * HD, HD)
        return pl.ds(pl.multiple_of(head * HD, HD), HD)

    def tile_rows(phase, number):
        return pl.ds(pl.multiple_of(TILES + phase * 2 * STAGE + number * TOK, TOK), TOK)

    def tile_part(phase, number, cols):
        return buf.at[1, tile_rows(phase, number), cols]

    def tile_copy(phase, direction, hop, group):
        cols = columns(group)
        if hop == 1:
            src = tile_part(phase, direction, cols)
        elif isinstance(phase, int) and phase == 0:
            src = latent_hbm.at[0, :, cols]
        else:
            src = buf.at[1, pl.ds(0, TOK), cols]
        target = 2 * hop + direction
        return remote(
            src, tile_part(phase, target, cols), zsend.at[phase, direction, hop, group],
            zrecv.at[phase, target, group], along_z[direction],
        )

    def scale_copy(phase, direction, hop):
        src = scale_own.at[phase] if hop == 0 else scale_in.at[phase, direction]
        target = 2 * hop + direction
        return remote(
            src, scale_in.at[phase, target], rsend.at[phase, direction, hop], rrecv.at[phase, target], along_z[direction]
        )

    def start_tile(phase, hop, group):
        for direction in range(2):
            @pl.when(sends[direction][hop])
            def _():
                tile_copy(phase, direction, hop, group).start()

    def wait_tile(phase, hop, group):
        for direction in range(2):
            @pl.when(receives[direction][hop])
            def _():
                tile_copy(phase, direction, hop, group).wait_recv()

        if hop == 0:
            start_tile(phase, 1, group)

    diagonal = lax.broadcasted_iota(jnp.int32, (TOK, HD), 0) == lax.broadcasted_iota(jnp.int32, (TOK, HD), 1)

    def take_scales(phase, hop):
        for direction in range(2):
            target = 2 * hop + direction

            @pl.when(receives[direction][hop])
            def _():
                scale_copy(phase, direction, hop).wait_recv()

            if hop == 0:
                @pl.when(sends[direction][1])
                def _():
                    scale_copy(phase, direction, 1).start()

            row = jnp.broadcast_to(scale_in[phase, target, 0:1, :], (TOK, HD))
            col = jnp.sum(jnp.where(diagonal, row, 0.0), axis=1, keepdims=True)
            scale_col[pl.ds(target * TOK, TOK), :] = jnp.broadcast_to(col, (TOK, HD))

    def root_scale():
        mean = jnp.sum(square[...], axis=1, keepdims=True) * (1.0 / HW)
        return jnp.broadcast_to(lax.rsqrt(mean + EPS), (TOK, HD))

    def send_scale(phase, col):
        row = jnp.sum(jnp.where(diagonal, col, 0.0), axis=0, keepdims=True)
        scale_own[phase] = jnp.broadcast_to(row, (8, HD))
        for direction in range(2):
            @pl.when(sends[direction][0])
            def _():
                scale_copy(phase, direction, 0).start()

    def begin_heads(col):
        def body(group, _):
            heads = [group * PER + i for i in range(PER)]
            normals = [buf[1, pl.ds(0, TOK), head_cols(head)].astype(F32) * col for head in heads]
            for head, normal in zip(heads, normals):
                cols = head_cols(head)
                query[:, cols] = (normal * gains_ref[0:1, cols]).astype(BF16)
                buf[0, pl.ds(0, TOK), cols] = (normal * gains_ref[1:2, cols]).astype(BF16)
                peak[head] = jnp.full((TOK, HD), MASKED, F32)
                total[head] = jnp.zeros((TOK, HD), F32)
                accum[:, cols] = jnp.zeros((TOK, HD), F32)
            return 0

        lax.fori_loop(0, GROUPS, body, 0)

    def value_rows(stage, count, phase):
        start = (stage + phase * 2) * STAGE if stage >= NEAR else stage * STAGE
        return pl.ds(pl.multiple_of(start, STAGE), count * STAGE)

    def keys_of(head, stage, count, phase):
        cols = head_cols(head)
        rows = value_rows(stage, count, phase)
        if stage < NEAR:
            return buf[0, rows, cols]
        scales = scale_col[pl.ds((stage - NEAR) * STAGE, STAGE), :]
        return (buf[1, rows, cols].astype(F32) * scales * gains_ref[1:2, cols]).astype(BF16)

    def mix(plan, weights, phase):
        mixed = []
        at = 0
        while at < len(plan):
            head, spans = plan[at]
            pair = 2 if at + 1 < len(plan) and plan[at + 1] == (head + 1, spans) else 1
            cols = pl.ds(head * HD, pair * HD)
            sums = None
            for i, (stage, count) in enumerate(spans):
                stacked = jnp.concatenate([weights[at + j][i] for j in range(pair)], axis=0)
                product = jnp.dot(stacked, buf[1, value_rows(stage, count, phase), cols], preferred_element_type=F32)
                sums = product if sums is None else sums + product
            mixed += [sums[j * TOK : (j + 1) * TOK, j * HD : (j + 1) * HD] for j in range(pair)]
            at += pair
        return mixed

    def update(phase, *parts):
        plan = [(head, spans) for heads, spans in parts for head in heads]
        cols = [head_cols(head) for head, _ in plan]
        keys = [[keys_of(head, stage, count, phase) for stage, count in spans] for head, spans in plan]
        queries = [query[:, c] for c in cols]
        old_peaks = [peak[head] for head, _ in plan]
        scores = []
        for q, each, (_, spans) in zip(queries, keys, plan):
            pieces = []
            for k, (stage, count) in zip(each, spans):
                raw = lax.dot_general(q, k, (((1,), (1,)), ((), ())), preferred_element_type=F32)
                pieces.append([
                    raw[:, i * STAGE : (i + 1) * STAGE] * SCORE_SCALE + bias[stage + i, 0:1, :] for i in range(count)
                ])
            scores.append(pieces)
        tops = [functools.reduce(jnp.maximum, sum(pieces, [])) for pieces in scores]
        peaks = [
            jnp.maximum(old, jnp.broadcast_to(jnp.max(top, axis=1, keepdims=True), (TOK, HD)))
            for old, top in zip(old_peaks, tops)
        ]
        expos = [[[jnp.exp2(s - p) for s in span] for span in pieces] for pieces, p in zip(scores, peaks)]
        weights = [[jnp.concatenate([e.astype(BF16) for e in span], axis=1) for span in each] for each in expos]
        mixed = mix(plan, weights, phase)
        factors = [jnp.exp2(old - new) for old, new in zip(old_peaks, peaks)]
        totals = [
            total[head] * f + functools.reduce(jnp.add, sum(each, []))
            for (head, _), f, each in zip(plan, factors, expos)
        ]
        sums = [accum[:, c] * f + m for c, f, m in zip(cols, factors, mixed)]
        for i, (head, _) in enumerate(plan):
            peak[head] = peaks[i]
            total[head] = totals[i]
            accum[:, cols[i]] = sums[i]

    def finish(heads):
        attended = [accum[:, head_cols(head)] / jnp.sum(total[head], axis=1, keepdims=True) for head in heads]
        squares = square[...]
        for head, values in zip(heads, attended):
            accum[:, head_cols(head)] = values
            squares = squares + values * values
        square[...] = squares

    def tiles_left(phase, hop):
        for direction in range(2):
            @pl.when(sends[direction][hop])
            def _():
                scale_copy(phase, direction, hop).wait_send()

                def body(group, _):
                    tile_copy(phase, direction, hop, group).wait_send()
                    return 0

                lax.fori_loop(0, GROUPS, body, 0)

    def earlier_sends_left():
        def ring_left(number, _):
            for direction in range(2):
                ring_copy(direction, number, False).wait_send()
            return 0

        for number in range(4):
            for direction in range(2):
                ring_copy(direction, number, True).wait_send()
        lax.fori_loop(4, RING, ring_left, 0)
        for which in range(2):
            for half in range(2):
                sib_copy(which, half, 1, True).wait_send()
        each_sibling(3, 7, lambda copy: copy.wait_send())
        for hop in range(2):
            tiles_left(0, hop)

    loads = [
        pltpu.make_async_copy(latent_hbm.at[0], buf.at[1, pl.ds(0, TOK)], local_sem.at[0]),
        pltpu.make_async_copy(cache_hbm.at[0], buf.at[0, pl.ds(CHIP, SHARD)], local_sem.at[1]),
        pltpu.make_async_copy(cache_hbm.at[1], buf.at[1, pl.ds(CHIP, SHARD)], local_sem.at[2]),
        pltpu.make_async_copy(mask_hbm, mask_ref, local_sem.at[3]),
        pltpu.make_async_copy(gains_hbm, gains_ref, local_sem.at[4]),
        pltpu.make_async_copy(steps_hbm, steps_ref, local_sem.at[5]),
    ]
    barrier = pltpu.get_barrier_semaphore()
    for device in (*along_y, sibling):
        pl.semaphore_signal(barrier, inc=1, device_id=device, device_id_type=MESH)
    for direction in range(2):
        @pl.when(sends[direction][0])
        def _():
            pl.semaphore_signal(barrier, inc=1, device_id=along_z[direction], device_id_type=MESH)

    for load in loads:
        load.start()
    pl.semaphore_wait(barrier, 3 + lax.min(space, 1) + lax.min(n_space - 1 - space, 1))

    start_tile(0, 0, 0)
    for number in range(4):
        for direction in range(2):
            ring_copy(direction, number, True).start()
    for which in range(2):
        for half in range(2):
            sib_copy(which, half, 1, True).start()

    for hop in range(2):
        for direction in range(2):
            @pl.when(jnp.logical_not(receives[direction][hop]))
            def _():
                for phase in range(STEPS):
                    buf[1, tile_rows(phase, 2 * hop + direction), :] = jnp.zeros((TOK, HW), BF16)
                    scale_in[phase, 2 * hop + direction] = jnp.zeros((8, HD), F32)

    for which in range(2):
        for stage in (0, 2):
            buf[which, pl.ds(stage * STAGE + 3 * STAGE // 4, STAGE // 4), :] = jnp.zeros((STAGE // 4, HW), BF16)

    for load in loads[3:]:
        load.wait()
    lane = lax.broadcasted_iota(jnp.int32, (8, HD), 1)
    for stage in (0, 2):
        bias[stage] = jnp.where(lane < 3 * STAGE // 4, 0.0, MASKED).astype(F32)
    bias[1] = jnp.zeros((8, HD), F32)
    for hop in range(2):
        low, high = (1, 2) if hop == 0 else (0, 3)
        low_ok = (mask_ref[0, 0, low] > 0) & (space - hop > 0)
        high_ok = (mask_ref[0, 0, high] > 0) & (space + hop + 1 < n_space)
        low_bias = jnp.where(low_ok, 0.0, MASKED).astype(F32)
        high_bias = jnp.where(high_ok, 0.0, MASKED).astype(F32)
        bias[NEAR + hop] = jnp.where(lane < TOK, low_bias, high_bias)

    loads[0].wait()
    square[...] = jnp.zeros((TOK, HD), F32)

    def add_squares(group, _):
        squares = square[...]
        for i in range(PER):
            values = buf[1, pl.ds(0, TOK), head_cols(group * PER + i)].astype(F32)
            squares = squares + values * values
        square[...] = squares
        return 0

    lax.fori_loop(0, GROUPS, add_squares, 0)
    col = root_scale()
    send_scale(0, col)
    for group in range(1, GROUPS):
        start_tile(0, 0, group)
    begin_heads(col)
    for load in loads[1:3]:
        load.wait()

    def phase_body(phase, _):
        first = phase == 0
        square[...] = jnp.zeros((TOK, HD), F32)

        def rounds(start, count):
            @pl.when(first)
            def _():
                for number in range(start, start + count):
                    ring_round(number)

        def last_shards(half):
            for target in (11, 13, 15):
                for which in range(2):
                    sib_copy(which, half, target).wait_recv()

        every = range(HEADS)

        @pl.when(first)
        def _():
            each_sibling(1, 1, lambda copy: copy.wait_recv())

        @pl.when(first)
        def _():
            update(phase, (every, ((0, 1),)))

        @pl.when(jnp.logical_not(first))
        def _():
            update(phase, (every[: HEADS // 2], ((0, 3),)))
            update(phase, (every[HEADS // 2 :], ((0, 3),)))

        near, far = ((NEAR, 1),), ((FAR, 1),)
        for group in range(GROUPS):
            rounds(2 * group, 2)
            wait_tile(phase, 0, group)
            if group == 0:
                take_scales(phase, 0)
            update(phase, (every[group * PER : (group + 1) * PER], near))

        @pl.when(first)
        def _():
            each_sibling(3, 4, lambda copy: copy.wait_recv())
            update(phase, (every, ((1, 1),)))

        @pl.when(jnp.logical_not(first))
        def _():
            earlier_sends_left()

        rounds(10, 2)
        wait_tile(phase, 1, 0)
        wait_tile(phase, 1, 1)
        take_scales(phase, 1)
        update(phase, (every[: 2 * PER], far))
        rounds(12, 2)
        wait_tile(phase, 1, 2)
        wait_tile(phase, 1, 3)
        update(phase, (every[2 * PER : 4 * PER], far))

        @pl.when(first)
        def _():
            last_shards(0)
            update(phase, (every[: HEADS // 2], ((2, 1),)))
            last_shards(1)
            wait_tile(phase, 1, 4)
            update(phase, (every[HEADS // 2 : 4 * PER], ((2, 1),)), (every[4 * PER :], ((2, 1), (FAR, 1))))
            finish(every)

        @pl.when(jnp.logical_not(first))
        def _():
            finish(every[: 4 * PER])
            wait_tile(phase, 1, 4)
            update(phase, (every[4 * PER :], far))
            finish(every[4 * PER :])

        @pl.when(first)
        def _():
            col = root_scale()
            step_size = steps_ref[0]
            square[...] = jnp.zeros((TOK, HD), F32)

            def move(group, _):
                squares = square[...]
                cols = [head_cols(group * PER + i) for i in range(PER)]
                moved = [
                    (buf[1, pl.ds(0, TOK), c].astype(F32) + step_size * (accum[:, c] * col)).astype(BF16)
                    for c in cols
                ]
                for c, values in zip(cols, moved):
                    buf[1, pl.ds(0, TOK), c] = values
                    wide = values.astype(F32)
                    squares = squares + wide * wide
                square[...] = squares

                @pl.when(group == 0)
                def _():
                    start_tile(1, 0, 0)

                return 0

            lax.fori_loop(0, GROUPS, move, 0)
            col = root_scale()
            send_scale(1, col)
            for group in range(1, GROUPS):
                start_tile(1, 0, group)
            begin_heads(col)

        return 0

    lax.fori_loop(0, STEPS, phase_body, 0)

    col = root_scale()
    last_size = steps_ref[STEPS - 1]

    cols = [head_cols(head) for head in range(HEADS)]
    velocities = [accum[:, c] * col for c in cols]
    moved = [buf[1, pl.ds(0, TOK), c].astype(F32) + last_size * v for c, v in zip(cols, velocities)]
    for c, velocity, denoised in zip(cols, velocities, moved):
        denoised_ref[0, :, c] = denoised.astype(BF16)
        velocity_ref[0, :, c] = velocity.astype(BF16)

    for hop in range(2):
        tiles_left(1, hop)


PIECE = 16
PIECES = TOK // PIECE


def hand_over(denoised_in, velocity_in, denoised_out, velocity_out, sems):
    copies = [
        pltpu.make_async_copy(source.at[0, pl.ds(PIECE * i, PIECE)], target.at[0, pl.ds(PIECE * i, PIECE)], sems.at[which, i])
        for i in range(PIECES)
        for which, (source, target) in enumerate(((denoised_in, denoised_out), (velocity_in, velocity_out)))
    ]
    for copy in copies:
        copy.start()
    for copy in copies:
        copy.wait()


def per_device(latent, past_cache, neighbour_mask, gains, step_sizes):
    dma = pltpu.SemaphoreType.DMA
    hbm = pl.BlockSpec(memory_space=pltpu.HBM)
    vmem = pl.BlockSpec(memory_space=pltpu.VMEM)
    operands = [
        pltpu.with_memory_space_constraint(x, pltpu.HBM)
        for x in (latent, past_cache, neighbour_mask, gains, step_sizes)
    ]
    results = pl.pallas_call(
        kernel,
        out_shape=(pltpu.VMEM((1, TOK, HW), BF16),) * 2,
        in_specs=[hbm] * 5,
        out_specs=(vmem,) * 2,
        scratch_shapes=[
            pltpu.SMEM((1, 1, 4), jnp.int32),
            pltpu.VMEM((2, HW), F32),
            pltpu.SMEM((STEPS,), F32),
            pltpu.VMEM((2, ROWS, HW), BF16),
            pltpu.VMEM((TOK, HW), BF16),
            pltpu.VMEM((TOK, HW), F32),
            pltpu.VMEM((HEADS, TOK, HD), F32),
            pltpu.VMEM((HEADS, TOK, HD), F32),
            pltpu.VMEM((STEPS, 8, HD), F32),
            pltpu.VMEM((STEPS, 4, 8, HD), F32),
            pltpu.VMEM((4 * TOK, HD), F32),
            pltpu.VMEM((5, 8, HD), F32),
            pltpu.VMEM((TOK, HD), F32),
            dma((6,)),
            dma((2, RING)),
            dma((2, 16, 2)),
            dma((2, 16, 2)),
            dma((STEPS, 2, 2, GROUPS)),
            dma((STEPS, 4, GROUPS)),
            dma((STEPS, 2, 2)),
            dma((STEPS, 4)),
        ],
        compiler_params=pltpu.CompilerParams(
            collective_id=0, has_side_effects=True, vmem_limit_bytes=32 * 1024 * 1024
        ),
        cost_estimate=pl.CostEstimate(flops=760_000_000, bytes_accessed=1_200_000, transcendentals=1_600_000),
    )(*operands)
    return pl.pallas_call(
        hand_over,
        out_shape=(jax.ShapeDtypeStruct((1, TOK, HW), BF16),) * 2,
        in_specs=[vmem] * 2,
        out_specs=(hbm,) * 2,
        scratch_shapes=[dma((2, PIECES))],
    )(*(pltpu.with_memory_space_constraint(x, pltpu.VMEM) for x in results))


def solution(mesh):
    in_specs = (P("tm", "space", None), P(None, "tm", "space"), P("tm", "space", None), P(), P())
    out_specs = (P("tm", "space", None), P("tm", "space", None))
    return jax.shard_map(
        per_device, mesh=mesh, in_specs=in_specs, out_specs=out_specs, check_vma=False
    )
```

```python
import functools
import math

import jax
import jax.numpy as jnp
from jax import lax
from jax.experimental import pallas as pl
from jax.experimental.pallas import tpu as pltpu
from jax.sharding import PartitionSpec as P

HD = 128
HEADS = 20
HW = HD * HEADS
TOK = 64
STEPS = 2
SHARD = 16
GROUPS = 5
PER = HEADS // GROUPS
GW = PER * HD
EPS = 1e-6
SCORE_SCALE = math.log2(math.e) / math.sqrt(HD)
MASKED = -1e30
MESH = pl.DeviceIdType.MESH
F32 = jnp.float32
BF16 = jnp.bfloat16

STAGE = 128
NEAR, FAR = 3, 4
TILES = 3 * STAGE
ROWS = TILES + STEPS * 2 * STAGE
CHIP = TOK
RING = 14


def kernel(
    latent_hbm, cache_hbm, mask_hbm, gains_hbm, steps_hbm,
    denoised_ref, velocity_ref,
    mask_ref, gains_ref, steps_ref, buf, query, accum, peak, total, scale_own, scale_in, scale_col, bias, square,
    local_sem, ysend, ssend, yrecv, zsend, zrecv, rsend, rrecv,
):
    tm, space = lax.axis_index("tm"), lax.axis_index("space")
    n_tm, n_space = lax.axis_size("tm"), lax.axis_size("space")
    along_y = ((lax.rem(tm + 2, n_tm), space), (lax.rem(tm + n_tm - 2, n_tm), space))
    sibling = (tm + 1 - 2 * lax.rem(tm, 2), space)
    along_z = ((tm, lax.rem(space + 1, n_space)), (tm, lax.rem(space + n_space - 1, n_space)))
    has_low, has_high = space > 0, space < n_space - 1
    sends = ((has_high, has_low & has_high), (has_low, has_low & has_high))
    receives = ((has_low, space > 1), (has_high, space < n_space - 2))

    def remote(src, dst, send, recv, device):
        return pltpu.make_async_remote_copy(
            src_ref=src, dst_ref=dst, send_sem=send, recv_sem=recv, device_id=device, device_id_type=MESH
        )

    def half_cols(half):
        return pl.ds(pl.multiple_of(half * (HW // 2), HW // 2), HW // 2)

    def shard(which, index, half):
        rows = CHIP + SHARD * index + jnp.where(index >= 2, 2 * SHARD, 0)
        return buf.at[which, pl.ds(pl.multiple_of(rows, SHARD), SHARD), half_cols(half)]

    def slot(distance, direction):
        return 4 * distance - 2 + jnp.where(distance == 4, 0, 2 * direction)

    def ring_place(direction, number):
        which = lax.rem(number // 2 + direction, 2)
        return which, lax.rem(number, 2), number // 4 + 1

    def ring_copy(direction, number, own):
        which, half, distance = ring_place(direction, number)
        target = slot(distance, direction)
        if own:
            src = cache_hbm.at[which, :, half_cols(half)]
        else:
            src = shard(which, slot(distance - 1, direction), half)
        return remote(
            src, shard(which, target, half), ysend.at[direction, number], yrecv.at[which, target, half],
            along_y[direction],
        )

    def sib_copy(which, half, target, own=False):
        src = cache_hbm.at[which, :, half_cols(half)] if own else shard(which, target - 1, half)
        return remote(
            src, shard(which, target, half), ssend.at[which, target, half], yrecv.at[which, target, half], sibling
        )

    def ring_round(number):
        for direction in range(2):
            which, half, distance = ring_place(direction, number)
            ring_copy(direction, number, False).wait_recv()

            @pl.when(number + 4 < RING)
            def _():
                ring_copy(direction, number + 4, False).start()

            sib_copy(which, half, slot(distance, direction) + 1).start()

    def each_sibling(first, count, act):
        def body(i, _):
            act(sib_copy(lax.rem(i, 2), lax.rem(i // 2, 2), first + 2 * (i // 4)))
            return 0

        lax.fori_loop(0, 4 * count, body, 0)

    def columns(group):
        return pl.ds(pl.multiple_of(group * GW, GW), GW)

    def head_cols(head):
        if isinstance(head, int):
            return pl.ds(head * HD, HD)
        return pl.ds(pl.multiple_of(head * HD, HD), HD)

    def tile_rows(phase, number):
        return pl.ds(pl.multiple_of(TILES + phase * 2 * STAGE + number * TOK, TOK), TOK)

    def tile_part(phase, number, cols):
        return buf.at[1, tile_rows(phase, number), cols]

    def tile_copy(phase, direction, hop, group):
        cols = columns(group)
        if hop == 1:
            src = tile_part(phase, direction, cols)
        elif isinstance(phase, int) and phase == 0:
            src = latent_hbm.at[0, :, cols]
        else:
            src = buf.at[1, pl.ds(0, TOK), cols]
        target = 2 * hop + direction
        return remote(
            src, tile_part(phase, target, cols), zsend.at[phase, direction, hop, group],
            zrecv.at[phase, target, group], along_z[direction],
        )

    def scale_copy(phase, direction, hop):
        src = scale_own.at[phase] if hop == 0 else scale_in.at[phase, direction]
        target = 2 * hop + direction
        return remote(
            src, scale_in.at[phase, target], rsend.at[phase, direction, hop], rrecv.at[phase, target], along_z[direction]
        )

    def start_tile(phase, hop, group):
        for direction in range(2):
            @pl.when(sends[direction][hop])
            def _():
                tile_copy(phase, direction, hop, group).start()

    def wait_tile(phase, hop, group):
        for direction in range(2):
            @pl.when(receives[direction][hop])
            def _():
                tile_copy(phase, direction, hop, group).wait_recv()

        if hop == 0:
            start_tile(phase, 1, group)

    diagonal = lax.broadcasted_iota(jnp.int32, (TOK, HD), 0) == lax.broadcasted_iota(jnp.int32, (TOK, HD), 1)

    def take_scales(phase, hop):
        for direction in range(2):
            target = 2 * hop + direction

            @pl.when(receives[direction][hop])
            def _():
                scale_copy(phase, direction, hop).wait_recv()

            if hop == 0:
                @pl.when(sends[direction][1])
                def _():
                    scale_copy(phase, direction, 1).start()

            row = jnp.broadcast_to(scale_in[phase, target, 0:1, :], (TOK, HD))
            col = jnp.sum(jnp.where(diagonal, row, 0.0), axis=1, keepdims=True)
            scale_col[pl.ds(target * TOK, TOK), :] = jnp.broadcast_to(col, (TOK, HD))

    def root_scale():
        mean = jnp.sum(square[...], axis=1, keepdims=True) * (1.0 / HW)
        return jnp.broadcast_to(lax.rsqrt(mean + EPS), (TOK, HD))

    def send_scale(phase, col):
        row = jnp.sum(jnp.where(diagonal, col, 0.0), axis=0, keepdims=True)
        scale_own[phase] = jnp.broadcast_to(row, (8, HD))
        for direction in range(2):
            @pl.when(sends[direction][0])
            def _():
                scale_copy(phase, direction, 0).start()

    def begin_heads(col):
        def body(group, _):
            heads = [group * PER + i for i in range(PER)]
            normals = [buf[1, pl.ds(0, TOK), head_cols(head)].astype(F32) * col for head in heads]
            for head, normal in zip(heads, normals):
                cols = head_cols(head)
                query[:, cols] = (normal * gains_ref[0:1, cols]).astype(BF16)
                buf[0, pl.ds(0, TOK), cols] = (normal * gains_ref[1:2, cols]).astype(BF16)
                peak[head] = jnp.full((TOK, HD), MASKED, F32)
                total[head] = jnp.zeros((TOK, HD), F32)
                accum[:, cols] = jnp.zeros((TOK, HD), F32)
            return 0

        lax.fori_loop(0, GROUPS, body, 0)

    def value_rows(stage, count, phase):
        start = (stage + phase * 2) * STAGE if stage >= NEAR else stage * STAGE
        return pl.ds(pl.multiple_of(start, STAGE), count * STAGE)

    def keys_of(head, stage, count, phase):
        cols = head_cols(head)
        rows = value_rows(stage, count, phase)
        if stage < NEAR:
            return buf[0, rows, cols]
        scales = scale_col[pl.ds((stage - NEAR) * STAGE, STAGE), :]
        return (buf[1, rows, cols].astype(F32) * scales * gains_ref[1:2, cols]).astype(BF16)

    def mix(plan, weights, phase):
        mixed = []
        at = 0
        while at < len(plan):
            head, spans = plan[at]
            pair = 2 if at + 1 < len(plan) and plan[at + 1] == (head + 1, spans) else 1
            cols = pl.ds(head * HD, pair * HD)
            sums = None
            for i, (stage, count) in enumerate(spans):
                stacked = jnp.concatenate([weights[at + j][i] for j in range(pair)], axis=0)
                product = jnp.dot(stacked, buf[1, value_rows(stage, count, phase), cols], preferred_element_type=F32)
                sums = product if sums is None else sums + product
            mixed += [sums[j * TOK : (j + 1) * TOK, j * HD : (j + 1) * HD] for j in range(pair)]
            at += pair
        return mixed

    def update(phase, *parts):
        plan = [(head, spans) for heads, spans in parts for head in heads]
        cols = [head_cols(head) for head, _ in plan]
        keys = [[keys_of(head, stage, count, phase) for stage, count in spans] for head, spans in plan]
        queries = [query[:, c] for c in cols]
        old_peaks = [peak[head] for head, _ in plan]
        scores = []
        for q, each, (_, spans) in zip(queries, keys, plan):
            pieces = []
            for k, (stage, count) in zip(each, spans):
                raw = lax.dot_general(q, k, (((1,), (1,)), ((), ())), preferred_element_type=F32)
                pieces.append([
                    raw[:, i * STAGE : (i + 1) * STAGE] * SCORE_SCALE + bias[stage + i, 0:1, :] for i in range(count)
                ])
            scores.append(pieces)
        tops = [functools.reduce(jnp.maximum, sum(pieces, [])) for pieces in scores]
        peaks = [
            jnp.maximum(old, jnp.broadcast_to(jnp.max(top, axis=1, keepdims=True), (TOK, HD)))
            for old, top in zip(old_peaks, tops)
        ]
        expos = [[[jnp.exp2(s - p) for s in span] for span in pieces] for pieces, p in zip(scores, peaks)]
        weights = [[jnp.concatenate([e.astype(BF16) for e in span], axis=1) for span in each] for each in expos]
        mixed = mix(plan, weights, phase)
        factors = [jnp.exp2(old - new) for old, new in zip(old_peaks, peaks)]
        totals = [
            total[head] * f + functools.reduce(jnp.add, sum(each, []))
            for (head, _), f, each in zip(plan, factors, expos)
        ]
        sums = [accum[:, c] * f + m for c, f, m in zip(cols, factors, mixed)]
        for i, (head, _) in enumerate(plan):
            peak[head] = peaks[i]
            total[head] = totals[i]
            accum[:, cols[i]] = sums[i]

    def finish(heads):
        attended = [accum[:, head_cols(head)] / jnp.sum(total[head], axis=1, keepdims=True) for head in heads]
        squares = square[...]
        for head, values in zip(heads, attended):
            accum[:, head_cols(head)] = values
            squares = squares + values * values
        square[...] = squares

    def tiles_left(phase, hop):
        for direction in range(2):
            @pl.when(sends[direction][hop])
            def _():
                scale_copy(phase, direction, hop).wait_send()

                def body(group, _):
                    tile_copy(phase, direction, hop, group).wait_send()
                    return 0

                lax.fori_loop(0, GROUPS, body, 0)

    def earlier_sends_left():
        def ring_left(number, _):
            for direction in range(2):
                ring_copy(direction, number, False).wait_send()
            return 0

        for number in range(4):
            for direction in range(2):
                ring_copy(direction, number, True).wait_send()
        lax.fori_loop(4, RING, ring_left, 0)
        for which in range(2):
            for half in range(2):
                sib_copy(which, half, 1, True).wait_send()
        each_sibling(3, 7, lambda copy: copy.wait_send())
        for hop in range(2):
            tiles_left(0, hop)

    loads = [
        pltpu.make_async_copy(latent_hbm.at[0], buf.at[1, pl.ds(0, TOK)], local_sem.at[0]),
        pltpu.make_async_copy(cache_hbm.at[0], buf.at[0, pl.ds(CHIP, SHARD)], local_sem.at[1]),
        pltpu.make_async_copy(cache_hbm.at[1], buf.at[1, pl.ds(CHIP, SHARD)], local_sem.at[2]),
        pltpu.make_async_copy(mask_hbm, mask_ref, local_sem.at[3]),
        pltpu.make_async_copy(gains_hbm, gains_ref, local_sem.at[4]),
        pltpu.make_async_copy(steps_hbm, steps_ref, local_sem.at[5]),
    ]
    barrier = pltpu.get_barrier_semaphore()
    for device in (*along_y, sibling):
        pl.semaphore_signal(barrier, inc=1, device_id=device, device_id_type=MESH)
    for direction in range(2):
        @pl.when(sends[direction][0])
        def _():
            pl.semaphore_signal(barrier, inc=1, device_id=along_z[direction], device_id_type=MESH)

    for load in loads:
        load.start()
    pl.semaphore_wait(barrier, 3 + lax.min(space, 1) + lax.min(n_space - 1 - space, 1))

    for part in range(2):
        start_tile(0, 0, part)
        for number in range(2 * part, 2 * part + 2):
            for direction in range(2):
                ring_copy(direction, number, True).start()
    for which in range(2):
        for half in range(2):
            sib_copy(which, half, 1, True).start()

    for hop in range(2):
        for direction in range(2):
            @pl.when(jnp.logical_not(receives[direction][hop]))
            def _():
                for phase in range(STEPS):
                    buf[1, tile_rows(phase, 2 * hop + direction), :] = jnp.zeros((TOK, HW), BF16)
                    scale_in[phase, 2 * hop + direction] = jnp.zeros((8, HD), F32)

    for which in range(2):
        for stage in (0, 2):
            buf[which, pl.ds(stage * STAGE + 3 * STAGE // 4, STAGE // 4), :] = jnp.zeros((STAGE // 4, HW), BF16)

    for load in loads[3:]:
        load.wait()
    lane = lax.broadcasted_iota(jnp.int32, (8, HD), 1)
    for stage in (0, 2):
        bias[stage] = jnp.where(lane < 3 * STAGE // 4, 0.0, MASKED).astype(F32)
    bias[1] = jnp.zeros((8, HD), F32)
    for hop in range(2):
        low, high = (1, 2) if hop == 0 else (0, 3)
        low_ok = (mask_ref[0, 0, low] > 0) & (space - hop > 0)
        high_ok = (mask_ref[0, 0, high] > 0) & (space + hop + 1 < n_space)
        low_bias = jnp.where(low_ok, 0.0, MASKED).astype(F32)
        high_bias = jnp.where(high_ok, 0.0, MASKED).astype(F32)
        bias[NEAR + hop] = jnp.where(lane < TOK, low_bias, high_bias)

    loads[0].wait()
    square[...] = jnp.zeros((TOK, HD), F32)

    def add_squares(group, _):
        squares = square[...]
        for i in range(PER):
            values = buf[1, pl.ds(0, TOK), head_cols(group * PER + i)].astype(F32)
            squares = squares + values * values
        square[...] = squares
        return 0

    lax.fori_loop(0, GROUPS, add_squares, 0)
    col = root_scale()
    send_scale(0, col)
    for group in range(2, GROUPS):
        start_tile(0, 0, group)
    begin_heads(col)
    for load in loads[1:3]:
        load.wait()

    def phase_body(phase, _):
        first = phase == 0
        square[...] = jnp.zeros((TOK, HD), F32)

        def rounds(start, count):
            @pl.when(first)
            def _():
                for number in range(start, start + count):
                    ring_round(number)

        def last_shards(half):
            for target in (11, 13, 15):
                for which in range(2):
                    sib_copy(which, half, target).wait_recv()

        every = range(HEADS)

        @pl.when(first)
        def _():
            each_sibling(1, 1, lambda copy: copy.wait_recv())

        @pl.when(first)
        def _():
            update(phase, (every, ((0, 1),)))

        @pl.when(jnp.logical_not(first))
        def _():
            update(phase, (every[: HEADS // 2], ((0, 3),)))
            update(phase, (every[HEADS // 2 :], ((0, 3),)))

        near, far = ((NEAR, 1),), ((FAR, 1),)
        for group in range(GROUPS):
            rounds(2 * group, 2)
            wait_tile(phase, 0, group)
            if group == 1:
                take_scales(phase, 0)
                update(phase, (every[: 2 * PER], near))
            elif group > 1:
                update(phase, (every[group * PER : (group + 1) * PER], near))

        @pl.when(first)
        def _():
            each_sibling(3, 4, lambda copy: copy.wait_recv())
            update(phase, (every, ((1, 1),)))

        @pl.when(jnp.logical_not(first))
        def _():
            earlier_sends_left()

        rounds(10, 2)
        wait_tile(phase, 1, 0)
        wait_tile(phase, 1, 1)
        take_scales(phase, 1)
        update(phase, (every[: 2 * PER], far))
        rounds(12, 2)
        wait_tile(phase, 1, 2)
        wait_tile(phase, 1, 3)
        update(phase, (every[2 * PER : 4 * PER], far))

        @pl.when(first)
        def _():
            last_shards(0)
            update(phase, (every[: HEADS // 2], ((2, 1),)))
            last_shards(1)
            wait_tile(phase, 1, 4)
            update(phase, (every[HEADS // 2 : 4 * PER], ((2, 1),)), (every[4 * PER :], ((2, 1), (FAR, 1))))
            finish(every)

        @pl.when(jnp.logical_not(first))
        def _():
            finish(every[: 4 * PER])
            wait_tile(phase, 1, 4)
            update(phase, (every[4 * PER :], far))
            finish(every[4 * PER :])

        @pl.when(first)
        def _():
            col = root_scale()
            step_size = steps_ref[0]
            square[...] = jnp.zeros((TOK, HD), F32)

            def move(group, _):
                squares = square[...]
                cols = [head_cols(group * PER + i) for i in range(PER)]
                moved = [
                    (buf[1, pl.ds(0, TOK), c].astype(F32) + step_size * (accum[:, c] * col)).astype(BF16)
                    for c in cols
                ]
                for c, values in zip(cols, moved):
                    buf[1, pl.ds(0, TOK), c] = values
                    wide = values.astype(F32)
                    squares = squares + wide * wide
                square[...] = squares

                @pl.when(group == 0)
                def _():
                    start_tile(1, 0, 0)

                return 0

            lax.fori_loop(0, GROUPS, move, 0)
            col = root_scale()
            send_scale(1, col)
            for group in range(1, GROUPS):
                start_tile(1, 0, group)
            begin_heads(col)

        return 0

    lax.fori_loop(0, STEPS, phase_body, 0)

    col = root_scale()
    last_size = steps_ref[STEPS - 1]

    cols = [head_cols(head) for head in range(HEADS)]
    velocities = [accum[:, c] * col for c in cols]
    moved = [buf[1, pl.ds(0, TOK), c].astype(F32) + last_size * v for c, v in zip(cols, velocities)]
    for c, velocity, denoised in zip(cols, velocities, moved):
        denoised_ref[0, :, c] = denoised.astype(BF16)
        velocity_ref[0, :, c] = velocity.astype(BF16)

    for hop in range(2):
        tiles_left(1, hop)


PIECE = 16
PIECES = TOK // PIECE


def hand_over(denoised_in, velocity_in, denoised_out, velocity_out, sems):
    copies = [
        pltpu.make_async_copy(source.at[0, pl.ds(PIECE * i, PIECE)], target.at[0, pl.ds(PIECE * i, PIECE)], sems.at[which, i])
        for i in range(PIECES)
        for which, (source, target) in enumerate(((denoised_in, denoised_out), (velocity_in, velocity_out)))
    ]
    for copy in copies:
        copy.start()
    for copy in copies:
        copy.wait()


def per_device(latent, past_cache, neighbour_mask, gains, step_sizes):
    dma = pltpu.SemaphoreType.DMA
    hbm = pl.BlockSpec(memory_space=pltpu.HBM)
    vmem = pl.BlockSpec(memory_space=pltpu.VMEM)
    operands = [
        pltpu.with_memory_space_constraint(x, pltpu.HBM)
        for x in (latent, past_cache, neighbour_mask, gains, step_sizes)
    ]
    results = pl.pallas_call(
        kernel,
        out_shape=(pltpu.VMEM((1, TOK, HW), BF16),) * 2,
        in_specs=[hbm] * 5,
        out_specs=(vmem,) * 2,
        scratch_shapes=[
            pltpu.SMEM((1, 1, 4), jnp.int32),
            pltpu.VMEM((2, HW), F32),
            pltpu.SMEM((STEPS,), F32),
            pltpu.VMEM((2, ROWS, HW), BF16),
            pltpu.VMEM((TOK, HW), BF16),
            pltpu.VMEM((TOK, HW), F32),
            pltpu.VMEM((HEADS, TOK, HD), F32),
            pltpu.VMEM((HEADS, TOK, HD), F32),
            pltpu.VMEM((STEPS, 8, HD), F32),
            pltpu.VMEM((STEPS, 4, 8, HD), F32),
            pltpu.VMEM((4 * TOK, HD), F32),
            pltpu.VMEM((5, 8, HD), F32),
            pltpu.VMEM((TOK, HD), F32),
            dma((6,)),
            dma((2, RING)),
            dma((2, 16, 2)),
            dma((2, 16, 2)),
            dma((STEPS, 2, 2, GROUPS)),
            dma((STEPS, 4, GROUPS)),
            dma((STEPS, 2, 2)),
            dma((STEPS, 4)),
        ],
        compiler_params=pltpu.CompilerParams(
            collective_id=0, has_side_effects=True, vmem_limit_bytes=32 * 1024 * 1024
        ),
        cost_estimate=pl.CostEstimate(flops=760_000_000, bytes_accessed=1_200_000, transcendentals=1_600_000),
    )(*operands)
    return pl.pallas_call(
        hand_over,
        out_shape=(jax.ShapeDtypeStruct((1, TOK, HW), BF16),) * 2,
        in_specs=[vmem] * 2,
        out_specs=(hbm,) * 2,
        scratch_shapes=[dma((2, PIECES))],
    )(*(pltpu.with_memory_space_constraint(x, pltpu.VMEM) for x in results))


def solution(mesh):
    in_specs = (P("tm", "space", None), P(None, "tm", "space"), P("tm", "space", None), P(), P())
    out_specs = (P("tm", "space", None), P("tm", "space", None))
    return jax.shard_map(
        per_device, mesh=mesh, in_specs=in_specs, out_specs=out_specs, check_vma=False
    )
```

```python
import functools
import math

import jax
import jax.numpy as jnp
from jax import lax
from jax.experimental import pallas as pl
from jax.experimental.pallas import tpu as pltpu
from jax.sharding import PartitionSpec as P

HD = 128
HEADS = 20
HW = HD * HEADS
TOK = 64
STEPS = 2
SHARD = 16
GROUPS = 5
PER = HEADS // GROUPS
GW = PER * HD
EPS = 1e-6
SCORE_SCALE = math.log2(math.e) / math.sqrt(HD)
MASKED = -1e30
MESH = pl.DeviceIdType.MESH
F32 = jnp.float32
BF16 = jnp.bfloat16

STAGE = 128
NEAR, FAR = 3, 4
TILES = 3 * STAGE
ROWS = TILES + STEPS * 2 * STAGE
CHIP = TOK
RING = 14


def kernel(
    latent_hbm, cache_hbm, mask_hbm, gains_hbm, steps_hbm,
    denoised_ref, velocity_ref,
    mask_ref, gains_ref, steps_ref, buf, query, accum, peak, total, scale_own, scale_in, scale_col, bias, square,
    local_sem, ysend, ssend, yrecv, zsend, zrecv, rsend, rrecv,
):
    tm, space = lax.axis_index("tm"), lax.axis_index("space")
    n_tm, n_space = lax.axis_size("tm"), lax.axis_size("space")
    along_y = ((lax.rem(tm + 2, n_tm), space), (lax.rem(tm + n_tm - 2, n_tm), space))
    sibling = (tm + 1 - 2 * lax.rem(tm, 2), space)
    along_z = ((tm, lax.rem(space + 1, n_space)), (tm, lax.rem(space + n_space - 1, n_space)))
    has_low, has_high = space > 0, space < n_space - 1
    sends = ((has_high, has_low & has_high), (has_low, has_low & has_high))
    receives = ((has_low, space > 1), (has_high, space < n_space - 2))

    def remote(src, dst, send, recv, device):
        return pltpu.make_async_remote_copy(
            src_ref=src, dst_ref=dst, send_sem=send, recv_sem=recv, device_id=device, device_id_type=MESH
        )

    def half_cols(half):
        return pl.ds(pl.multiple_of(half * (HW // 2), HW // 2), HW // 2)

    def shard(which, index, half):
        rows = CHIP + SHARD * index + jnp.where(index >= 2, 2 * SHARD, 0)
        return buf.at[which, pl.ds(pl.multiple_of(rows, SHARD), SHARD), half_cols(half)]

    def slot(distance, direction):
        return 4 * distance - 2 + jnp.where(distance == 4, 0, 2 * direction)

    def ring_place(direction, number):
        which = lax.rem(number // 2 + direction, 2)
        return which, lax.rem(number, 2), number // 4 + 1

    def ring_copy(direction, number, own):
        which, half, distance = ring_place(direction, number)
        target = slot(distance, direction)
        if own:
            src = cache_hbm.at[which, :, half_cols(half)]
        else:
            src = shard(which, slot(distance - 1, direction), half)
        return remote(
            src, shard(which, target, half), ysend.at[direction, number], yrecv.at[which, target, half],
            along_y[direction],
        )

    def sib_copy(which, half, target, own=False):
        src = cache_hbm.at[which, :, half_cols(half)] if own else shard(which, target - 1, half)
        return remote(
            src, shard(which, target, half), ssend.at[which, target, half], yrecv.at[which, target, half], sibling
        )

    def ring_round(number):
        for direction in range(2):
            which, half, distance = ring_place(direction, number)
            ring_copy(direction, number, False).wait_recv()

            @pl.when(number + 4 < RING)
            def _():
                ring_copy(direction, number + 4, False).start()

            sib_copy(which, half, slot(distance, direction) + 1).start()

    def each_sibling(first, count, act):
        def body(i, _):
            act(sib_copy(lax.rem(i, 2), lax.rem(i // 2, 2), first + 2 * (i // 4)))
            return 0

        lax.fori_loop(0, 4 * count, body, 0)

    def columns(group):
        return pl.ds(pl.multiple_of(group * GW, GW), GW)

    def head_cols(head):
        if isinstance(head, int):
            return pl.ds(head * HD, HD)
        return pl.ds(pl.multiple_of(head * HD, HD), HD)

    def tile_rows(phase, number):
        return pl.ds(pl.multiple_of(TILES + phase * 2 * STAGE + number * TOK, TOK), TOK)

    def tile_part(phase, number, cols):
        return buf.at[1, tile_rows(phase, number), cols]

    def tile_copy(phase, direction, hop, group):
        cols = columns(group)
        if hop == 1:
            src = tile_part(phase, direction, cols)
        elif isinstance(phase, int) and phase == 0:
            src = latent_hbm.at[0, :, cols]
        else:
            src = buf.at[1, pl.ds(0, TOK), cols]
        target = 2 * hop + direction
        return remote(
            src, tile_part(phase, target, cols), zsend.at[phase, direction, hop, group],
            zrecv.at[phase, target, group], along_z[direction],
        )

    def scale_copy(phase, direction, hop):
        src = scale_own.at[phase] if hop == 0 else scale_in.at[phase, direction]
        target = 2 * hop + direction
        return remote(
            src, scale_in.at[phase, target], rsend.at[phase, direction, hop], rrecv.at[phase, target], along_z[direction]
        )

    def start_tile(phase, hop, group):
        for direction in range(2):
            @pl.when(sends[direction][hop])
            def _():
                tile_copy(phase, direction, hop, group).start()

    def wait_tile(phase, hop, group):
        for direction in range(2):
            @pl.when(receives[direction][hop])
            def _():
                tile_copy(phase, direction, hop, group).wait_recv()

        if hop == 0:
            start_tile(phase, 1, group)

    diagonal = lax.broadcasted_iota(jnp.int32, (TOK, HD), 0) == lax.broadcasted_iota(jnp.int32, (TOK, HD), 1)

    def take_scales(phase, hop):
        for direction in range(2):
            target = 2 * hop + direction

            @pl.when(receives[direction][hop])
            def _():
                scale_copy(phase, direction, hop).wait_recv()

            if hop == 0:
                @pl.when(sends[direction][1])
                def _():
                    scale_copy(phase, direction, 1).start()

            row = jnp.broadcast_to(scale_in[phase, target, 0:1, :], (TOK, HD))
            col = jnp.sum(jnp.where(diagonal, row, 0.0), axis=1, keepdims=True)
            scale_col[pl.ds(target * TOK, TOK), :] = jnp.broadcast_to(col, (TOK, HD))

    def root_scale():
        mean = jnp.sum(square[...], axis=1, keepdims=True) * (1.0 / HW)
        return jnp.broadcast_to(lax.rsqrt(mean + EPS), (TOK, HD))

    def send_scale(phase, col):
        row = jnp.sum(jnp.where(diagonal, col, 0.0), axis=0, keepdims=True)
        scale_own[phase] = jnp.broadcast_to(row, (8, HD))
        for direction in range(2):
            @pl.when(sends[direction][0])
            def _():
                scale_copy(phase, direction, 0).start()

    def begin_heads(col):
        def body(group, _):
            heads = [group * PER + i for i in range(PER)]
            normals = [buf[1, pl.ds(0, TOK), head_cols(head)].astype(F32) * col for head in heads]
            for head, normal in zip(heads, normals):
                cols = head_cols(head)
                query[:, cols] = (normal * gains_ref[0:1, cols]).astype(BF16)
                buf[0, pl.ds(0, TOK), cols] = (normal * gains_ref[1:2, cols]).astype(BF16)
                peak[head] = jnp.full((TOK, HD), MASKED, F32)
                total[head] = jnp.zeros((TOK, HD), F32)
                accum[:, cols] = jnp.zeros((TOK, HD), F32)
            return 0

        lax.fori_loop(0, GROUPS, body, 0)

    def value_rows(stage, count, phase):
        start = (stage + phase * 2) * STAGE if stage >= NEAR else stage * STAGE
        return pl.ds(pl.multiple_of(start, STAGE), count * STAGE)

    def keys_of(head, stage, count, phase):
        cols = head_cols(head)
        rows = value_rows(stage, count, phase)
        if stage < NEAR:
            return buf[0, rows, cols]
        scales = scale_col[pl.ds((stage - NEAR) * STAGE, STAGE), :]
        return (buf[1, rows, cols].astype(F32) * scales * gains_ref[1:2, cols]).astype(BF16)

    def mix(plan, weights, phase):
        mixed = []
        at = 0
        while at < len(plan):
            head, spans = plan[at]
            pair = 2 if at + 1 < len(plan) and plan[at + 1] == (head + 1, spans) else 1
            cols = pl.ds(head * HD, pair * HD)
            sums = None
            for i, (stage, count) in enumerate(spans):
                stacked = jnp.concatenate([weights[at + j][i] for j in range(pair)], axis=0)
                product = jnp.dot(stacked, buf[1, value_rows(stage, count, phase), cols], preferred_element_type=F32)
                sums = product if sums is None else sums + product
            mixed += [sums[j * TOK : (j + 1) * TOK, j * HD : (j + 1) * HD] for j in range(pair)]
            at += pair
        return mixed

    def update(phase, *parts):
        plan = [(head, spans) for heads, spans in parts for head in heads]
        cols = [head_cols(head) for head, _ in plan]
        keys = [[keys_of(head, stage, count, phase) for stage, count in spans] for head, spans in plan]
        queries = [query[:, c] for c in cols]
        old_peaks = [peak[head] for head, _ in plan]
        scores = []
        for q, each, (_, spans) in zip(queries, keys, plan):
            pieces = []
            for k, (stage, count) in zip(each, spans):
                raw = lax.dot_general(q, k, (((1,), (1,)), ((), ())), preferred_element_type=F32)
                pieces.append([
                    raw[:, i * STAGE : (i + 1) * STAGE] * SCORE_SCALE + bias[stage + i, 0:1, :] for i in range(count)
                ])
            scores.append(pieces)
        tops = [functools.reduce(jnp.maximum, sum(pieces, [])) for pieces in scores]
        peaks = [
            jnp.maximum(old, jnp.broadcast_to(jnp.max(top, axis=1, keepdims=True), (TOK, HD)))
            for old, top in zip(old_peaks, tops)
        ]
        expos = [[[jnp.exp2(s - p) for s in span] for span in pieces] for pieces, p in zip(scores, peaks)]
        weights = [[jnp.concatenate([e.astype(BF16) for e in span], axis=1) for span in each] for each in expos]
        mixed = mix(plan, weights, phase)
        factors = [jnp.exp2(old - new) for old, new in zip(old_peaks, peaks)]
        totals = [
            total[head] * f + functools.reduce(jnp.add, sum(each, []))
            for (head, _), f, each in zip(plan, factors, expos)
        ]
        sums = [accum[:, c] * f + m for c, f, m in zip(cols, factors, mixed)]
        for i, (head, _) in enumerate(plan):
            peak[head] = peaks[i]
            total[head] = totals[i]
            accum[:, cols[i]] = sums[i]

    def finish(heads):
        attended = [accum[:, head_cols(head)] / jnp.sum(total[head], axis=1, keepdims=True) for head in heads]
        squares = square[...]
        for head, values in zip(heads, attended):
            accum[:, head_cols(head)] = values
            squares = squares + values * values
        square[...] = squares

    def tiles_left(phase, hop):
        for direction in range(2):
            @pl.when(sends[direction][hop])
            def _():
                scale_copy(phase, direction, hop).wait_send()

                def body(group, _):
                    tile_copy(phase, direction, hop, group).wait_send()
                    return 0

                lax.fori_loop(0, GROUPS, body, 0)

    def earlier_sends_left():
        def ring_left(number, _):
            for direction in range(2):
                ring_copy(direction, number, False).wait_send()
            return 0

        for number in range(4):
            for direction in range(2):
                ring_copy(direction, number, True).wait_send()
        lax.fori_loop(4, RING, ring_left, 0)
        for which in range(2):
            for half in range(2):
                sib_copy(which, half, 1, True).wait_send()
        each_sibling(3, 7, lambda copy: copy.wait_send())
        for hop in range(2):
            tiles_left(0, hop)

    loads = [
        pltpu.make_async_copy(latent_hbm.at[0], buf.at[1, pl.ds(0, TOK)], local_sem.at[0]),
        pltpu.make_async_copy(cache_hbm.at[0], buf.at[0, pl.ds(CHIP, SHARD)], local_sem.at[1]),
        pltpu.make_async_copy(cache_hbm.at[1], buf.at[1, pl.ds(CHIP, SHARD)], local_sem.at[2]),
        pltpu.make_async_copy(mask_hbm, mask_ref, local_sem.at[3]),
        pltpu.make_async_copy(gains_hbm, gains_ref, local_sem.at[4]),
        pltpu.make_async_copy(steps_hbm, steps_ref, local_sem.at[5]),
    ]
    barrier = pltpu.get_barrier_semaphore()
    for device in (*along_y, sibling):
        pl.semaphore_signal(barrier, inc=1, device_id=device, device_id_type=MESH)
    for direction in range(2):
        @pl.when(sends[direction][0])
        def _():
            pl.semaphore_signal(barrier, inc=1, device_id=along_z[direction], device_id_type=MESH)

    for load in loads:
        load.start()
    pl.semaphore_wait(barrier, 3 + lax.min(space, 1) + lax.min(n_space - 1 - space, 1))

    start_tile(0, 0, 0)
    for number in range(4):
        for direction in range(2):
            ring_copy(direction, number, True).start()
    for which in range(2):
        for half in range(2):
            sib_copy(which, half, 1, True).start()

    for hop in range(2):
        for direction in range(2):
            @pl.when(jnp.logical_not(receives[direction][hop]))
            def _():
                for phase in range(STEPS):
                    buf[1, tile_rows(phase, 2 * hop + direction), :] = jnp.zeros((TOK, HW), BF16)
                    scale_in[phase, 2 * hop + direction] = jnp.zeros((8, HD), F32)

    for which in range(2):
        for stage in (0, 2):
            buf[which, pl.ds(stage * STAGE + 3 * STAGE // 4, STAGE // 4), :] = jnp.zeros((STAGE // 4, HW), BF16)

    for load in loads[3:]:
        load.wait()
    lane = lax.broadcasted_iota(jnp.int32, (8, HD), 1)
    for stage in (0, 2):
        bias[stage] = jnp.where(lane < 3 * STAGE // 4, 0.0, MASKED).astype(F32)
    bias[1] = jnp.zeros((8, HD), F32)
    for hop in range(2):
        low, high = (1, 2) if hop == 0 else (0, 3)
        low_ok = (mask_ref[0, 0, low] > 0) & (space - hop > 0)
        high_ok = (mask_ref[0, 0, high] > 0) & (space + hop + 1 < n_space)
        low_bias = jnp.where(low_ok, 0.0, MASKED).astype(F32)
        high_bias = jnp.where(high_ok, 0.0, MASKED).astype(F32)
        bias[NEAR + hop] = jnp.where(lane < TOK, low_bias, high_bias)

    loads[0].wait()
    square[...] = jnp.zeros((TOK, HD), F32)

    def add_squares(group, _):
        squares = square[...]
        for i in range(PER):
            values = buf[1, pl.ds(0, TOK), head_cols(group * PER + i)].astype(F32)
            squares = squares + values * values
        square[...] = squares
        return 0

    lax.fori_loop(0, GROUPS, add_squares, 0)
    col = root_scale()
    send_scale(0, col)
    for group in range(1, GROUPS):
        start_tile(0, 0, group)
    begin_heads(col)
    for load in loads[1:3]:
        load.wait()

    def phase_body(phase, _):
        first = phase == 0
        square[...] = jnp.zeros((TOK, HD), F32)

        def rounds(start, count):
            @pl.when(first)
            def _():
                for number in range(start, start + count):
                    ring_round(number)

        def last_shards(half):
            for target in (11, 13, 15):
                for which in range(2):
                    sib_copy(which, half, target).wait_recv()

        every = range(HEADS)

        @pl.when(first)
        def _():
            each_sibling(1, 1, lambda copy: copy.wait_recv())

        @pl.when(first)
        def _():
            update(phase, (every, ((0, 1),)))

        @pl.when(jnp.logical_not(first))
        def _():
            update(phase, (every[: HEADS // 2], ((0, 3),)))
            update(phase, (every[HEADS // 2 :], ((0, 3),)))

        near, far = ((NEAR, 1),), ((FAR, 1),)
        for group in range(GROUPS):
            rounds(2 * group, 2)
            wait_tile(phase, 0, group)
            if group == 0:
                take_scales(phase, 0)
            update(phase, (every[group * PER : (group + 1) * PER], near))

        @pl.when(first)
        def _():
            each_sibling(3, 4, lambda copy: copy.wait_recv())
            update(phase, (every, ((1, 1),)))

        @pl.when(jnp.logical_not(first))
        def _():
            earlier_sends_left()

        rounds(10, 2)
        wait_tile(phase, 1, 0)
        wait_tile(phase, 1, 1)
        take_scales(phase, 1)
        update(phase, (every[: 2 * PER], far))
        rounds(12, 2)
        wait_tile(phase, 1, 2)
        wait_tile(phase, 1, 3)
        update(phase, (every[2 * PER : 4 * PER], far))

        @pl.when(first)
        def _():
            last_shards(0)
            update(phase, (every[: HEADS // 2], ((2, 1),)))
            last_shards(1)
            wait_tile(phase, 1, 4)
            update(phase, (every[HEADS // 2 : 4 * PER], ((2, 1),)), (every[4 * PER :], ((2, 1), (FAR, 1))))
            finish(every)

        @pl.when(jnp.logical_not(first))
        def _():
            finish(every[: 4 * PER])
            tiles_left(1, 0)
            wait_tile(phase, 1, 4)
            update(phase, (every[4 * PER :], far))
            finish(every[4 * PER :])

        @pl.when(first)
        def _():
            col = root_scale()
            step_size = steps_ref[0]
            square[...] = jnp.zeros((TOK, HD), F32)

            def move(group, _):
                squares = square[...]
                cols = [head_cols(group * PER + i) for i in range(PER)]
                moved = [
                    (buf[1, pl.ds(0, TOK), c].astype(F32) + step_size * (accum[:, c] * col)).astype(BF16)
                    for c in cols
                ]
                for c, values in zip(cols, moved):
                    buf[1, pl.ds(0, TOK), c] = values
                    wide = values.astype(F32)
                    squares = squares + wide * wide
                square[...] = squares

                @pl.when(group == 0)
                def _():
                    start_tile(1, 0, 0)

                return 0

            lax.fori_loop(0, GROUPS, move, 0)
            col = root_scale()
            send_scale(1, col)
            for group in range(1, GROUPS):
                start_tile(1, 0, group)
            begin_heads(col)

        return 0

    lax.fori_loop(0, STEPS, phase_body, 0)

    col = root_scale()
    last_size = steps_ref[STEPS - 1]

    cols = [head_cols(head) for head in range(HEADS)]
    velocities = [accum[:, c] * col for c in cols]
    moved = [buf[1, pl.ds(0, TOK), c].astype(F32) + last_size * v for c, v in zip(cols, velocities)]
    for c, velocity, denoised in zip(cols, velocities, moved):
        denoised_ref[0, :, c] = denoised.astype(BF16)
        velocity_ref[0, :, c] = velocity.astype(BF16)

    tiles_left(1, 1)


PIECE = 32
PIECES = TOK // PIECE


def hand_over(denoised_in, velocity_in, denoised_out, velocity_out, sems):
    copies = [
        pltpu.make_async_copy(source.at[0, pl.ds(PIECE * i, PIECE)], target.at[0, pl.ds(PIECE * i, PIECE)], sems.at[which, i])
        for i in range(PIECES)
        for which, (source, target) in enumerate(((denoised_in, denoised_out), (velocity_in, velocity_out)))
    ]
    for copy in copies:
        copy.start()
    for copy in copies:
        copy.wait()


def per_device(latent, past_cache, neighbour_mask, gains, step_sizes):
    dma = pltpu.SemaphoreType.DMA
    hbm = pl.BlockSpec(memory_space=pltpu.HBM)
    vmem = pl.BlockSpec(memory_space=pltpu.VMEM)
    operands = [
        pltpu.with_memory_space_constraint(x, pltpu.HBM)
        for x in (latent, past_cache, neighbour_mask, gains, step_sizes)
    ]
    results = pl.pallas_call(
        kernel,
        out_shape=(pltpu.VMEM((1, TOK, HW), BF16),) * 2,
        in_specs=[hbm] * 5,
        out_specs=(vmem,) * 2,
        scratch_shapes=[
            pltpu.SMEM((1, 1, 4), jnp.int32),
            pltpu.VMEM((2, HW), F32),
            pltpu.SMEM((STEPS,), F32),
            pltpu.VMEM((2, ROWS, HW), BF16),
            pltpu.VMEM((TOK, HW), BF16),
            pltpu.VMEM((TOK, HW), F32),
            pltpu.VMEM((HEADS, TOK, HD), F32),
            pltpu.VMEM((HEADS, TOK, HD), F32),
            pltpu.VMEM((STEPS, 8, HD), F32),
            pltpu.VMEM((STEPS, 4, 8, HD), F32),
            pltpu.VMEM((4 * TOK, HD), F32),
            pltpu.VMEM((5, 8, HD), F32),
            pltpu.VMEM((TOK, HD), F32),
            dma((6,)),
            dma((2, RING)),
            dma((2, 16, 2)),
            dma((2, 16, 2)),
            dma((STEPS, 2, 2, GROUPS)),
            dma((STEPS, 4, GROUPS)),
            dma((STEPS, 2, 2)),
            dma((STEPS, 4)),
        ],
        compiler_params=pltpu.CompilerParams(
            collective_id=0, has_side_effects=True, vmem_limit_bytes=32 * 1024 * 1024
        ),
        cost_estimate=pl.CostEstimate(flops=760_000_000, bytes_accessed=1_200_000, transcendentals=1_600_000),
    )(*operands)
    return pl.pallas_call(
        hand_over,
        out_shape=(jax.ShapeDtypeStruct((1, TOK, HW), BF16),) * 2,
        in_specs=[vmem] * 2,
        out_specs=(hbm,) * 2,
        scratch_shapes=[dma((2, PIECES))],
    )(*(pltpu.with_memory_space_constraint(x, pltpu.VMEM) for x in results))


def solution(mesh):
    in_specs = (P("tm", "space", None), P(None, "tm", "space"), P("tm", "space", None), P(), P())
    out_specs = (P("tm", "space", None), P("tm", "space", None))
    return jax.shard_map(
        per_device, mesh=mesh, in_specs=in_specs, out_specs=out_specs, check_vma=False
    )
```
